512 devices in a mesh: lat: 16 (over y, z_lo), lon: 32 (over z_hi, x, core).
Axes of the slice: x: 4, y: 8, z: 8 (z_hi: 4, z_lo: 2; z = z_hi * 2 + z_lo), core: 2. Of those that a mesh axis runs over, the one named last changes fastest.
Arguments:
- fields: bfloat16 [384, 512, 192], P('lat', 'lon'), may hold values from -6 to 6
- first_weight: bfloat16 [3, 3, 192, 192], replicated, may hold values from -0.15625 to 0.15625
- first_gamma: float32 [192, 192], replicated, may hold values from 0 to 0.010416667
- first_beta: float32 [192], replicated, may hold values from 0.5 to 2
- second_weight: bfloat16 [3, 3, 192, 192], replicated, may hold values from -0.15625 to 0.15625
- second_gamma: float32 [192, 192], replicated, may hold values from 0 to 0.010416667
- second_beta: float32 [192], replicated, may hold values from 0.5 to 2
- cotangent: bfloat16 [384, 512, 192], P('lat', 'lon'), may hold values from -0.015625 to 0.015625
Outputs:
- encoded: bfloat16 [384, 512, 192], P('lat', 'lon')
- first_wgrad: bfloat16 [3, 3, 192, 192], replicated
- first_ggrad: float32 [192, 192], replicated
- first_bgrad: float32 [192], replicated
- second_wgrad: bfloat16 [3, 3, 192, 192], replicated
- second_ggrad: float32 [192, 192], replicated
- second_bgrad: float32 [192], replicated
The draws below stay inside these ranges and needn't reach their ends.
All inputs are finite; a program needn't handle non-finite values.
Results may differ from the reference program's by a relative error of at most 0.007.
Values may be sent and summed in bfloat16 or wider, within the bound.
A program may use at most 64 MiB of HBM per device.

```python
import math
import jax
import jax.numpy as jnp
from jax import lax

C = 192
HD = 24
WD = 16
H = 384
W = 512


def block_scale(key, shape, cuts, least, top_value):
    level, own = 1.0, jax.random.fold_in(key, 6)
    for dim, parts in cuts:
        draws = jnp.exp(jax.random.uniform(jax.random.fold_in(own, dim), (parts,), jnp.float32, least / len(cuts), top_value / len(cuts)))
        level = level * jnp.repeat(draws, shape[dim] // parts).reshape([-1 if axis == dim else 1 for axis in range(len(shape))])
    return level


def gaussian(own_key, shape, deviation, reach, split=(), held_as=jnp.bfloat16):
    result = jax.random.normal(own_key, shape, jnp.float32) * deviation
    if len(split) > 0:
        result = block_scale(own_key, shape, split, -0.22, 0.18) * result
    return jnp.clip(result, min=-reach, max=reach).astype(held_as)


def setup_inputs(seed: int = 0) -> dict:
    splits = jax.random.split(jax.random.key(seed), 9)
    return {
        "fields": gaussian(splits[0], (H, W, C), 1.0, 6.0, ((0, 16), (1, 32))),
        "first_weight": gaussian(splits[1], (3, 3, C, C), (9 * C) ** -0.5, 0.15625),
        "first_gamma": jnp.clip(jax.random.uniform(splits[2], (C, C), jnp.float32, 0.0, 0.010416667), 0.0, 0.010416667),
        "first_beta": jnp.clip(jnp.exp(jax.random.uniform(splits[3], (C,), jnp.float32, math.log(0.5), math.log(2.0))), 0.5, 2.0),
        "second_weight": gaussian(splits[4], (3, 3, C, C), (9 * C) ** -0.5, 0.15625),
        "second_gamma": jnp.clip(jax.random.uniform(splits[5], (C, C), jnp.float32, 0.0, 0.010416667), 0.0, 0.010416667),
        "second_beta": jnp.clip(jnp.exp(jax.random.uniform(splits[6], (C,), jnp.float32, math.log(0.5), math.log(2.0))), 0.5, 2.0),
        "cotangent": gaussian(splits[7], (H, W, C), (1.0 / (HD * WD)), 0.015625, ((0, 16), (1, 32))),
    }


def extend(field):
    half = field.shape[1] // 2
    top_row = jnp.roll(field[:1], half, axis=1)
    bottom_row = jnp.roll(field[-1:], half, axis=1)
    rows = jnp.concatenate([top_row, field, bottom_row], axis=0)
    return jnp.concatenate([rows[:, -1:], rows, rows[:, :1]], axis=1)

def retract(grad):
    half = (grad.shape[1] - 2) // 2
    rows = grad[:, 1:-1]
    rows = rows.at[:, 0].add(grad[:, -1]).at[:, -1].add(grad[:, 0])
    inner = rows[1:-1]
    inner = inner.at[0].add(jnp.roll(rows[0], half, axis=0))
    inner = inner.at[-1].add(jnp.roll(rows[-1], half, axis=0))
    return inner

def convolve(padded, weight):
    rows_n = padded.shape[0] - 2
    cols_n = padded.shape[1] - 2
    chans = padded.shape[2]
    total = jnp.zeros((rows_n * cols_n, weight.shape[3]), jnp.float32)
    for row_off in range(3):
        for col_off in range(3):
            window = padded[row_off:row_off + rows_n, col_off:col_off + cols_n].reshape(-1, chans)
            total = total + jnp.dot(window, weight[row_off, col_off], preferred_element_type=jnp.float32)
    return total.reshape(rows_n, cols_n, -1)

def spread(grad, weight):
    rows_n, cols_n, outs_n = grad.shape
    flat = grad.reshape(-1, outs_n)
    total = jnp.zeros((rows_n + 2, cols_n + 2, weight.shape[2]), jnp.float32)
    for row_off in range(3):
        for col_off in range(3):
            term = lax.dot_general(flat, weight[row_off, col_off], (((1,), (1,)), ((), ())), preferred_element_type=jnp.float32)
            term = term.reshape(rows_n, cols_n, -1)
            total = total + jnp.pad(term, ((row_off, 2 - row_off), (col_off, 2 - col_off), (0, 0)))
    return total

def weight_grad(padded, grad):
    rows_n, cols_n, outs_n = grad.shape
    chans = padded.shape[2]
    flat = grad.reshape(-1, outs_n)
    pieces = []
    for row_off in range(3):
        for col_off in range(3):
            window = padded[row_off:row_off + rows_n, col_off:col_off + cols_n].reshape(-1, chans)
            pieces.append(lax.dot_general(window, flat, (((0,), (0,)), ((), ())), preferred_element_type=jnp.float32))
    return jnp.stack(pieces).reshape(3, 3, chans, outs_n)

def normalize(z, gamma, beta):
    chans = z.shape[2]
    sq = z * z
    summed = lax.dot_general(sq.reshape(-1, chans), gamma, (((1,), (1,)), ((), ())), precision=lax.Precision.HIGHEST)
    scale = lax.rsqrt(beta + summed.reshape(z.shape))
    return (z * scale, scale, sq)

def denormalize(upper, z, scale, sq, gamma):
    chans = z.shape[2]
    lever = upper * z * scale * scale * scale
    flat = lever.reshape(-1, chans)
    mixed = jnp.dot(flat, gamma, precision=lax.Precision.HIGHEST).reshape(z.shape)
    lower = upper * scale - z * mixed
    gamma_grad = -0.5 * lax.dot_general(flat, sq.reshape(-1, chans), (((0,), (0,)), ((), ())), precision=lax.Precision.HIGHEST)
    beta_grad = -0.5 * lax.optimization_barrier(jnp.sum(flat, axis=0))
    return (lower, gamma_grad, beta_grad)

def reference(fields, first_weight, first_gamma, first_beta, second_weight, second_gamma, second_beta, cotangent):
    padded_x = extend(fields)
    z_first = convolve(padded_x, first_weight)
    h_first, scale_one, sq_one = normalize(z_first, first_gamma, first_beta)
    hidden = h_first.astype(jnp.bfloat16)
    padded_h = extend(hidden)
    z_second = convolve(padded_h, second_weight)
    out_float, scale_two, sq_two = normalize(z_second, second_gamma, second_beta)
    encoded = out_float.astype(jnp.bfloat16)
    dz_two, ggrad_two, bgrad_two = denormalize(cotangent.astype(jnp.float32), z_second, scale_two, sq_two, second_gamma)
    grad_two = dz_two.astype(jnp.bfloat16)
    wgrad_two = weight_grad(padded_h, grad_two)
    dhidden = retract(spread(grad_two, second_weight))
    dz_one, ggrad_one, bgrad_one = denormalize(dhidden, z_first, scale_one, sq_one, first_gamma)
    grad_one = dz_one.astype(jnp.bfloat16)
    wgrad_one = weight_grad(padded_x, grad_one)
    return (encoded, wgrad_one.astype(jnp.bfloat16), ggrad_one, bgrad_one, wgrad_two.astype(jnp.bfloat16), ggrad_two, bgrad_two)
```

```python
import functools

import jax
import jax.numpy as jnp
from jax import lax
from jax.experimental import pallas as pl
from jax.experimental.pallas import tpu as pltpu
from jax.sharding import PartitionSpec as P

MESH = pl.DeviceIdType.MESH
BF16 = jnp.bfloat16
F32 = jnp.float32
NX, NY, NZ = 4, 8, 8
ROWS = 3072
HALF = ROWS // 2
PART = HALF // NX
SHARD = PART // NY
SLOTS = 32


def coordinates():
    lat, lon = lax.axis_index("lat"), lax.axis_index("lon")
    core = lax.rem(lon, 2)
    x = lax.rem(lax.div(lon, 2), NX)
    z = lax.div(lon, 2 * NX) * 2 + lax.rem(lat, 2)
    y = lax.div(lat, 2)
    return core, x, y, z


def at(core, x, y, z):
    return (y * 2 + lax.rem(z, 2), lax.div(z, 2) * (2 * NX) + x * 2 + core)


def partners():
    core, x, y, z = coordinates()
    found = [at(1 - core, x, y, z)]
    found += [at(core, lax.rem(x + d, NX), y, z) for d in range(1, NX)]
    found += [at(core, x, lax.rem(y + d, NY), z) for d in range(1, NY)]
    found += [at(core, x, y, lax.rem(z + d, NZ)) for d in range(1, NZ)]
    return found


class Reduction:
    def __init__(self, layer, grads, core_out, core_in, x_out, x_in, y_out, y_in, z_in, y_all, full, sums, send, recv):
        self.layer = layer
        self.grads, self.full = grads, full
        self.core_out, self.core_in = core_out, core_in
        self.x_out, self.x_in = x_out, x_in
        self.y_out, self.y_in = y_out, y_in
        self.z_in, self.y_all = z_in, y_all
        self.sums = sums
        self.send, self.recv = send, recv
        self.me = coordinates()

    def copy(self, source, target, slot, device):
        made = pltpu.make_async_remote_copy(
            src_ref=source,
            dst_ref=target,
            send_sem=self.send.at[self.layer, slot],
            recv_sem=self.recv.at[self.layer, slot],
            device_id=device,
            device_id_type=MESH,
        )
        return made

    def core_copy(self):
        core, x, y, z = self.me
        return self.copy(self.core_out, self.core_in, 0, at(1 - core, x, y, z))

    def x_copy(self, d):
        core, x, y, z = self.me
        return self.copy(self.x_out.at[d - 1], self.x_in.at[d - 1], d, at(core, lax.rem(x + d, NX), y, z))

    def y_copy(self, d):
        core, x, y, z = self.me
        return self.copy(self.y_out.at[d - 1], self.y_in.at[d - 1], 3 + d, at(core, x, lax.rem(y + d, NY), z))

    def z_copy(self, d):
        core, x, y, z = self.me
        return self.copy(self.z_in.at[z], self.z_in.at[z], 10 + d, at(core, x, y, lax.rem(z + d, NZ)))

    def z_arrival(self, d):
        core, x, y, z = self.me
        other = lax.rem(z + NZ - d, NZ)
        return self.copy(self.z_in.at[other], self.z_in.at[other], 10 + d, at(core, x, y, other))

    def y_gather(self, d, arrival=False):
        core, x, y, z = self.me
        row = lax.rem(y + NY - d, NY) if arrival else y
        ref = self.y_all.at[row]
        return self.copy(ref, ref, 17 + d, at(core, x, lax.rem(y + d, NY), z))

    def part(self, core, x):
        return self.full.at[core, x]

    def x_gather(self, d, arrival=False):
        core, x, y, z = self.me
        ref = self.part(core, lax.rem(x + NX - d, NX) if arrival else x)
        return self.copy(ref, ref, 24 + d, at(core, lax.rem(x + d, NX), y, z))

    def core_gather(self, d, arrival=False):
        core, x, y, z = self.me
        ref = self.part(1 - core if arrival else core, lax.rem(x + NX - d, NX))
        return self.copy(ref, ref, 28 + d, at(1 - core, x, y, z))

    def start_core(self):
        core, x, y, z = self.me
        self.core_out[...] = self.grads[1 - core].astype(BF16)
        self.core_copy().start()

    def core_to_x(self):
        core, x, y, z = self.me
        self.core_copy().wait_recv()
        for d in range(1, NX):
            other = lax.rem(x + d, NX)
            self.x_out[d - 1] = (self.grads[core, other] + self.core_in[other].astype(F32)).astype(BF16)
            self.x_copy(d).start()
        own = self.grads[core, x] + self.core_in[x].astype(F32)
        self.sums[...] = own.reshape(self.sums.shape)

    def x_to_y(self):
        core, x, y, z = self.me
        total = self.sums[...]
        for d in range(1, NX):
            self.x_copy(d).wait_recv()
            total = total + self.x_in[d - 1].astype(F32).reshape(total.shape)
        self.sums[...] = total
        for d in range(1, NY):
            self.y_out[d - 1] = self.sums[lax.rem(y + d, NY)].astype(BF16)
            self.y_copy(d).start()

    def y_to_z(self):
        core, x, y, z = self.me
        total = self.sums[y]
        for d in range(1, NY):
            self.y_copy(d).wait_recv()
            total = total + self.y_in[d - 1].astype(F32)
        self.z_in[z] = total.astype(BF16)
        for d in range(1, NZ):
            self.z_copy(d).start()

    def z_to_y(self):
        core, x, y, z = self.me
        for d in range(1, NZ):
            self.z_arrival(d).wait_recv()
        total = self.z_in[0].astype(F32)
        for place in range(1, NZ):
            total = total + self.z_in[place].astype(F32)
        self.y_all[y] = total.astype(BF16)
        for d in range(1, NY):
            self.y_gather(d).start()

    def y_to_x(self):
        core, x, y, z = self.me
        for d in range(1, NY):
            self.y_gather(d, arrival=True).wait_recv()
        whole = self.y_all[...].astype(F32).reshape(PART, 128)
        for block in range(PART // 128):
            turned = whole[block * 128 : (block + 1) * 128].T
            self.full[core, x, block * 128 : (block + 1) * 128] = turned.astype(BF16)
        for d in range(1, NX):
            self.x_gather(d).start()
        self.core_gather(0).start()

    def x_to_core(self):
        for d in range(1, NX):
            self.x_gather(d, arrival=True).wait_recv()
            self.core_gather(d).start()

    def core_done(self):
        for d in range(NX):
            self.core_gather(d, arrival=True).wait_recv()

    def drain(self):
        self.core_copy().wait_send()
        for d in range(1, NX):
            self.x_copy(d).wait_send()
            self.x_gather(d).wait_send()
        for d in range(1, NY):
            self.y_copy(d).wait_send()
            self.y_gather(d).wait_send()
        for d in range(1, NZ):
            self.z_copy(d).wait_send()
        for d in range(NX):
            self.core_gather(d).wait_send()

    def block(self, index):
        per = PART // 128
        core, rest = divmod(index, NX * per)
        x, place = divmod(rest, per)
        return self.full[core, x, place * 128 : (place + 1) * 128]

    def unpack(self, wgrad, ggrad, bgrad):
        for tap in range(10):
            pair, odd = divmod(tap, 2)
            low = slice(64 * odd, 64 * odd + 64)
            target = ggrad if tap == 9 else wgrad.at[tap]
            dtype = F32 if tap == 9 else BF16
            target[0:128, 0:128] = self.block(tap).astype(dtype)
            target[0:128, 128:192] = self.block(15 + pair)[:, low].astype(dtype)
            target[128:192, 0:128] = self.block(10 + pair)[low].astype(dtype)
            half, side = divmod(10 + pair, 2)
            corner = self.block(15 + half)[low, 64 * side : 64 * side + 64]
            target[128:192, 128:192] = corner.astype(dtype)
        offsets = self.block(23).astype(F32)
        bgrad[0:1, 0:128] = offsets[0:1]
        bgrad[0:1, 128:192] = offsets[1:2, 0:64]


def reduction_scratch():
    return [
        pltpu.VMEM((2, NX, PART, 128), BF16),
        pltpu.VMEM((2, NX, PART, 128), BF16),
        pltpu.VMEM((2, NX - 1, PART, 128), BF16),
        pltpu.VMEM((2, NX - 1, PART, 128), BF16),
        pltpu.VMEM((2, NY - 1, SHARD, 128), BF16),
        pltpu.VMEM((2, NY - 1, SHARD, 128), BF16),
        pltpu.VMEM((2, NZ, SHARD, 128), BF16),
        pltpu.VMEM((2, NY, SHARD, 128), BF16),
        pltpu.VMEM((2, 2, NX, PART, 128), BF16),
        pltpu.VMEM((2, NY, SHARD, 128), F32),
        pltpu.SemaphoreType.DMA((2, SLOTS)),
        pltpu.SemaphoreType.DMA((2, SLOTS)),
    ]


def reductions(grads, scratch):
    *buffers, send, recv = scratch
    return [
        Reduction(layer, grads.at[layer], *[buffer.at[layer] for buffer in buffers], send, recv)
        for layer in range(2)
    ]


def reduce_kernel(grads, w1, g1, b1, w2, g2, b2, *scratch):
    barrier = pltpu.get_barrier_semaphore()
    met = partners()
    for device in met:
        pl.semaphore_signal(barrier, inc=1, device_id=device, device_id_type=MESH)
    pl.semaphore_wait(barrier, len(met))
    one, two = reductions(grads, scratch)
    two.start_core()
    one.start_core()
    two.core_to_x()
    one.core_to_x()
    two.x_to_y()
    one.x_to_y()
    two.y_to_z()
    one.y_to_z()
    two.z_to_y()
    one.z_to_y()
    two.y_to_x()
    one.y_to_x()
    two.x_to_core()
    one.x_to_core()
    two.core_done()
    two.unpack(w2, g2, b2)
    one.core_done()
    one.unpack(w1, g1, b1)
    two.drain()
    one.drain()


def pack(wgrad, ggrad, bgrad):
    turned = jnp.concatenate([wgrad.reshape(9, 192, 192), ggrad[None]]).transpose(0, 2, 1)
    right = turned[:, :, 128:].reshape(5, 2, 192, 64).transpose(0, 2, 1, 3).reshape(5, 192, 128)
    tiles = jnp.concatenate([turned[:, :, :128], right])
    lower = jnp.concatenate([tiles[:, 128:].reshape(960, 128), jnp.zeros((64, 128), F32)]).reshape(8, 128, 128)
    offsets = jnp.pad(bgrad, (0, 64)).reshape(2, 128).T
    last = jnp.pad(offsets, ((0, 0), (0, 126)))[None]
    blocks = jnp.concatenate([tiles[:, :128], lower, last])
    return blocks.reshape(2, NX, PART, 128)


def reduce_all(packed):
    shapes = [
        jax.ShapeDtypeStruct((9, 192, 192), BF16),
        jax.ShapeDtypeStruct((192, 192), F32),
        jax.ShapeDtypeStruct((1, 192), F32),
    ] * 2
    outs = pl.pallas_call(
        reduce_kernel,
        out_shape=shapes,
        in_specs=[pl.BlockSpec(memory_space=pltpu.VMEM)],
        out_specs=[pl.BlockSpec(memory_space=pltpu.VMEM)] * 6,
        scratch_shapes=reduction_scratch(),
        compiler_params=pltpu.CompilerParams(
            collective_id=0, has_side_effects=True, vmem_limit_bytes=48 * 1024 * 1024
        ),
    )(packed)
    return outs
def padded_2(block, sides, width, periodic):
    for axis, dim in sides:
        count = lax.axis_size(axis)
        forward = [(i, i + 1) for i in range(count - 1)]
        if periodic:
            forward.append((count - 1, 0))
        backward = [(target, source) for source, target in forward]
        low = lax.ppermute(
            lax.slice_in_dim(block, block.shape[dim] - width, None, axis=dim), axis, forward
        )
        high = lax.ppermute(lax.slice_in_dim(block, 0, width, axis=dim), axis, backward)
        block = jnp.concatenate([low, block, high], axis=dim)
    return block


def from_behind(block, axis, distance):
    devices = range(lax.axis_size(axis))
    route = [((i - distance) % len(devices), i) for i in devices]
    return lax.ppermute(block, axis, route)


def border(field):
    half = lax.axis_size("lon") // 2
    last_band = lax.axis_size("lat") - 1
    band = lax.axis_index("lat")
    rows = padded_2(field, (("lat", 0),), 1, False)
    edges = jnp.stack([field[0], field[-1]])
    folded = from_behind(edges, "lon", half)
    top_row = jnp.where(band == 0, folded[0], rows[0])
    bottom_row = jnp.where(band == last_band, folded[1], rows[-1])
    rows = jnp.concatenate([top_row[None], rows[1:-1], bottom_row[None]], axis=0)
    return padded_2(rows, (("lon", 1),), 1, True)


def unborder(grad):
    half = lax.axis_size("lon") // 2
    last_band = lax.axis_size("lat") - 1
    band = lax.axis_index("lat")
    sides = jnp.stack([grad[:, 0], grad[:, -1]], axis=1)
    arrived = padded_2(sides.astype(jnp.bfloat16), (("lon", 1),), 1, True).astype(sides.dtype)
    rows = grad[:, 1:-1]
    rows = rows.at[:, 0].add(arrived[:, 0]).at[:, -1].add(arrived[:, -1])
    edges = jnp.stack([rows[0], rows[-1]])
    returned = from_behind(edges, "lon", half)
    across = padded_2(edges, (("lat", 0),), 1, False)
    top_add = jnp.where(band == 0, returned[0], across[0])
    bottom_add = jnp.where(band == last_band, returned[1], across[-1])
    inner = rows[1:-1]
    inner = inner.at[0].add(top_add)
    inner = inner.at[-1].add(bottom_add)
    return inner


def convolve(padded, weight):
    rows_n = padded.shape[0] - 2
    cols_n = padded.shape[1] - 2
    chans = padded.shape[2]
    total = jnp.zeros((rows_n * cols_n, weight.shape[3]), jnp.float32)
    for row_off in range(3):
        for col_off in range(3):
            window = padded[row_off : row_off + rows_n, col_off : col_off + cols_n].reshape(
                -1, chans
            )
            total = total + jnp.dot(
                window, weight[row_off, col_off], preferred_element_type=jnp.float32
            )
    return total.reshape(rows_n, cols_n, -1)


def spread(grad, weight):
    rows_n, cols_n, outs_n = grad.shape
    flat = grad.reshape(-1, outs_n)
    total = jnp.zeros((rows_n + 2, cols_n + 2, weight.shape[2]), jnp.float32)
    for row_off in range(3):
        for col_off in range(3):
            term = lax.dot_general(
                flat,
                weight[row_off, col_off],
                (((1,), (1,)), ((), ())),
                preferred_element_type=jnp.float32,
            )
            term = term.reshape(rows_n, cols_n, -1)
            total = total + jnp.pad(term, ((row_off, 2 - row_off), (col_off, 2 - col_off), (0, 0)))
    return total


def weight_grad(padded, grad):
    rows_n, cols_n, outs_n = grad.shape
    chans = padded.shape[2]
    flat = grad.reshape(-1, outs_n)
    pieces = []
    for row_off in range(3):
        for col_off in range(3):
            window = padded[row_off : row_off + rows_n, col_off : col_off + cols_n].reshape(
                -1, chans
            )
            pieces.append(
                lax.dot_general(
                    window, flat, (((0,), (0,)), ((), ())), preferred_element_type=jnp.float32
                )
            )
    return jnp.stack(pieces).reshape(3, 3, chans, outs_n)


def normalize(z, gamma, beta):
    chans = z.shape[2]
    sq = z * z
    summed = lax.dot_general(
        sq.reshape(-1, chans), gamma, (((1,), (1,)), ((), ())), precision=lax.Precision.HIGHEST
    )
    scale = lax.rsqrt(beta + summed.reshape(z.shape))
    return (z * scale, scale, sq)


def denormalize(upper, z, scale, sq, gamma):
    chans = z.shape[2]
    lever = upper * z * scale * scale * scale
    flat = lever.reshape(-1, chans)
    mixed = jnp.dot(flat, gamma, precision=lax.Precision.HIGHEST).reshape(z.shape)
    lower = upper * scale - z * mixed
    gamma_grad = -0.5 * lax.dot_general(
        flat, sq.reshape(-1, chans), (((0,), (0,)), ((), ())), precision=lax.Precision.HIGHEST
    )
    beta_grad = -0.5 * jnp.sum(flat, axis=0)
    return (lower, gamma_grad, beta_grad)


def per_device(
    fields,
    first_weight,
    first_gamma,
    first_beta,
    second_weight,
    second_gamma,
    second_beta,
    cotangent,
):
    padded_x = border(fields)
    z_first = convolve(padded_x, first_weight)
    h_first, scale_one, sq_one = normalize(z_first, first_gamma, first_beta)
    hidden = h_first.astype(jnp.bfloat16)
    padded_h = border(hidden)
    z_second = convolve(padded_h, second_weight)
    out_float, scale_two, sq_two = normalize(z_second, second_gamma, second_beta)
    encoded = out_float.astype(jnp.bfloat16)
    dz_two, ggrad_two, bgrad_two = denormalize(
        cotangent.astype(jnp.float32), z_second, scale_two, sq_two, second_gamma
    )
    grad_two = dz_two.astype(jnp.bfloat16)
    wgrad_two = weight_grad(padded_h, grad_two)
    dhidden = unborder(spread(grad_two, second_weight))
    dz_one, ggrad_one, bgrad_one = denormalize(dhidden, z_first, scale_one, sq_one, first_gamma)
    grad_one = dz_one.astype(jnp.bfloat16)
    wgrad_one = weight_grad(padded_x, grad_one)
    packed = jnp.stack([pack(wgrad_one, ggrad_one, bgrad_one), pack(wgrad_two, ggrad_two, bgrad_two)])
    w1, g1, b1, w2, g2, b2 = reduce_all(packed)
    shape = (3, 3, 192, 192)
    return (encoded, w1.reshape(shape), g1, b1.reshape(192), w2.reshape(shape), g2, b2.reshape(192))


def solution(mesh):
    return jax.shard_map(
        per_device,
        mesh=mesh,
        in_specs=(P("lat", "lon", None), P(), P(), P(), P(), P(), P(), P("lat", "lon", None)),
        out_specs=(P("lat", "lon", None), P(), P(), P(), P(), P(), P()),
        check_vma=False,
    )
```

```python
import jax
import jax.numpy as jnp
from jax import lax
from jax.experimental import pallas as pl
from jax.experimental.pallas import tpu as pltpu
from jax.sharding import PartitionSpec as P

MESH = pl.DeviceIdType.MESH
BF16 = jnp.bfloat16
F32 = jnp.float32
NX, NY, NZ = 4, 8, 8
ROWS = 3072
HALF = ROWS // 2
PART = HALF // NX
SHARD = PART // NY
SLOTS = 32


def coordinates():
    lat, lon = lax.axis_index("lat"), lax.axis_index("lon")
    core = lax.rem(lon, 2)
    x = lax.rem(lax.div(lon, 2), NX)
    z = lax.div(lon, 2 * NX) * 2 + lax.rem(lat, 2)
    y = lax.div(lat, 2)
    return core, x, y, z


def at(core, x, y, z):
    return (y * 2 + lax.rem(z, 2), lax.div(z, 2) * (2 * NX) + x * 2 + core)


def partners():
    core, x, y, z = coordinates()
    found = [at(1 - core, x, y, z)]
    found += [at(core, lax.rem(x + d, NX), y, z) for d in range(1, NX)]
    found += [at(core, x, lax.rem(y + d, NY), z) for d in range(1, NY)]
    found += [at(core, x, y, lax.rem(z + d, NZ)) for d in range(1, NZ)]
    return found


class Reduction:
    def __init__(self, layer, grads, core_out, core_in, x_out, x_in, y_out, y_in, z_in, y_all, full, sums, send, recv):
        self.layer = layer
        self.grads, self.full = grads, full
        self.core_out, self.core_in = core_out, core_in
        self.x_out, self.x_in = x_out, x_in
        self.y_out, self.y_in = y_out, y_in
        self.z_in, self.y_all = z_in, y_all
        self.sums = sums
        self.send, self.recv = send, recv
        self.me = coordinates()

    def copy(self, source, target, slot, device):
        made = pltpu.make_async_remote_copy(
            src_ref=source,
            dst_ref=target,
            send_sem=self.send.at[self.layer, slot],
            recv_sem=self.recv.at[self.layer, slot],
            device_id=device,
            device_id_type=MESH,
        )
        return made

    def core_copy(self):
        core, x, y, z = self.me
        return self.copy(self.core_out, self.core_in, 0, at(1 - core, x, y, z))

    def x_copy(self, d):
        core, x, y, z = self.me
        return self.copy(self.x_out.at[d - 1], self.x_in.at[d - 1], d, at(core, lax.rem(x + d, NX), y, z))

    def y_copy(self, d):
        core, x, y, z = self.me
        return self.copy(self.y_out.at[d - 1], self.y_in.at[d - 1], 3 + d, at(core, x, lax.rem(y + d, NY), z))

    def z_copy(self, d):
        core, x, y, z = self.me
        return self.copy(self.z_in.at[z], self.z_in.at[z], 10 + d, at(core, x, y, lax.rem(z + d, NZ)))

    def z_arrival(self, d):
        core, x, y, z = self.me
        other = lax.rem(z + NZ - d, NZ)
        return self.copy(self.z_in.at[other], self.z_in.at[other], 10 + d, at(core, x, y, other))

    def y_gather(self, d, arrival=False):
        core, x, y, z = self.me
        row = lax.rem(y + NY - d, NY) if arrival else y
        ref = self.y_all.at[row]
        return self.copy(ref, ref, 17 + d, at(core, x, lax.rem(y + d, NY), z))

    def part(self, core, x):
        return self.full.at[core, x]

    def x_gather(self, d, arrival=False):
        core, x, y, z = self.me
        ref = self.part(core, lax.rem(x + NX - d, NX) if arrival else x)
        return self.copy(ref, ref, 24 + d, at(core, lax.rem(x + d, NX), y, z))

    def core_gather(self, d, arrival=False):
        core, x, y, z = self.me
        ref = self.part(1 - core if arrival else core, lax.rem(x + NX - d, NX))
        return self.copy(ref, ref, 28 + d, at(1 - core, x, y, z))

    def start_core(self):
        core, x, y, z = self.me
        self.core_out[...] = self.grads[1 - core].astype(BF16)
        self.core_copy().start()

    def core_to_x(self):
        core, x, y, z = self.me
        self.core_copy().wait_recv()
        for d in range(1, NX):
            other = lax.rem(x + d, NX)
            self.x_out[d - 1] = (self.grads[core, other] + self.core_in[other].astype(F32)).astype(BF16)
            self.x_copy(d).start()
        own = self.grads[core, x] + self.core_in[x].astype(F32)
        self.sums[...] = own.reshape(self.sums.shape)

    def x_to_y(self):
        core, x, y, z = self.me
        total = self.sums[...]
        for d in range(1, NX):
            self.x_copy(d).wait_recv()
            total = total + self.x_in[d - 1].astype(F32).reshape(total.shape)
        self.sums[...] = total
        for d in range(1, NY):
            self.y_out[d - 1] = self.sums[lax.rem(y + d, NY)].astype(BF16)
            self.y_copy(d).start()

    def y_to_z(self):
        core, x, y, z = self.me
        total = self.sums[y]
        for d in range(1, NY):
            self.y_copy(d).wait_recv()
            total = total + self.y_in[d - 1].astype(F32)
        self.z_in[z] = total.astype(BF16)
        for d in range(1, NZ):
            self.z_copy(d).start()

    def z_to_y(self):
        core, x, y, z = self.me
        for d in range(1, NZ):
            self.z_arrival(d).wait_recv()
        total = self.z_in[0].astype(F32)
        for place in range(1, NZ):
            total = total + self.z_in[place].astype(F32)
        self.y_all[y] = total.astype(BF16)
        for d in range(1, NY):
            self.y_gather(d).start()

    def y_to_x(self):
        core, x, y, z = self.me
        for d in range(1, NY):
            self.y_gather(d, arrival=True).wait_recv()
        whole = self.y_all[...].astype(F32).reshape(PART, 128)
        for block in range(PART // 128):
            turned = whole[block * 128 : (block + 1) * 128].T
            self.full[core, x, block * 128 : (block + 1) * 128] = turned.astype(BF16)
        for d in range(1, NX):
            self.x_gather(d).start()
        self.core_gather(0).start()

    def x_to_core(self):
        for d in range(1, NX):
            self.x_gather(d, arrival=True).wait_recv()
            self.core_gather(d).start()

    def core_done(self):
        for d in range(NX):
            self.core_gather(d, arrival=True).wait_recv()

    def drain(self):
        self.core_copy().wait_send()
        for d in range(1, NX):
            self.x_copy(d).wait_send()
            self.x_gather(d).wait_send()
        for d in range(1, NY):
            self.y_copy(d).wait_send()
            self.y_gather(d).wait_send()
        for d in range(1, NZ):
            self.z_copy(d).wait_send()
        for d in range(NX):
            self.core_gather(d).wait_send()

    def block(self, index):
        per = PART // 128
        core, rest = divmod(index, NX * per)
        x, place = divmod(rest, per)
        return self.full[core, x, place * 128 : (place + 1) * 128]

    def unpack(self, wgrad, ggrad, bgrad):
        for tap in range(10):
            pair, odd = divmod(tap, 2)
            low = slice(64 * odd, 64 * odd + 64)
            target = ggrad if tap == 9 else wgrad.at[tap]
            dtype = F32 if tap == 9 else BF16
            target[0:128, 0:128] = self.block(tap).astype(dtype)
            target[0:128, 128:192] = self.block(15 + pair)[:, low].astype(dtype)
            target[128:192, 0:128] = self.block(10 + pair)[low].astype(dtype)
            half, side = divmod(10 + pair, 2)
            corner = self.block(15 + half)[low, 64 * side : 64 * side + 64]
            target[128:192, 128:192] = corner.astype(dtype)
        offsets = self.block(23).astype(F32)
        bgrad[0:1, 0:128] = offsets[0:1]
        bgrad[0:1, 128:192] = offsets[1:2, 0:64]


def reduction_scratch():
    return [
        pltpu.VMEM((2, NX, PART, 128), BF16),
        pltpu.VMEM((2, NX, PART, 128), BF16),
        pltpu.VMEM((2, NX - 1, PART, 128), BF16),
        pltpu.VMEM((2, NX - 1, PART, 128), BF16),
        pltpu.VMEM((2, NY - 1, SHARD, 128), BF16),
        pltpu.VMEM((2, NY - 1, SHARD, 128), BF16),
        pltpu.VMEM((2, NZ, SHARD, 128), BF16),
        pltpu.VMEM((2, NY, SHARD, 128), BF16),
        pltpu.VMEM((2, 2, NX, PART, 128), BF16),
        pltpu.VMEM((2, NY, SHARD, 128), F32),
        pltpu.SemaphoreType.DMA((2, SLOTS)),
        pltpu.SemaphoreType.DMA((2, SLOTS)),
    ]


def reductions(grads, scratch):
    *buffers, send, recv = scratch
    return [
        Reduction(layer, grads.at[layer], *[buffer.at[layer] for buffer in buffers], send, recv)
        for layer in range(2)
    ]


def neighbours():
    lat, lon = lax.axis_index("lat"), lax.axis_index("lon")
    lats, lons = lax.axis_size("lat"), lax.axis_size("lon")
    first = (lat == 0).astype(jnp.int32)
    last = (lat == lats - 1).astype(jnp.int32)
    rows = []
    for pole, step, side in ((first, -1, 1), (last, 1, 0)):
        for east in (-1, 0, 1):
            device = (lat + step * (1 - pole), lax.rem(lon + lons + east + pole * (lons // 2), lons))
            landing = side + pole * (1 - 2 * side)
            rows.append((device, landing * 3 + 1 - east))
    west = (lat, lax.rem(lon + lons - 1, lons))
    east = (lat, lax.rem(lon + 1, lons))
    return first, last, rows, west, east


def dot(left, right, dims=((1,), (0,))):
    return lax.dot_general(left, right, (dims, ((), ())), preferred_element_type=F32)


def split(value):
    high = value.astype(BF16)
    return high, (value - high.astype(F32)).astype(BF16)


def dot_split(left, right, dims=((1,), (0,))):
    left_high, left_low = split(left)
    right_high, right_low = split(right)
    return dot(left_high, right_high, dims) + dot(left_high, right_low, dims) + dot(left_low, right_high, dims)


def flat(value):
    return value.reshape(-1, value.shape[-1])


def keep_shifted(store, value):
    store[0] = pltpu.roll(value, 1, axis=1)
    store[1] = value
    store[2] = pltpu.roll(value, 23, axis=1)


def outer_window(store, rows, ghosts, a, b, first, last):
    turned = 2 - 2 * a
    top = store[b, pl.ds(a + first * turned, ghosts)]
    middle = store[b, ghosts + a : rows - ghosts + a]
    bottom = store[b, pl.ds(rows - ghosts + a + last * turned, ghosts)]
    return flat(jnp.concatenate([top, middle, bottom], axis=0)).astype(BF16)


def inner_window(store, a, b, start):
    return flat(store[b, start + a : start + a + 24, 0:16]).astype(BF16)


def outer_convolution(store, weight, rows, ghosts, first, last):
    total = None
    for a in range(3):
        for b in range(3):
            term = dot(outer_window(store, rows, ghosts, a, b, first, last), weight[3 * a + b])
            total = term if total is None else total + term
    return total


def place_block(grads, index, value):
    per = PART // 128
    core, rest = divmod(index, NX * per)
    x, place = divmod(rest, per)
    grads[core, x, place * 128 : (place + 1) * 128] = value


def place_lower(grads, tile, value):
    per = PART // 128
    core, rest = divmod(15 + tile // 2, NX * per)
    x, place = divmod(rest, per)
    start = place * 128 + 64 * (tile % 2)
    grads[core, x, start : start + 64] = value


def pack_gradients(grads, store, start, grad, lever, sq, turn):
    turned = grad.T.astype(BF16)
    kept = None
    for tap in range(10):
        if tap < 9:
            block = dot(turned, inner_window(store, tap // 3, tap % 3, start))
        else:
            block = -0.5 * dot_split(sq.T, lever)
        place_block(grads, tap, block[0:128, 0:128])
        place_lower(grads, tap, block[128:192, 0:128])
        if tap % 2 == 0:
            kept = block[:, 128:192]
        else:
            both = jnp.concatenate([kept, block[:, 128:192]], axis=1)
            tile = 10 + tap // 2
            place_block(grads, tile, both[0:128])
            place_lower(grads, tile, both[128:192])
    offsets = -0.5 * jnp.sum(lever, axis=0, keepdims=True)
    turn[...] = jnp.zeros_like(turn)
    turn[0:1, :] = offsets[:, 0:128]
    turn[1:2, 0:64] = offsets[:, 128:192]
    place_lower(grads, 15, jnp.zeros((64, 128), F32))
    place_block(grads, 23, turn[...].T)


def kernel(
    x, w1, gamma1, beta1, w2, gamma2, beta2, cot,
    encoded, out_w1, out_g1, out_b1, out_w2, out_g2, out_b2,
    grads, top_out, bottom_out, west_out, east_out, rows_in, west_in, east_in, halo_send, halo_recv,
    field, cotangent, x_store, h_store, g_store, z_keep, scale_keep, turn, stage, strips, *scratch,
):
    barrier = pltpu.get_barrier_semaphore()
    first, last, rows, west, east = neighbours()
    met = partners() + [device for device, _ in rows] + [west, east]
    for device in met:
        pl.semaphore_signal(barrier, inc=1, device_id=device, device_id_type=MESH)

    field[3:27, 0:16] = x[...].astype(F32)
    cotangent[1:25, 0:16] = cot[...].astype(F32)
    top_out[0] = cot[0]
    bottom_out[0] = cot[23]
    for k in range(3):
        top_out[1 + k] = x[k]
        bottom_out[1 + k] = x[23 - k]

    def strip(target, tile, places, edge):
        for half, lanes in enumerate((128, 64)):
            span = slice(128 * half, 128 * half + lanes)
            for ref, chosen, at_row in ((x, places, 0), (cot, (edge,), 72)):
                stage.reshape(24, 8, 128)[:, :, 0:lanes] = ref[:, tile : tile + 8, span].astype(F32)
                for k, place in enumerate(chosen):
                    rows24 = stage[pl.ds(place - tile, 24, stride=8), :]
                    strips[half, at_row + 24 * k : at_row + 24 * k + 24] = rows24
        target[...] = strips[...].astype(BF16)

    strip(west_out, 0, (0, 1, 2), 0)
    strip(east_out, 8, (13, 14, 15), 15)

    pl.semaphore_wait(barrier, len(met))

    def halo(source, target, sent, landed, device):
        return pltpu.make_async_remote_copy(
            src_ref=source,
            dst_ref=target,
            send_sem=halo_send.at[sent],
            recv_sem=halo_recv.at[landed],
            device_id=device,
            device_id_type=MESH,
        )

    copies = [halo(west_out, east_in, 6, 6, west), halo(east_out, west_in, 7, 7, east)]
    for index, (device, slot) in enumerate(rows):
        source = top_out if index < 3 else bottom_out
        copies.append(halo(source, rows_in.at[slot], index, slot, device))
    for copy in copies:
        copy.start()

    for slot in range(6):
        halo(top_out, rows_in.at[slot], 0, slot, rows[0][0]).wait_recv()
    lane8 = lax.broadcasted_iota(jnp.int32, (8, 192), 0)
    for side in range(2):
        for k in range(4):
            target = cotangent if k == 0 else field
            if k == 0:
                row = 25 * side
            else:
                row = 26 + k if side else 3 - k
            target[row, 0:16] = rows_in[3 * side + 1, k].astype(F32)
            from_west = rows_in[3 * side, k].astype(F32)[8:16]
            from_east = rows_in[3 * side + 2, k].astype(F32)[0:8]
            target[row, 16:24] = jnp.where(lane8 < 4, from_east, from_west)
    copies[0].wait_recv()
    copies[1].wait_recv()
    for half, lanes in enumerate((128, 64)):
        span = slice(128 * half, 128 * half + lanes)
        for target, start, size in ((field, 3, 3), (cotangent, 1, 1)):
            for source, offset in ((east_in, 0), (west_in, 8 - size)):
                arrived = source[half].astype(F32)
                for k in range(size):
                    at_row = 24 * k if size == 3 else 72
                    stage[pl.ds(offset + k, 24, stride=8), :] = arrived[at_row : at_row + 24]
            target[start : start + 24, 16:24, span] = stage.reshape(24, 8, 128)[:, :, 0:lanes]

    keep_shifted(x_store, field[...])
    z1 = outer_convolution(x_store, w1, 28, 2, first, last)
    scale1 = lax.rsqrt(beta1[...] + dot_split(z1 * z1, gamma1[...], ((1,), (1,))))
    hidden = (z1 * scale1).astype(BF16).astype(F32)
    keep_shifted(h_store, hidden.reshape(28, 24, 192))
    z_keep[...] = flat(z1.reshape(28, 24, 192)[2:26, 0:16])
    scale_keep[...] = flat(scale1.reshape(28, 24, 192)[2:26, 0:16])

    z2 = outer_convolution(h_store, w2, 26, 1, first, last)
    sq2 = z2 * z2
    scale2 = lax.rsqrt(beta2[...] + dot_split(sq2, gamma2[...], ((1,), (1,))))
    encoded[...] = (z2 * scale2).reshape(26, 24, 192)[1:25, 0:16].astype(BF16)
    upper = flat(cotangent[...])
    lever2 = upper * z2 * scale2 * scale2 * scale2
    lower2 = upper * scale2 - z2 * dot_split(lever2, gamma2[...])
    grad2 = lower2.astype(BF16).astype(F32).reshape(26, 24, 192)
    keep_shifted(g_store, grad2)

    def inside(value):
        return flat(value.reshape(26, 24, 192)[1:25, 0:16])

    one, two = reductions(grads, scratch)
    pack_gradients(grads.at[1], h_store, 1, inside(grad2), inside(lever2), inside(sq2), turn)
    two.start_core()

    total = None
    blank = jnp.zeros((1, 16, 192), F32)
    for a in range(3):
        for b in range(3):
            shifted = g_store.at[2 - b]
            if a == 0:
                window = jnp.concatenate([shifted[2:25, 0:16], blank], axis=0)
            elif a == 1:
                window = shifted[1:25, 0:16]
            else:
                window = jnp.concatenate([blank, shifted[1:24, 0:16]], axis=0)
            term = dot(flat(window).astype(BF16), w2[3 * a + b], ((1,), (1,)))
            total = term if total is None else total + term
    ghosts = []
    for row, a in ((0, 2 - 2 * first), (25, 2 * last)):
        ghost = None
        for b in range(3):
            term = dot(g_store[2 - b, row, 0:16].astype(BF16), w2[3 * a + b], ((1,), (1,)))
            ghost = term if ghost is None else ghost + term
        ghosts.append(ghost)
    upper1 = jnp.concatenate([total[0:16] + ghosts[0], total[16:368], total[368:384] + ghosts[1]], axis=0)
    two.core_to_x()

    z1 = z_keep[...]
    scale1 = scale_keep[...]
    lever1 = upper1 * z1 * scale1 * scale1 * scale1
    lower1 = upper1 * scale1 - z1 * dot_split(lever1, gamma1[...])
    grad1 = lower1.astype(BF16).astype(F32)
    pack_gradients(grads.at[0], x_store, 2, grad1, lever1, z1 * z1, turn)
    one.start_core()
    two.x_to_y()
    one.core_to_x()
    two.y_to_z()
    one.x_to_y()
    two.z_to_y()
    one.y_to_z()
    two.y_to_x()
    one.z_to_y()
    two.x_to_core()
    one.y_to_x()
    two.core_done()
    two.unpack(out_w2, out_g2, out_b2)
    one.x_to_core()
    one.core_done()
    one.unpack(out_w1, out_g1, out_b1)
    for copy in copies:
        copy.wait_send()
    two.drain()
    one.drain()


def per_device(
    fields,
    first_weight,
    first_gamma,
    first_beta,
    second_weight,
    second_gamma,
    second_beta,
    cotangent,
):
    gradients = [
        jax.ShapeDtypeStruct((9, 192, 192), BF16),
        jax.ShapeDtypeStruct((192, 192), F32),
        jax.ShapeDtypeStruct((1, 192), F32),
    ]
    vmem = pl.BlockSpec(memory_space=pltpu.VMEM)
    shape = (3, 3, 192, 192)
    encoded, w1, g1, b1, w2, g2, b2 = pl.pallas_call(
        kernel,
        out_shape=[jax.ShapeDtypeStruct((24, 16, 192), BF16)] + gradients * 2,
        in_specs=[vmem] * 8,
        out_specs=[vmem] * 7,
        scratch_shapes=[
            pltpu.VMEM((2, 2, NX, PART, 128), F32),
            pltpu.VMEM((4, 16, 192), BF16),
            pltpu.VMEM((4, 16, 192), BF16),
            pltpu.VMEM((2, 96, 128), BF16),
            pltpu.VMEM((2, 96, 128), BF16),
            pltpu.VMEM((6, 4, 16, 192), BF16),
            pltpu.VMEM((2, 96, 128), BF16),
            pltpu.VMEM((2, 96, 128), BF16),
            pltpu.SemaphoreType.DMA((8,)),
            pltpu.SemaphoreType.DMA((8,)),
            pltpu.VMEM((30, 24, 192), F32),
            pltpu.VMEM((26, 24, 192), F32),
            pltpu.VMEM((3, 30, 24, 192), F32),
            pltpu.VMEM((3, 28, 24, 192), F32),
            pltpu.VMEM((3, 26, 24, 192), F32),
            pltpu.VMEM((384, 192), F32),
            pltpu.VMEM((384, 192), F32),
            pltpu.VMEM((128, 128), F32),
            pltpu.VMEM((192, 128), F32),
            pltpu.VMEM((2, 96, 128), F32),
            *reduction_scratch(),
        ],
        compiler_params=pltpu.CompilerParams(
            collective_id=0, has_side_effects=True, vmem_limit_bytes=48 * 1024 * 1024
        ),
    )(
        fields,
        first_weight.reshape(9, 192, 192),
        first_gamma,
        first_beta.reshape(1, 192),
        second_weight.reshape(9, 192, 192),
        second_gamma,
        second_beta.reshape(1, 192),
        cotangent,
    )
    return (encoded, w1.reshape(shape), g1, b1.reshape(192), w2.reshape(shape), g2, b2.reshape(192))


def solution(mesh):
    return jax.shard_map(
        per_device,
        mesh=mesh,
        in_specs=(P("lat", "lon", None), P(), P(), P(), P(), P(), P(), P("lat", "lon", None)),
        out_specs=(P("lat", "lon", None), P(), P(), P(), P(), P(), P()),
        check_vma=False,
    )
```

```python
import jax
import jax.numpy as jnp
from jax import lax
from jax.experimental import pallas as pl
from jax.experimental.pallas import tpu as pltpu
from jax.sharding import PartitionSpec as P

MESH = pl.DeviceIdType.MESH
BF16 = jnp.bfloat16
F32 = jnp.float32
NX, NY, NZ = 4, 8, 8
ROWS = 3072
HALF = ROWS // 2
PART = HALF // NX
SHARD = PART // NY
SLOTS = 32


def coordinates():
    lat, lon = lax.axis_index("lat"), lax.axis_index("lon")
    core = lax.rem(lon, 2)
    x = lax.rem(lax.div(lon, 2), NX)
    z = lax.div(lon, 2 * NX) * 2 + lax.rem(lat, 2)
    y = lax.div(lat, 2)
    return core, x, y, z


def at(core, x, y, z):
    return (y * 2 + lax.rem(z, 2), lax.div(z, 2) * (2 * NX) + x * 2 + core)


def partners():
    core, x, y, z = coordinates()
    found = [at(1 - core, x, y, z)]
    found += [at(core, lax.rem(x + d, NX), y, z) for d in range(1, NX)]
    found += [at(core, x, lax.rem(y + d, NY), z) for d in range(1, NY)]
    found += [at(core, x, y, lax.rem(z + d, NZ)) for d in range(1, NZ)]
    return found


class Reduction:
    def __init__(self, layer, grads, core_out, core_in, x_out, x_in, y_out, y_in, z_in, y_all, full, sums, send, recv):
        self.layer = layer
        self.grads, self.full = grads, full
        self.core_out, self.core_in = core_out, core_in
        self.x_out, self.x_in = x_out, x_in
        self.y_out, self.y_in = y_out, y_in
        self.z_in, self.y_all = z_in, y_all
        self.sums = sums
        self.send, self.recv = send, recv
        self.me = coordinates()

    def copy(self, source, target, slot, device):
        made = pltpu.make_async_remote_copy(
            src_ref=source,
            dst_ref=target,
            send_sem=self.send.at[self.layer, slot],
            recv_sem=self.recv.at[self.layer, slot],
            device_id=device,
            device_id_type=MESH,
        )
        return made

    def core_copy(self):
        core, x, y, z = self.me
        return self.copy(self.core_out, self.core_in, 0, at(1 - core, x, y, z))

    def x_copy(self, d):
        core, x, y, z = self.me
        return self.copy(self.x_out.at[d - 1], self.x_in.at[d - 1], d, at(core, lax.rem(x + d, NX), y, z))

    def y_copy(self, d):
        core, x, y, z = self.me
        return self.copy(self.y_out.at[d - 1], self.y_in.at[d - 1], 3 + d, at(core, x, lax.rem(y + d, NY), z))

    def z_copy(self, d):
        core, x, y, z = self.me
        return self.copy(self.z_in.at[z], self.z_in.at[z], 10 + d, at(core, x, y, lax.rem(z + d, NZ)))

    def z_arrival(self, d):
        core, x, y, z = self.me
        other = lax.rem(z + NZ - d, NZ)
        return self.copy(self.z_in.at[other], self.z_in.at[other], 10 + d, at(core, x, y, other))

    def y_gather(self, d, arrival=False):
        core, x, y, z = self.me
        row = lax.rem(y + NY - d, NY) if arrival else y
        ref = self.y_all.at[row]
        return self.copy(ref, ref, 17 + d, at(core, x, lax.rem(y + d, NY), z))

    def part(self, core, x):
        return self.full.at[core, x]

    def x_gather(self, d, arrival=False):
        core, x, y, z = self.me
        ref = self.part(core, lax.rem(x + NX - d, NX) if arrival else x)
        return self.copy(ref, ref, 24 + d, at(core, lax.rem(x + d, NX), y, z))

    def core_gather(self, d, arrival=False):
        core, x, y, z = self.me
        ref = self.part(1 - core if arrival else core, lax.rem(x + NX - d, NX))
        return self.copy(ref, ref, 28 + d, at(1 - core, x, y, z))

    def start_core(self):
        core, x, y, z = self.me
        self.core_out[...] = self.grads[1 - core].astype(BF16)
        self.core_copy().start()

    def core_to_x(self):
        core, x, y, z = self.me
        self.core_copy().wait_recv()
        for d in range(1, NX):
            other = lax.rem(x + d, NX)
            self.x_out[d - 1] = (self.grads[core, other] + self.core_in[other].astype(F32)).astype(BF16)
            self.x_copy(d).start()
        own = self.grads[core, x] + self.core_in[x].astype(F32)
        self.sums[...] = own.reshape(self.sums.shape)

    def x_to_y(self):
        core, x, y, z = self.me
        total = self.sums[...]
        for d in range(1, NX):
            self.x_copy(d).wait_recv()
            total = total + self.x_in[d - 1].astype(F32).reshape(total.shape)
        self.sums[...] = total
        for d in range(1, NY):
            self.y_out[d - 1] = self.sums[lax.rem(y + d, NY)].astype(BF16)
            self.y_copy(d).start()

    def y_to_z(self):
        core, x, y, z = self.me
        total = self.sums[y]
        for d in range(1, NY):
            self.y_copy(d).wait_recv()
            total = total + self.y_in[d - 1].astype(F32)
        self.z_in[z] = total.astype(BF16)
        for d in range(1, NZ):
            self.z_copy(d).start()

    def z_to_y(self):
        core, x, y, z = self.me
        for d in range(1, NZ):
            self.z_arrival(d).wait_recv()
        total = self.z_in[0].astype(F32)
        for place in range(1, NZ):
            total = total + self.z_in[place].astype(F32)
        self.y_all[y] = total.astype(BF16)
        for d in range(1, NY):
            self.y_gather(d).start()

    def y_to_x(self):
        core, x, y, z = self.me
        for d in range(1, NY):
            self.y_gather(d, arrival=True).wait_recv()
        whole = self.y_all[...].astype(F32).reshape(PART, 128)
        for block in range(PART // 128):
            turned = whole[block * 128 : (block + 1) * 128].T
            self.full[core, x, block * 128 : (block + 1) * 128] = turned.astype(BF16)
        for d in range(1, NX):
            self.x_gather(d).start()
        self.core_gather(0).start()

    def x_to_core(self):
        for d in range(1, NX):
            self.x_gather(d, arrival=True).wait_recv()
            self.core_gather(d).start()

    def core_done(self):
        for d in range(NX):
            self.core_gather(d, arrival=True).wait_recv()

    def drain(self):
        self.core_copy().wait_send()
        for d in range(1, NX):
            self.x_copy(d).wait_send()
            self.x_gather(d).wait_send()
        for d in range(1, NY):
            self.y_copy(d).wait_send()
            self.y_gather(d).wait_send()
        for d in range(1, NZ):
            self.z_copy(d).wait_send()
        for d in range(NX):
            self.core_gather(d).wait_send()

    def block(self, index):
        per = PART // 128
        core, rest = divmod(index, NX * per)
        x, place = divmod(rest, per)
        return self.full[core, x, place * 128 : (place + 1) * 128]

    def unpack(self, wgrad, ggrad, bgrad):
        for tap in range(10):
            pair, odd = divmod(tap, 2)
            low = slice(64 * odd, 64 * odd + 64)
            target = ggrad if tap == 9 else wgrad.at[tap]
            dtype = F32 if tap == 9 else BF16
            target[0:128, 0:128] = self.block(tap).astype(dtype)
            target[0:128, 128:192] = self.block(15 + pair)[:, low].astype(dtype)
            target[128:192, 0:128] = self.block(10 + pair)[low].astype(dtype)
            half, side = divmod(10 + pair, 2)
            corner = self.block(15 + half)[low, 64 * side : 64 * side + 64]
            target[128:192, 128:192] = corner.astype(dtype)
        offsets = self.block(23).astype(F32)
        bgrad[0:1, 0:128] = offsets[0:1]
        bgrad[0:1, 128:192] = offsets[1:2, 0:64]


def reduction_scratch():
    return [
        pltpu.VMEM((2, NX, PART, 128), BF16),
        pltpu.VMEM((2, NX, PART, 128), BF16),
        pltpu.VMEM((2, NX - 1, PART, 128), BF16),
        pltpu.VMEM((2, NX - 1, PART, 128), BF16),
        pltpu.VMEM((2, NY - 1, SHARD, 128), BF16),
        pltpu.VMEM((2, NY - 1, SHARD, 128), BF16),
        pltpu.VMEM((2, NZ, SHARD, 128), BF16),
        pltpu.VMEM((2, NY, SHARD, 128), BF16),
        pltpu.VMEM((2, 2, NX, PART, 128), BF16),
        pltpu.VMEM((2, NY, SHARD, 128), F32),
        pltpu.SemaphoreType.DMA((2, SLOTS)),
        pltpu.SemaphoreType.DMA((2, SLOTS)),
    ]


def reductions(grads, scratch):
    *buffers, send, recv = scratch
    return [
        Reduction(layer, grads.at[layer], *[buffer.at[layer] for buffer in buffers], send, recv)
        for layer in range(2)
    ]


def neighbours():
    lat, lon = lax.axis_index("lat"), lax.axis_index("lon")
    lats, lons = lax.axis_size("lat"), lax.axis_size("lon")
    first = (lat == 0).astype(jnp.int32)
    last = (lat == lats - 1).astype(jnp.int32)
    rows = []
    for pole, step, side in ((first, -1, 1), (last, 1, 0)):
        for east in (-1, 0, 1):
            device = (lat + step * (1 - pole), lax.rem(lon + lons + east + pole * (lons // 2), lons))
            landing = side + pole * (1 - 2 * side)
            rows.append((device, landing * 3 + 1 - east))
    west = (lat, lax.rem(lon + lons - 1, lons))
    east = (lat, lax.rem(lon + 1, lons))
    return first, last, rows, west, east


def dot(left, right, dims=((1,), (0,))):
    return lax.dot_general(left, right, (dims, ((), ())), preferred_element_type=F32)


def split(value):
    high = value.astype(BF16)
    return high, (value - high.astype(F32)).astype(BF16)


def dot_split(left, right, dims=((1,), (0,))):
    left_high, left_low = split(left)
    right_high, right_low = split(right)
    return dot(left_high, right_high, dims) + dot(left_high, right_low, dims) + dot(left_low, right_high, dims)


def flat(value):
    return value.reshape(-1, value.shape[-1])


def keep_shifted(store, value):
    store[0] = pltpu.roll(value, 1, axis=1)
    store[1] = value
    store[2] = pltpu.roll(value, 23, axis=1)


def outer_window(store, rows, ghosts, a, b, first, last):
    turned = 2 - 2 * a
    top = store[b, pl.ds(a + first * turned, ghosts)]
    middle = store[b, ghosts + a : rows - ghosts + a]
    bottom = store[b, pl.ds(rows - ghosts + a + last * turned, ghosts)]
    return flat(jnp.concatenate([top, middle, bottom], axis=0)).astype(BF16)


def inner_window(store, a, b, start):
    return flat(store[b, start + a : start + a + 24, 0:16]).astype(BF16)


def outer_convolution(store, weight, rows, ghosts, first, last):
    total = None
    for a in range(3):
        for b in range(3):
            term = dot(outer_window(store, rows, ghosts, a, b, first, last), weight[3 * a + b])
            total = term if total is None else total + term
    return total


def place_block(grads, index, value):
    per = PART // 128
    core, rest = divmod(index, NX * per)
    x, place = divmod(rest, per)
    grads[core, x, place * 128 : (place + 1) * 128] = value


def place_lower(grads, tile, value):
    per = PART // 128
    core, rest = divmod(15 + tile // 2, NX * per)
    x, place = divmod(rest, per)
    start = place * 128 + 64 * (tile % 2)
    grads[core, x, start : start + 64] = value


def pack_gradients(grads, store, start, grad, lever, sq, turn):
    turned = grad.T.astype(BF16)
    kept = None
    for tap in range(10):
        if tap < 9:
            block = dot(turned, inner_window(store, tap // 3, tap % 3, start))
        else:
            block = -0.5 * dot_split(sq.T, lever)
        place_block(grads, tap, block[0:128, 0:128])
        place_lower(grads, tap, block[128:192, 0:128])
        if tap % 2 == 0:
            kept = block[:, 128:192]
        else:
            both = jnp.concatenate([kept, block[:, 128:192]], axis=1)
            tile = 10 + tap // 2
            place_block(grads, tile, both[0:128])
            place_lower(grads, tile, both[128:192])
    offsets = -0.5 * jnp.sum(lever, axis=0, keepdims=True)
    turn[...] = jnp.zeros_like(turn)
    turn[0:1, :] = offsets[:, 0:128]
    turn[1:2, 0:64] = offsets[:, 128:192]
    place_lower(grads, 15, jnp.zeros((64, 128), F32))
    place_block(grads, 23, turn[...].T)


def kernel(
    x_far, w1_far, gamma1_far, beta1_far, w2_far, gamma2_far, beta2_far, cot_far,
    encoded_far, out_w1_far, out_g1_far, out_b1_far, out_w2_far, out_g2_far, out_b2_far,
    encoded, out_w1, out_g1, out_b1, out_w2, out_g2, out_b2, written,
    grads, top_out, bottom_out, west_out, east_out, rows_in, west_in, east_in, halo_send, halo_recv,
    field, cotangent, x_store, h_store, g_store, z_keep, scale_keep, turn, stage, strips,
    x, cot, w1, gamma1, beta1, w2, gamma2, beta2, fetched, *scratch,
):
    barrier = pltpu.get_barrier_semaphore()
    first, last, rows, west, east = neighbours()
    met = partners() + [device for device, _ in rows] + [west, east]
    for device in met:
        pl.semaphore_signal(barrier, inc=1, device_id=device, device_id_type=MESH)

    pairs = [
        (x_far, x), (cot_far, cot), (w1_far, w1), (gamma1_far, gamma1),
        (beta1_far, beta1), (w2_far, w2), (gamma2_far, gamma2), (beta2_far, beta2),
    ]
    fetches = [pltpu.make_async_copy(far, near, fetched.at[i]) for i, (far, near) in enumerate(pairs)]
    for fetch in fetches:
        fetch.start()
    pairs = [
        (encoded, encoded_far), (out_w2, out_w2_far), (out_g2, out_g2_far), (out_b2, out_b2_far),
        (out_w1, out_w1_far), (out_g1, out_g1_far), (out_b1, out_b1_far),
    ]
    writes = [pltpu.make_async_copy(near, far, written.at[i]) for i, (near, far) in enumerate(pairs)]
    fetches[0].wait()
    fetches[1].wait()
    field[3:27, 0:16] = x[...].astype(F32)
    cotangent[1:25, 0:16] = cot[...].astype(F32)
    top_out[0] = cot[0]
    bottom_out[0] = cot[23]
    for k in range(3):
        top_out[1 + k] = x[k]
        bottom_out[1 + k] = x[23 - k]

    def strip(target, tile, places, edge):
        for half, lanes in enumerate((128, 64)):
            span = slice(128 * half, 128 * half + lanes)
            for ref, chosen, at_row in ((x, places, 0), (cot, (edge,), 72)):
                stage.reshape(24, 8, 128)[:, :, 0:lanes] = ref[:, tile : tile + 8, span].astype(F32)
                for k, place in enumerate(chosen):
                    rows24 = stage[pl.ds(place - tile, 24, stride=8), :]
                    strips[half, at_row + 24 * k : at_row + 24 * k + 24] = rows24
        target[...] = strips[...].astype(BF16)

    strip(west_out, 0, (0, 1, 2), 0)
    strip(east_out, 8, (13, 14, 15), 15)

    pl.semaphore_wait(barrier, len(met))

    def halo(source, target, sent, landed, device):
        return pltpu.make_async_remote_copy(
            src_ref=source,
            dst_ref=target,
            send_sem=halo_send.at[sent],
            recv_sem=halo_recv.at[landed],
            device_id=device,
            device_id_type=MESH,
        )

    copies = [halo(west_out, east_in, 6, 6, west), halo(east_out, west_in, 7, 7, east)]
    for index, (device, slot) in enumerate(rows):
        source = top_out if index < 3 else bottom_out
        copies.append(halo(source, rows_in.at[slot], index, slot, device))
    for copy in copies:
        copy.start()

    for slot in range(6):
        halo(top_out, rows_in.at[slot], 0, slot, rows[0][0]).wait_recv()
    lane8 = lax.broadcasted_iota(jnp.int32, (8, 192), 0)
    for side in range(2):
        for k in range(4):
            target = cotangent if k == 0 else field
            if k == 0:
                row = 25 * side
            else:
                row = 26 + k if side else 3 - k
            target[row, 0:16] = rows_in[3 * side + 1, k].astype(F32)
            from_west = rows_in[3 * side, k].astype(F32)[8:16]
            from_east = rows_in[3 * side + 2, k].astype(F32)[0:8]
            target[row, 16:24] = jnp.where(lane8 < 4, from_east, from_west)
    copies[0].wait_recv()
    copies[1].wait_recv()
    for half, lanes in enumerate((128, 64)):
        span = slice(128 * half, 128 * half + lanes)
        for target, start, size in ((field, 3, 3), (cotangent, 1, 1)):
            for source, offset in ((east_in, 0), (west_in, 8 - size)):
                arrived = source[half].astype(F32)
                for k in range(size):
                    at_row = 24 * k if size == 3 else 72
                    stage[pl.ds(offset + k, 24, stride=8), :] = arrived[at_row : at_row + 24]
            target[start : start + 24, 16:24, span] = stage.reshape(24, 8, 128)[:, :, 0:lanes]

    for fetch in fetches[2:]:
        fetch.wait()
    keep_shifted(x_store, field[...])
    z1 = outer_convolution(x_store, w1, 28, 2, first, last)
    scale1 = lax.rsqrt(beta1[...] + dot_split(z1 * z1, gamma1[...], ((1,), (1,))))
    hidden = (z1 * scale1).astype(BF16).astype(F32)
    keep_shifted(h_store, hidden.reshape(28, 24, 192))
    z_keep[...] = flat(z1.reshape(28, 24, 192)[2:26, 0:16])
    scale_keep[...] = flat(scale1.reshape(28, 24, 192)[2:26, 0:16])

    z2 = outer_convolution(h_store, w2, 26, 1, first, last)
    sq2 = z2 * z2
    scale2 = lax.rsqrt(beta2[...] + dot_split(sq2, gamma2[...], ((1,), (1,))))
    encoded[...] = (z2 * scale2).reshape(26, 24, 192)[1:25, 0:16].astype(BF16)
    writes[0].start()
    upper = flat(cotangent[...])
    lever2 = upper * z2 * scale2 * scale2 * scale2
    lower2 = upper * scale2 - z2 * dot_split(lever2, gamma2[...])
    grad2 = lower2.astype(BF16).astype(F32).reshape(26, 24, 192)
    keep_shifted(g_store, grad2)

    def inside(value):
        return flat(value.reshape(26, 24, 192)[1:25, 0:16])

    one, two = reductions(grads, scratch)
    pack_gradients(grads.at[1], h_store, 1, inside(grad2), inside(lever2), inside(sq2), turn)
    two.start_core()

    total = None
    blank = jnp.zeros((1, 16, 192), F32)
    for a in range(3):
        for b in range(3):
            shifted = g_store.at[2 - b]
            if a == 0:
                window = jnp.concatenate([shifted[2:25, 0:16], blank], axis=0)
            elif a == 1:
                window = shifted[1:25, 0:16]
            else:
                window = jnp.concatenate([blank, shifted[1:24, 0:16]], axis=0)
            term = dot(flat(window).astype(BF16), w2[3 * a + b], ((1,), (1,)))
            total = term if total is None else total + term
    ghosts = []
    for row, a in ((0, 2 - 2 * first), (25, 2 * last)):
        ghost = None
        for b in range(3):
            term = dot(g_store[2 - b, row, 0:16].astype(BF16), w2[3 * a + b], ((1,), (1,)))
            ghost = term if ghost is None else ghost + term
        ghosts.append(ghost)
    upper1 = jnp.concatenate([total[0:16] + ghosts[0], total[16:368], total[368:384] + ghosts[1]], axis=0)
    two.core_to_x()

    z1 = z_keep[...]
    scale1 = scale_keep[...]
    lever1 = upper1 * z1 * scale1 * scale1 * scale1
    lower1 = upper1 * scale1 - z1 * dot_split(lever1, gamma1[...])
    grad1 = lower1.astype(BF16).astype(F32)
    pack_gradients(grads.at[0], x_store, 2, grad1, lever1, z1 * z1, turn)
    one.start_core()
    two.x_to_y()
    one.core_to_x()
    two.y_to_z()
    one.x_to_y()
    two.z_to_y()
    one.y_to_z()
    two.y_to_x()
    one.z_to_y()
    two.x_to_core()
    one.y_to_x()
    two.core_done()
    two.unpack(out_w2, out_g2, out_b2)
    for write in writes[1:4]:
        write.start()
    one.x_to_core()
    one.core_done()
    one.unpack(out_w1, out_g1, out_b1)
    for write in writes[4:]:
        write.start()
    for copy in copies:
        copy.wait_send()
    two.drain()
    one.drain()
    for write in writes:
        write.wait()


def write_out(*refs):
    sources, targets, held = refs[:7], refs[7:14], refs[14:21]
    came, left = refs[21:]
    order = (1, 4, 0, 2, 5, 3, 6)
    inward = {i: pltpu.make_async_copy(sources[i], held[i], came.at[i]) for i in order}
    outward = {i: pltpu.make_async_copy(held[i], targets[i], left.at[i]) for i in order}
    for i in order:
        inward[i].start()
    for i in order:
        inward[i].wait()
        outward[i].start()
    for i in order:
        outward[i].wait()


def per_device(
    fields,
    first_weight,
    first_gamma,
    first_beta,
    second_weight,
    second_gamma,
    second_beta,
    cotangent,
):
    gradients = [
        jax.ShapeDtypeStruct((9, 192, 192), BF16),
        jax.ShapeDtypeStruct((192, 192), F32),
        jax.ShapeDtypeStruct((1, 192), F32),
    ]
    shape = (3, 3, 192, 192)
    shapes = [jax.ShapeDtypeStruct((24, 16, 192), BF16)] + gradients * 2
    results = pl.pallas_call(
        kernel,
        out_shape=shapes,
        in_specs=[pl.BlockSpec(memory_space=pl.ANY)] * 8,
        out_specs=[pl.BlockSpec(memory_space=pl.ANY)] * 7,
        scratch_shapes=[
            *[pltpu.VMEM(shape.shape, shape.dtype) for shape in shapes],
            pltpu.SemaphoreType.DMA((7,)),
            pltpu.VMEM((2, 2, NX, PART, 128), F32),
            pltpu.VMEM((4, 16, 192), BF16),
            pltpu.VMEM((4, 16, 192), BF16),
            pltpu.VMEM((2, 96, 128), BF16),
            pltpu.VMEM((2, 96, 128), BF16),
            pltpu.VMEM((6, 4, 16, 192), BF16),
            pltpu.VMEM((2, 96, 128), BF16),
            pltpu.VMEM((2, 96, 128), BF16),
            pltpu.SemaphoreType.DMA((8,)),
            pltpu.SemaphoreType.DMA((8,)),
            pltpu.VMEM((30, 24, 192), F32),
            pltpu.VMEM((26, 24, 192), F32),
            pltpu.VMEM((3, 30, 24, 192), F32),
            pltpu.VMEM((3, 28, 24, 192), F32),
            pltpu.VMEM((3, 26, 24, 192), F32),
            pltpu.VMEM((384, 192), F32),
            pltpu.VMEM((384, 192), F32),
            pltpu.VMEM((128, 128), F32),
            pltpu.VMEM((192, 128), F32),
            pltpu.VMEM((2, 96, 128), F32),
            pltpu.VMEM((24, 16, 192), BF16),
            pltpu.VMEM((24, 16, 192), BF16),
            pltpu.VMEM((9, 192, 192), BF16),
            pltpu.VMEM((192, 192), F32),
            pltpu.VMEM((1, 192), F32),
            pltpu.VMEM((9, 192, 192), BF16),
            pltpu.VMEM((192, 192), F32),
            pltpu.VMEM((1, 192), F32),
            pltpu.SemaphoreType.DMA((8,)),
            *reduction_scratch(),
        ],
        compiler_params=pltpu.CompilerParams(
            collective_id=0, has_side_effects=True, vmem_limit_bytes=56 * 1024 * 1024
        ),
    )(
        fields,
        first_weight.reshape(9, 192, 192),
        first_gamma,
        first_beta.reshape(1, 192),
        second_weight.reshape(9, 192, 192),
        second_gamma,
        second_beta.reshape(1, 192),
        cotangent,
    )
    encoded, w1, g1, b1, w2, g2, b2 = pl.pallas_call(
        write_out,
        out_shape=shapes,
        in_specs=[pl.BlockSpec(memory_space=pl.ANY)] * 7,
        out_specs=[pl.BlockSpec(memory_space=pl.ANY)] * 7,
        scratch_shapes=[
            *[pltpu.VMEM(shape.shape, shape.dtype) for shape in shapes],
            pltpu.SemaphoreType.DMA((7,)),
            pltpu.SemaphoreType.DMA((7,)),
        ],
        compiler_params=pltpu.CompilerParams(vmem_limit_bytes=56 * 1024 * 1024),
    )(*results)
    return (encoded, w1.reshape(shape), g1, b1.reshape(192), w2.reshape(shape), g2, b2.reshape(192))


def solution(mesh):
    return jax.shard_map(
        per_device,
        mesh=mesh,
        in_specs=(P("lat", "lon", None), P(), P(), P(), P(), P(), P(), P("lat", "lon", None)),
        out_specs=(P("lat", "lon", None), P(), P(), P(), P(), P(), P()),
        check_vma=False,
    )
```

```python
import jax
import jax.numpy as jnp
from jax import lax
from jax.experimental import pallas as pl
from jax.experimental.pallas import tpu as pltpu
from jax.sharding import PartitionSpec as P

MESH = pl.DeviceIdType.MESH
BF16 = jnp.bfloat16
F32 = jnp.float32
NX, NY, NZ = 4, 8, 8
SIZES = {"x": NX, "y": NY, "z": NZ}
CHUNKS, CHUNK, PIECE = 6, 256, 32
SLOTS = 24


def coordinates():
    lat, lon = lax.axis_index("lat"), lax.axis_index("lon")
    core = lax.rem(lon, 2)
    x = lax.rem(lax.div(lon, 2), NX)
    z = lax.div(lon, 2 * NX) * 2 + lax.rem(lat, 2)
    y = lax.div(lat, 2)
    return core, x, y, z


def at(core, x, y, z):
    return (y * 2 + lax.rem(z, 2), lax.div(z, 2) * (2 * NX) + x * 2 + core)


def partners():
    core, x, y, z = coordinates()
    found = [at(1 - core, x, y, z)]
    found += [at(core, lax.rem(x + d, NX), y, z) for d in range(1, NX)]
    found += [at(core, x, lax.rem(y + d, NY), z) for d in range(1, NY)]
    found += [at(core, x, y, lax.rem(z + d, NZ)) for d in range(1, NZ)]
    return found


class Link:
    def __init__(self, axis, send, recv):
        place = dict(zip(("core", "x", "y", "z"), coordinates()))
        self.size, self.me = SIZES[axis], place[axis]
        self.axis, self.place = axis, place
        self.send_sem, self.recv_sem = send, recv

    def copy(self, source, target, d):
        place = dict(self.place)
        place[self.axis] = lax.rem(self.me + d, self.size)
        return pltpu.make_async_remote_copy(
            src_ref=source,
            dst_ref=target,
            send_sem=self.send_sem,
            recv_sem=self.recv_sem,
            device_id=at(**place),
            device_id_type=MESH,
        )


class Scatter(Link):
    def __init__(self, axis, send, recv, out, into):
        super().__init__(axis, send, recv)
        self.out, self.into = out, into

    def start(self, piece):
        for d in range(1, self.size):
            self.out[d - 1] = piece(lax.rem(self.me + d, self.size)).astype(BF16)
            self.copy(self.out.at[d - 1], self.into.at[d - 1], d).start()

    def finish(self, own):
        self.copy(self.out, self.into, 1).wait_recv()
        total = own
        for d in range(1, self.size):
            total = total + self.into[d - 1].astype(F32)
        return total

    def drain(self):
        self.copy(self.out, self.into, 1).wait_send()


class Share(Link):
    def __init__(self, axis, send, recv, held):
        super().__init__(axis, send, recv)
        self.held = held

    def start(self, value):
        self.held[self.me] = value.astype(BF16)
        for d in range(1, self.size):
            self.copy(self.held.at[self.me], self.held.at[self.me], d).start()

    def others(self):
        span = self.held.at[0 : self.size - 1]
        return self.copy(span, span, 1)

    def finish(self):
        self.others().wait_recv()

    def total(self):
        self.finish()
        total = self.held[0].astype(F32)
        for k in range(1, self.size):
            total = total + self.held[k].astype(F32)
        return total

    def drain(self):
        self.others().wait_send()


class Reduction:
    def __init__(self, layer, grads, core_out, core_in, x_out, x_in, y_out, y_in, z_out, z_in, held8, held4, sums, full, send, recv):
        self.grads, self.full = grads, full
        self.core_out, self.core_in = core_out, core_in
        self.sums = sums
        self.me = coordinates()
        self.send, self.recv = send.at[layer], recv.at[layer]

        def scatter(axis, slot, out, into):
            return Scatter(axis, self.send.at[slot], self.recv.at[slot], out, into)

        def share(axis, slot, held):
            return Share(axis, self.send.at[slot], self.recv.at[slot], held)

        self.a = [
            scatter("x", 3, x_out, x_in),
            scatter("y", 4, y_out.at[0], y_in.at[0]),
            share("z", 5, held8.at[0]),
            share("y", 6, held8.at[1]),
        ]
        self.b = [
            scatter("y", 10, y_out.at[1], y_in.at[1]),
            share("z", 11, held8.at[2]),
            share("x", 12, held4.at[0]),
            share("y", 13, held8.at[3]),
        ]
        self.c = [
            scatter("z", 14, z_out, z_in),
            share("y", 15, held8.at[4]),
            share("x", 16, held4.at[1]),
            share("z", 17, held8.at[5]),
        ]

    def partner_copy(self, slot, source, target):
        core, x, y, z = self.me
        return pltpu.make_async_remote_copy(
            src_ref=source,
            dst_ref=target,
            send_sem=self.send.at[slot],
            recv_sem=self.recv.at[slot],
            device_id=at(1 - core, x, y, z),
            device_id_type=MESH,
        )

    def core_copies(self):
        spans = (slice(0, 4), slice(4, 5), slice(5, 6))
        return [self.partner_copy(i, self.core_out.at[s], self.core_in.at[s]) for i, s in enumerate(spans)]

    def x_gather(self, d, arrival=False):
        core, x, y, z = self.me
        ref = self.full.at[core, lax.rem(x + NX - d, NX) if arrival else x]
        return Link("x", self.send.at[6 + d], self.recv.at[6 + d]).copy(ref, ref, d)

    def core_gather(self, d, arrival=False):
        core, x, y, z = self.me
        chunk = lax.rem(x + NX - d, NX) if d < NX else d
        ref = self.full.at[1 - core if arrival else core, chunk]
        return self.partner_copy(18 + d, ref, ref)

    def half(self, chunk):
        return self.grads[self.me[0], chunk] + self.core_in[chunk].astype(F32)

    def start(self):
        core = self.me[0]
        copies = self.core_copies()
        self.core_out[0:4] = self.grads[1 - core, 0:4].astype(BF16)
        copies[0].start()
        self.core_out[4:6] = self.grads[1 - core, 4:6].astype(BF16)
        copies[1].start()
        copies[2].start()

    def step1(self):
        copies = self.core_copies()
        copies[0].wait_recv()
        self.a[0].start(self.half)
        for i, stream in ((1, self.b), (2, self.c)):
            copies[i].wait_recv()
            self.sums[i] = self.half(3 + i).reshape(8, PIECE, 128)
            stream[0].start(lambda k, i=i: self.sums[i, k])

    def step2(self):
        core, x, y, z = self.me
        self.sums[0] = self.a[0].finish(self.half(x)).reshape(8, PIECE, 128)
        self.a[1].start(lambda k: self.sums[0, k])
        self.b[1].start(self.b[0].finish(self.sums[1, y]))
        self.c[1].start(self.c[0].finish(self.sums[2, z]))

    def step3(self):
        core, x, y, z = self.me
        self.a[2].start(self.a[1].finish(self.sums[0, y]))
        self.b[2].start(self.b[1].total())
        self.c[2].start(self.c[1].total())

    def step4(self):
        self.a[3].start(self.a[2].total())
        self.b[3].start(self.b[2].total())
        self.c[3].start(self.c[2].total())

    def turn(self, share, chunk):
        share.finish()
        whole = share.held[...].astype(F32).reshape(CHUNK, 128)
        for block in range(2):
            rows = slice(block * 128, block * 128 + 128)
            self.full[self.me[0], chunk, rows] = whole[rows].T.astype(BF16)

    def step5(self):
        self.turn(self.a[3], self.me[1])
        for d in range(1, NX):
            self.x_gather(d).start()
        self.core_gather(0).start()
        self.turn(self.b[3], 4)
        self.core_gather(4).start()
        self.turn(self.c[3], 5)
        self.core_gather(5).start()

    def step6(self):
        for d in range(1, NX):
            self.x_gather(d, arrival=True).wait_recv()
            self.core_gather(d).start()

    def step7(self):
        for d in range(CHUNKS):
            self.core_gather(d, arrival=True).wait_recv()

    def drain(self):
        for copy in self.core_copies():
            copy.wait_send()
        for phase in self.a + self.b + self.c:
            phase.drain()
        for d in range(1, NX):
            self.x_gather(d).wait_send()
        for d in range(CHUNKS):
            self.core_gather(d).wait_send()

    def block(self, index):
        core, rest = divmod(index, 12)
        chunk, side = divmod(rest, 2)
        return self.full[core, chunk, side * 128 : side * 128 + 128]

    def unpack(self, wgrad, ggrad, bgrad):
        for tap in range(10):
            pair, odd = divmod(tap, 2)
            low = slice(64 * odd, 64 * odd + 64)
            target = ggrad if tap == 9 else wgrad.at[tap]
            dtype = F32 if tap == 9 else BF16
            target[0:128, 0:128] = self.block(tap).astype(dtype)
            target[0:128, 128:192] = self.block(15 + pair)[:, low].astype(dtype)
            target[128:192, 0:128] = self.block(10 + pair)[low].astype(dtype)
            half, side = divmod(10 + pair, 2)
            corner = self.block(15 + half)[low, 64 * side : 64 * side + 64]
            target[128:192, 128:192] = corner.astype(dtype)
        offsets = self.block(23).astype(F32)
        bgrad[0:1, 0:128] = offsets[0:1]
        bgrad[0:1, 128:192] = offsets[1:2, 0:64]


def reduction_scratch():
    return [
        pltpu.VMEM((2, CHUNKS, CHUNK, 128), BF16),
        pltpu.VMEM((2, CHUNKS, CHUNK, 128), BF16),
        pltpu.VMEM((2, NX - 1, CHUNK, 128), BF16),
        pltpu.VMEM((2, NX - 1, CHUNK, 128), BF16),
        pltpu.VMEM((2, 2, NY - 1, PIECE, 128), BF16),
        pltpu.VMEM((2, 2, NY - 1, PIECE, 128), BF16),
        pltpu.VMEM((2, NZ - 1, PIECE, 128), BF16),
        pltpu.VMEM((2, NZ - 1, PIECE, 128), BF16),
        pltpu.VMEM((2, 6, 8, PIECE, 128), BF16),
        pltpu.VMEM((2, 2, NX, PIECE, 128), BF16),
        pltpu.VMEM((2, 3, 8, PIECE, 128), F32),
        pltpu.VMEM((2, 2, CHUNKS, CHUNK, 128), BF16),
        pltpu.SemaphoreType.DMA((2, SLOTS)),
        pltpu.SemaphoreType.DMA((2, SLOTS)),
    ]


def reductions(grads, scratch):
    *buffers, send, recv = scratch
    return [
        Reduction(layer, grads.at[layer], *[buffer.at[layer] for buffer in buffers], send, recv)
        for layer in range(2)
    ]


def neighbours():
    lat, lon = lax.axis_index("lat"), lax.axis_index("lon")
    lats, lons = lax.axis_size("lat"), lax.axis_size("lon")
    first = (lat == 0).astype(jnp.int32)
    last = (lat == lats - 1).astype(jnp.int32)
    rows = []
    for pole, step, side in ((first, -1, 1), (last, 1, 0)):
        for east in (-1, 0, 1):
            device = (lat + step * (1 - pole), lax.rem(lon + lons + east + pole * (lons // 2), lons))
            landing = side + pole * (1 - 2 * side)
            rows.append((device, landing * 3 + 1 - east))
    west = (lat, lax.rem(lon + lons - 1, lons))
    east = (lat, lax.rem(lon + 1, lons))
    return first, last, rows, west, east


def dot(left, right, dims=((1,), (0,))):
    return lax.dot_general(left, right, (dims, ((), ())), preferred_element_type=F32)


def split(value):
    high = value.astype(BF16)
    return high, (value - high.astype(F32)).astype(BF16)


def dot_split(left, right, dims=((1,), (0,))):
    left_high, left_low = split(left)
    right_high, right_low = split(right)
    return dot(left_high, right_high, dims) + dot(left_high, right_low, dims) + dot(left_low, right_high, dims)


def flat(value):
    return value.reshape(-1, value.shape[-1])


def keep_shifted(store, value):
    store[0] = pltpu.roll(value, 1, axis=1)
    store[1] = value
    store[2] = pltpu.roll(value, 23, axis=1)


def outer_window(store, rows, ghosts, a, b, first, last):
    turned = 2 - 2 * a
    top = store[b, pl.ds(a + first * turned, ghosts)]
    middle = store[b, ghosts + a : rows - ghosts + a]
    bottom = store[b, pl.ds(rows - ghosts + a + last * turned, ghosts)]
    return flat(jnp.concatenate([top, middle, bottom], axis=0)).astype(BF16)


def inner_window(store, a, b, start):
    return flat(store[b, start + a : start + a + 24, 0:16]).astype(BF16)


def outer_convolution(store, weight, rows, ghosts, first, last):
    total = None
    for a in range(3):
        for b in range(3):
            term = dot(outer_window(store, rows, ghosts, a, b, first, last), weight[3 * a + b])
            total = term if total is None else total + term
    return total


def place_block(grads, index, value):
    core, rest = divmod(index, 12)
    chunk, side = divmod(rest, 2)
    grads[core, chunk, side * 128 : side * 128 + 128] = value


def place_lower(grads, tile, value):
    core, rest = divmod(15 + tile // 2, 12)
    chunk, side = divmod(rest, 2)
    start = side * 128 + 64 * (tile % 2)
    grads[core, chunk, start : start + 64] = value


def pack_gradients(grads, store, start, grad, lever, sq, turn):
    turned = grad.T.astype(BF16)
    kept = None
    for tap in range(10):
        if tap < 9:
            block = dot(turned, inner_window(store, tap // 3, tap % 3, start))
        else:
            block = -0.5 * dot_split(sq.T, lever)
        place_block(grads, tap, block[0:128, 0:128])
        place_lower(grads, tap, block[128:192, 0:128])
        if tap % 2 == 0:
            kept = block[:, 128:192]
        else:
            both = jnp.concatenate([kept, block[:, 128:192]], axis=1)
            tile = 10 + tap // 2
            place_block(grads, tile, both[0:128])
            place_lower(grads, tile, both[128:192])
    offsets = -0.5 * jnp.sum(lever, axis=0, keepdims=True)
    turn[...] = jnp.zeros_like(turn)
    turn[0:1, :] = offsets[:, 0:128]
    turn[1:2, 0:64] = offsets[:, 128:192]
    place_lower(grads, 15, jnp.zeros((64, 128), F32))
    place_block(grads, 23, turn[...].T)


def kernel(
    x_far, w1_far, gamma1_far, beta1_far, w2_far, gamma2_far, beta2_far, cot_far,
    encoded, out_w1, out_g1, out_b1, out_w2, out_g2, out_b2,
    grads, top_out, bottom_out, west_out, east_out, rows_in, west_in, east_in, halo_send, halo_recv,
    field, cotangent, x_store, h_store, g_store, z_keep, scale_keep, turn, stage, strips,
    x, cot, w1, gamma1, beta1, w2, gamma2, beta2, fetched, *scratch,
):
    barrier = pltpu.get_barrier_semaphore()
    first, last, rows, west, east = neighbours()
    met = partners() + [device for device, _ in rows] + [west, east]
    for device in met:
        pl.semaphore_signal(barrier, inc=1, device_id=device, device_id_type=MESH)

    pairs = [
        (x_far, x), (cot_far, cot), (w1_far, w1), (gamma1_far, gamma1),
        (beta1_far, beta1), (w2_far, w2), (gamma2_far, gamma2), (beta2_far, beta2),
    ]
    fetches = [pltpu.make_async_copy(far, near, fetched.at[i]) for i, (far, near) in enumerate(pairs)]
    for fetch in fetches:
        fetch.start()
    fetches[0].wait()
    fetches[1].wait()
    field[3:27, 0:16] = x[...].astype(F32)
    cotangent[1:25, 0:16] = cot[...].astype(F32)
    top_out[0] = cot[0]
    bottom_out[0] = cot[23]
    for k in range(3):
        top_out[1 + k] = x[k]
        bottom_out[1 + k] = x[23 - k]

    def strip(target, tile, places, edge):
        for half, lanes in enumerate((128, 64)):
            span = slice(128 * half, 128 * half + lanes)
            for ref, chosen, at_row in ((x, places, 0), (cot, (edge,), 72)):
                stage.reshape(24, 8, 128)[:, :, 0:lanes] = ref[:, tile : tile + 8, span].astype(F32)
                for k, place in enumerate(chosen):
                    rows24 = stage[pl.ds(place - tile, 24, stride=8), :]
                    strips[half, at_row + 24 * k : at_row + 24 * k + 24] = rows24
        target[...] = strips[...].astype(BF16)

    strip(west_out, 0, (0, 1, 2), 0)
    strip(east_out, 8, (13, 14, 15), 15)

    pl.semaphore_wait(barrier, len(met))

    def halo(source, target, sent, landed, device):
        return pltpu.make_async_remote_copy(
            src_ref=source,
            dst_ref=target,
            send_sem=halo_send.at[sent],
            recv_sem=halo_recv.at[landed],
            device_id=device,
            device_id_type=MESH,
        )

    copies = [halo(west_out, east_in, 6, 6, west), halo(east_out, west_in, 7, 7, east)]
    for index, (device, slot) in enumerate(rows):
        source = top_out if index < 3 else bottom_out
        copies.append(halo(source, rows_in.at[slot], index, slot, device))
    for copy in copies:
        copy.start()

    for slot in range(6):
        halo(top_out, rows_in.at[slot], 0, slot, rows[0][0]).wait_recv()
    lane8 = lax.broadcasted_iota(jnp.int32, (8, 192), 0)
    for side in range(2):
        for k in range(4):
            target = cotangent if k == 0 else field
            if k == 0:
                row = 25 * side
            else:
                row = 26 + k if side else 3 - k
            target[row, 0:16] = rows_in[3 * side + 1, k].astype(F32)
            from_west = rows_in[3 * side, k].astype(F32)[8:16]
            from_east = rows_in[3 * side + 2, k].astype(F32)[0:8]
            target[row, 16:24] = jnp.where(lane8 < 4, from_east, from_west)
    copies[0].wait_recv()
    copies[1].wait_recv()
    for half, lanes in enumerate((128, 64)):
        span = slice(128 * half, 128 * half + lanes)
        for target, start, size in ((field, 3, 3), (cotangent, 1, 1)):
            for source, offset in ((east_in, 0), (west_in, 8 - size)):
                arrived = source[half].astype(F32)
                for k in range(size):
                    at_row = 24 * k if size == 3 else 72
                    stage[pl.ds(offset + k, 24, stride=8), :] = arrived[at_row : at_row + 24]
            target[start : start + 24, 16:24, span] = stage.reshape(24, 8, 128)[:, :, 0:lanes]

    for fetch in fetches[2:]:
        fetch.wait()
    keep_shifted(x_store, field[...])
    z1 = outer_convolution(x_store, w1, 28, 2, first, last)
    scale1 = lax.rsqrt(beta1[...] + dot_split(z1 * z1, gamma1[...], ((1,), (1,))))
    hidden = (z1 * scale1).astype(BF16).astype(F32)
    keep_shifted(h_store, hidden.reshape(28, 24, 192))
    z_keep[...] = flat(z1.reshape(28, 24, 192)[2:26, 0:16])
    scale_keep[...] = flat(scale1.reshape(28, 24, 192)[2:26, 0:16])

    z2 = outer_convolution(h_store, w2, 26, 1, first, last)
    sq2 = z2 * z2
    scale2 = lax.rsqrt(beta2[...] + dot_split(sq2, gamma2[...], ((1,), (1,))))
    encoded[...] = (z2 * scale2).reshape(26, 24, 192)[1:25, 0:16].astype(BF16)
    upper = flat(cotangent[...])
    lever2 = upper * z2 * scale2 * scale2 * scale2
    lower2 = upper * scale2 - z2 * dot_split(lever2, gamma2[...])
    grad2 = lower2.astype(BF16).astype(F32).reshape(26, 24, 192)
    keep_shifted(g_store, grad2)

    def inside(value):
        return flat(value.reshape(26, 24, 192)[1:25, 0:16])

    one, two = reductions(grads, scratch)
    pack_gradients(grads.at[1], h_store, 1, inside(grad2), inside(lever2), inside(sq2), turn)
    two.start()

    total = None
    blank = jnp.zeros((1, 16, 192), F32)
    for a in range(3):
        for b in range(3):
            shifted = g_store.at[2 - b]
            if a == 0:
                window = jnp.concatenate([shifted[2:25, 0:16], blank], axis=0)
            elif a == 1:
                window = shifted[1:25, 0:16]
            else:
                window = jnp.concatenate([blank, shifted[1:24, 0:16]], axis=0)
            term = dot(flat(window).astype(BF16), w2[3 * a + b], ((1,), (1,)))
            total = term if total is None else total + term
    ghosts = []
    for row, a in ((0, 2 - 2 * first), (25, 2 * last)):
        ghost = None
        for b in range(3):
            term = dot(g_store[2 - b, row, 0:16].astype(BF16), w2[3 * a + b], ((1,), (1,)))
            ghost = term if ghost is None else ghost + term
        ghosts.append(ghost)
    upper1 = jnp.concatenate([total[0:16] + ghosts[0], total[16:368], total[368:384] + ghosts[1]], axis=0)
    two.step1()

    z1 = z_keep[...]
    scale1 = scale_keep[...]
    lever1 = upper1 * z1 * scale1 * scale1 * scale1
    lower1 = upper1 * scale1 - z1 * dot_split(lever1, gamma1[...])
    grad1 = lower1.astype(BF16).astype(F32)
    pack_gradients(grads.at[0], x_store, 2, grad1, lever1, z1 * z1, turn)
    one.start()
    two.step2()
    one.step1()
    two.step3()
    one.step2()
    two.step4()
    one.step3()
    two.step5()
    one.step4()
    two.step6()
    one.step5()
    two.step7()
    two.unpack(out_w2, out_g2, out_b2)
    one.step6()
    one.step7()
    one.unpack(out_w1, out_g1, out_b1)
    for copy in copies:
        copy.wait_send()
    two.drain()
    one.drain()


def write_out(*refs):
    sources, targets, done = refs[:7], refs[7:14], refs[14]
    copies = [pltpu.make_async_copy(sources[i], targets[i], done.at[i]) for i in (1, 4, 0, 2, 5, 3, 6)]
    for copy in copies:
        copy.start()
    for copy in copies:
        copy.wait()


def per_device(
    fields,
    first_weight,
    first_gamma,
    first_beta,
    second_weight,
    second_gamma,
    second_beta,
    cotangent,
):
    gradients = [
        jax.ShapeDtypeStruct((9, 192, 192), BF16),
        jax.ShapeDtypeStruct((192, 192), F32),
        jax.ShapeDtypeStruct((1, 192), F32),
    ]
    shape = (3, 3, 192, 192)
    shapes = [jax.ShapeDtypeStruct((24, 16, 192), BF16)] + gradients * 2
    anywhere, vmem = pl.BlockSpec(memory_space=pl.ANY), pl.BlockSpec(memory_space=pltpu.VMEM)
    operands = [
        fields,
        first_weight.reshape(9, 192, 192),
        first_gamma,
        first_beta.reshape(1, 192),
        second_weight.reshape(9, 192, 192),
        second_gamma,
        second_beta.reshape(1, 192),
        cotangent,
    ]
    results = pl.pallas_call(
        kernel,
        out_shape=shapes,
        in_specs=[anywhere] * 8,
        out_specs=[vmem] * 7,
        scratch_shapes=[
            pltpu.VMEM((2, 2, CHUNKS, CHUNK, 128), F32),
            pltpu.VMEM((4, 16, 192), BF16),
            pltpu.VMEM((4, 16, 192), BF16),
            pltpu.VMEM((2, 96, 128), BF16),
            pltpu.VMEM((2, 96, 128), BF16),
            pltpu.VMEM((6, 4, 16, 192), BF16),
            pltpu.VMEM((2, 96, 128), BF16),
            pltpu.VMEM((2, 96, 128), BF16),
            pltpu.SemaphoreType.DMA((8,)),
            pltpu.SemaphoreType.DMA((8,)),
            pltpu.VMEM((30, 24, 192), F32),
            pltpu.VMEM((26, 24, 192), F32),
            pltpu.VMEM((3, 30, 24, 192), F32),
            pltpu.VMEM((3, 28, 24, 192), F32),
            pltpu.VMEM((3, 26, 24, 192), F32),
            pltpu.VMEM((384, 192), F32),
            pltpu.VMEM((384, 192), F32),
            pltpu.VMEM((128, 128), F32),
            pltpu.VMEM((192, 128), F32),
            pltpu.VMEM((2, 96, 128), F32),
            pltpu.VMEM((24, 16, 192), BF16),
            pltpu.VMEM((24, 16, 192), BF16),
            pltpu.VMEM((9, 192, 192), BF16),
            pltpu.VMEM((192, 192), F32),
            pltpu.VMEM((1, 192), F32),
            pltpu.VMEM((9, 192, 192), BF16),
            pltpu.VMEM((192, 192), F32),
            pltpu.VMEM((1, 192), F32),
            pltpu.SemaphoreType.DMA((8,)),
            *reduction_scratch(),
        ],
        compiler_params=pltpu.CompilerParams(
            collective_id=0, has_side_effects=True, vmem_limit_bytes=44 * 1024 * 1024
        ),
    )(*[pltpu.with_memory_space_constraint(operand, pltpu.HBM) for operand in operands])
    encoded, w1, g1, b1, w2, g2, b2 = pl.pallas_call(
        write_out,
        out_shape=shapes,
        in_specs=[vmem] * 7,
        out_specs=[anywhere] * 7,
        scratch_shapes=[pltpu.SemaphoreType.DMA((7,))],
        compiler_params=pltpu.CompilerParams(vmem_limit_bytes=8 * 1024 * 1024),
    )(*results)
    return (encoded, w1.reshape(shape), g1, b1.reshape(192), w2.reshape(shape), g2, b2.reshape(192))


def solution(mesh):
    return jax.shard_map(
        per_device,
        mesh=mesh,
        in_specs=(P("lat", "lon", None), P(), P(), P(), P(), P(), P(), P("lat", "lon", None)),
        out_specs=(P("lat", "lon", None), P(), P(), P(), P(), P(), P()),
        check_vma=False,
    )
```

```python
import jax
import jax.numpy as jnp
from jax import lax
from jax.experimental import pallas as pl
from jax.experimental.pallas import tpu as pltpu
from jax.sharding import PartitionSpec as P

MESH = pl.DeviceIdType.MESH
BF16 = jnp.bfloat16
F32 = jnp.float32
NX, NY, NZ = 4, 8, 8
SIZES = {"x": NX, "y": NY, "z": NZ}
BLOCKS = 12
SLOTS = 36


def coordinates():
    lat, lon = lax.axis_index("lat"), lax.axis_index("lon")
    core = lax.rem(lon, 2)
    x = lax.rem(lax.div(lon, 2), NX)
    z = lax.div(lon, 2 * NX) * 2 + lax.rem(lat, 2)
    y = lax.div(lat, 2)
    return core, x, y, z


def at(core, x, y, z):
    return (y * 2 + lax.rem(z, 2), lax.div(z, 2) * (2 * NX) + x * 2 + core)


def partners():
    core, x, y, z = coordinates()
    found = [at(1 - core, x, y, z)]
    found += [at(core, lax.rem(x + d, NX), y, z) for d in range(1, NX)]
    found += [at(core, x, lax.rem(y + d, NY), z) for d in range(1, NY)]
    found += [at(core, x, y, lax.rem(z + d, NZ)) for d in range(1, NZ)]
    return found


def far_first(size):
    return sorted(range(1, size), key=lambda d: -min(d, size - d))


class Link:
    def __init__(self, axis, send, recv):
        place = dict(zip(("core", "x", "y", "z"), coordinates()))
        self.size, self.me = SIZES[axis], place[axis]
        self.axis, self.place = axis, place
        self.send_sem, self.recv_sem = send, recv

    def copy(self, source, target, d):
        place = dict(self.place)
        place[self.axis] = lax.rem(self.me + d, self.size)
        return pltpu.make_async_remote_copy(
            src_ref=source,
            dst_ref=target,
            send_sem=self.send_sem,
            recv_sem=self.recv_sem,
            device_id=at(**place),
            device_id_type=MESH,
        )


class Scatter(Link):
    def __init__(self, axis, send, recv, out, into):
        super().__init__(axis, send, recv)
        self.out, self.into = out, into

    def start(self, piece):
        for d in far_first(self.size):
            self.out[d - 1] = piece(lax.rem(self.me + d, self.size)).astype(BF16)
            self.copy(self.out.at[d - 1], self.into.at[d - 1], d).start()

    def finish(self, own):
        self.copy(self.out, self.into, 1).wait_recv()
        total = own
        for d in range(1, self.size):
            total = total + self.into[d - 1].astype(F32)
        return total

    def drain(self):
        self.copy(self.out, self.into, 1).wait_send()


class Share(Link):
    def __init__(self, axis, send, recv, held):
        super().__init__(axis, send, recv)
        self.held = held

    def start(self, value):
        self.held[self.me] = value.astype(BF16)
        for d in far_first(self.size):
            self.copy(self.held.at[self.me], self.held.at[self.me], d).start()

    def others(self):
        span = self.held.at[0 : self.size - 1]
        return self.copy(span, span, 1)

    def finish(self):
        self.others().wait_recv()

    def total(self):
        self.finish()
        total = self.held[0].astype(F32)
        for k in range(1, self.size):
            total = total + self.held[k].astype(F32)
        return total

    def drain(self):
        self.others().wait_send()


class Reduction:
    def __init__(self, layer, grads, core_out, core_in, x_out, x_in, y_out, y_in, z_out, z_in, y_out2, y_in2, z_out2, z_in2, held16, held32, held4, sums16, sums32, full, send, recv):
        self.grads, self.full = grads, full
        self.core_out, self.core_in = core_out, core_in
        self.me = coordinates()
        self.send, self.recv = send.at[layer], recv.at[layer]
        self.slots = 0
        self.streams = [
            self.twice(0, "x", "y", "z", (x_out.at[0], x_in.at[0]), (y_out, y_in), held16.at[0], held16.at[1], sums16.at[0]),
            self.twice(4, "x", "z", "y", (x_out.at[1], x_in.at[1]), (z_out, z_in), held16.at[2], held16.at[3], sums16.at[1]),
            self.once(8, "y", "x", "z", (y_out2, y_in2), held4.at[0], held32.at[0], held32.at[1], sums32.at[0]),
            self.once(10, "z", "x", "y", (z_out2, z_in2), held4.at[1], held32.at[2], held32.at[3], sums32.at[1]),
        ]

    def slot(self):
        self.slots += 1
        return self.send.at[self.slots - 1], self.recv.at[self.slots - 1]

    def place(self, axis):
        return self.me["xyz".index(axis) + 1]

    def partner_copy(self, sems, source, target):
        core, x, y, z = self.me
        return pltpu.make_async_remote_copy(
            src_ref=source,
            dst_ref=target,
            send_sem=sems[0],
            recv_sem=sems[1],
            device_id=at(1 - core, x, y, z),
            device_id_type=MESH,
        )

    def core_phase(self, first, count):
        sems = self.slot()
        span = slice(first, first + count)
        copy = self.partner_copy(sems, self.core_out.at[span], self.core_in.at[span])

        def start():
            self.core_out[span] = self.grads[1 - self.me[0], span].astype(BF16)
            copy.start()

        return start, copy

    def half(self, block):
        return self.grads[self.me[0], block] + self.core_in[block].astype(F32)

    def turned(self, piece):
        return piece.astype(F32).T.astype(BF16)

    def twice(self, first, axis, second, third, wide, narrow, held, spread, sums):
        core = self.me[0]
        begin, core_copy = self.core_phase(first, 4)
        one = Scatter(axis, *self.slot(), *wide)
        two = Scatter(second, *self.slot(), *narrow)
        three = Share(third, *self.slot(), held)
        four = Share(second, *self.slot(), spread)
        gather_sems = [self.slot() for _ in range(1, NX)]
        last_sems = [self.slot() for _ in range(NX)]
        me, here = self.place(axis), self.place(second)

        def block(d):
            return first + lax.rem(me + NX - d, NX)

        def gather(d, arrival=False):
            ref = self.full.at[core, block(d) if arrival else block(0)]
            return Link(axis, *gather_sems[d - 1]).copy(ref, ref, d)

        def last(d, arrival=False):
            ref = self.full.at[1 - core if arrival else core, block(d)]
            return self.partner_copy(last_sems[d], ref, ref)

        def step1():
            core_copy.wait_recv()
            one.start(lambda k: self.half(first + k))

        def step2():
            sums[...] = one.finish(self.half(first + me)).reshape(sums.shape)
            two.start(lambda k: sums[k])

        def step3():
            three.start(two.finish(sums[here]))

        def step4():
            four.start(three.total())

        def step5():
            four.finish()
            self.full[core, block(0)] = self.turned(spread[...].reshape(128, 128))
            for d in range(1, NX):
                gather(d).start()
            last(0).start()

        def step6():
            for d in range(1, NX):
                gather(d, arrival=True).wait_recv()
                last(d).start()

        def done():
            for d in range(NX):
                last(d, arrival=True).wait_recv()

        def drain():
            core_copy.wait_send()
            for phase in (one, two, three, four):
                phase.drain()
            for d in range(NX):
                last(d).wait_send()
            for d in range(1, NX):
                gather(d).wait_send()

        return (begin, step1, step2, step3, step4, step5, step6, done, drain)

    def once(self, first, axis, second, third, wide, held, held_more, spread, sums):
        core = self.me[0]
        begin, core_copy = self.core_phase(first, 2)
        one = Scatter(axis, *self.slot(), *wide)
        two = Share(second, *self.slot(), held)
        three = Share(third, *self.slot(), held_more)
        four = Share(axis, *self.slot(), spread)
        last_sems = self.slot()
        me = self.place(axis)

        def last(arrival=False):
            ref = self.full.at[1 - core if arrival else core, first : first + 2]
            return self.partner_copy(last_sems, ref, ref)

        def step1():
            core_copy.wait_recv()
            total = self.grads[core, first : first + 2] + self.core_in[first : first + 2].astype(F32)
            sums[...] = total.reshape(sums.shape)
            one.start(lambda k: sums[k])

        def step2():
            two.start(one.finish(sums[me]))

        def step3():
            three.start(two.total())

        def step4():
            four.start(three.total())

        def step5():
            four.finish()
            whole = spread[...].reshape(2, 128, 128)
            for side in range(2):
                self.full[core, first + side] = self.turned(whole[side])
            last().start()

        def step6():
            pass

        def done():
            last(arrival=True).wait_recv()

        def drain():
            core_copy.wait_send()
            for phase in (one, two, three, four):
                phase.drain()
            last().wait_send()

        return (begin, step1, step2, step3, step4, step5, step6, done, drain)

    def step(self, index, streams=(0, 1, 2, 3)):
        for k in streams:
            self.streams[k][index]()

    def drain(self):
        self.step(8)

    def block(self, index):
        return self.full[divmod(index, BLOCKS)]

    def unpack(self, wgrad, ggrad, bgrad):
        for tap in range(10):
            pair, odd = divmod(tap, 2)
            low = slice(64 * odd, 64 * odd + 64)
            target = ggrad if tap == 9 else wgrad.at[tap]
            dtype = F32 if tap == 9 else BF16
            target[0:128, 0:128] = self.block(tap).astype(dtype)
            target[0:128, 128:192] = self.block(15 + pair)[:, low].astype(dtype)
            target[128:192, 0:128] = self.block(10 + pair)[low].astype(dtype)
            half, side = divmod(10 + pair, 2)
            corner = self.block(15 + half)[low, 64 * side : 64 * side + 64]
            target[128:192, 128:192] = corner.astype(dtype)
        offsets = self.block(23).astype(F32)
        bgrad[0:1, 0:128] = offsets[0:1]
        bgrad[0:1, 128:192] = offsets[1:2, 0:64]


def reduction_scratch():
    return [
        pltpu.VMEM((2, BLOCKS, 128, 128), BF16),
        pltpu.VMEM((2, BLOCKS, 128, 128), BF16),
        pltpu.VMEM((2, 2, NX - 1, 128, 128), BF16),
        pltpu.VMEM((2, 2, NX - 1, 128, 128), BF16),
        pltpu.VMEM((2, NY - 1, 16, 128), BF16),
        pltpu.VMEM((2, NY - 1, 16, 128), BF16),
        pltpu.VMEM((2, NZ - 1, 16, 128), BF16),
        pltpu.VMEM((2, NZ - 1, 16, 128), BF16),
        pltpu.VMEM((2, NY - 1, 32, 128), BF16),
        pltpu.VMEM((2, NY - 1, 32, 128), BF16),
        pltpu.VMEM((2, NZ - 1, 32, 128), BF16),
        pltpu.VMEM((2, NZ - 1, 32, 128), BF16),
        pltpu.VMEM((2, 4, 8, 16, 128), BF16),
        pltpu.VMEM((2, 4, 8, 32, 128), BF16),
        pltpu.VMEM((2, 2, NX, 32, 128), BF16),
        pltpu.VMEM((2, 2, 8, 16, 128), F32),
        pltpu.VMEM((2, 2, 8, 32, 128), F32),
        pltpu.VMEM((2, 2, BLOCKS, 128, 128), BF16),
        pltpu.SemaphoreType.DMA((2, SLOTS)),
        pltpu.SemaphoreType.DMA((2, SLOTS)),
    ]


def reductions(grads, scratch):
    *buffers, send, recv = scratch
    return [
        Reduction(layer, grads.at[layer], *[buffer.at[layer] for buffer in buffers], send, recv)
        for layer in range(2)
    ]


def neighbours():
    lat, lon = lax.axis_index("lat"), lax.axis_index("lon")
    lats, lons = lax.axis_size("lat"), lax.axis_size("lon")
    first = (lat == 0).astype(jnp.int32)
    last = (lat == lats - 1).astype(jnp.int32)
    rows = []
    for pole, step, side in ((first, -1, 1), (last, 1, 0)):
        for east in (-1, 0, 1):
            device = (lat + step * (1 - pole), lax.rem(lon + lons + east + pole * (lons // 2), lons))
            landing = side + pole * (1 - 2 * side)
            rows.append((device, landing * 3 + 1 - east))
    west = (lat, lax.rem(lon + lons - 1, lons))
    east = (lat, lax.rem(lon + 1, lons))
    return first, last, rows, west, east


def dot(left, right, dims=((1,), (0,))):
    return lax.dot_general(left, right, (dims, ((), ())), preferred_element_type=F32)


def split(value):
    high = value.astype(BF16)
    return high, (value - high.astype(F32)).astype(BF16)


def dot_split(left, right, dims=((1,), (0,))):
    left_high, left_low = split(left)
    right_high, right_low = split(right)
    return dot(left_high, right_high, dims) + dot(left_high, right_low, dims) + dot(left_low, right_high, dims)


def flat(value):
    return value.reshape(-1, value.shape[-1])


def keep_shifted(store, value):
    store[0] = pltpu.roll(value, 1, axis=1)
    store[1] = value
    store[2] = pltpu.roll(value, 23, axis=1)


def outer_window(store, rows, ghosts, a, b, first, last):
    turned = 2 - 2 * a
    top = store[b, pl.ds(a + first * turned, ghosts)]
    middle = store[b, ghosts + a : rows - ghosts + a]
    bottom = store[b, pl.ds(rows - ghosts + a + last * turned, ghosts)]
    return flat(jnp.concatenate([top, middle, bottom], axis=0)).astype(BF16)


def inner_window(store, a, b, start):
    return flat(store[b, start + a : start + a + 24, 0:16]).astype(BF16)


def outer_convolution(store, weight, rows, ghosts, first, last):
    total = None
    for a in range(3):
        for b in range(3):
            term = dot(outer_window(store, rows, ghosts, a, b, first, last), weight[3 * a + b])
            total = term if total is None else total + term
    return total


def place_block(grads, index, value):
    core, block = divmod(index, BLOCKS)
    grads[core, block] = value


def place_lower(grads, tile, value):
    core, block = divmod(15 + tile // 2, BLOCKS)
    start = 64 * (tile % 2)
    grads[core, block, start : start + 64] = value


def pack_gradients(grads, store, start, grad, lever, sq, turn):
    turned = grad.T.astype(BF16)
    kept = None
    for tap in range(10):
        if tap < 9:
            block = dot(turned, inner_window(store, tap // 3, tap % 3, start))
        else:
            block = -0.5 * dot_split(sq.T, lever)
        place_block(grads, tap, block[0:128, 0:128])
        place_lower(grads, tap, block[128:192, 0:128])
        if tap % 2 == 0:
            kept = block[:, 128:192]
        else:
            both = jnp.concatenate([kept, block[:, 128:192]], axis=1)
            tile = 10 + tap // 2
            place_block(grads, tile, both[0:128])
            place_lower(grads, tile, both[128:192])
    offsets = -0.5 * jnp.sum(lever, axis=0, keepdims=True)
    turn[...] = jnp.zeros_like(turn)
    turn[0:1, :] = offsets[:, 0:128]
    turn[1:2, 0:64] = offsets[:, 128:192]
    place_lower(grads, 15, jnp.zeros((64, 128), F32))
    place_block(grads, 23, turn[...].T)


def kernel(
    x_far, w1_far, gamma1_far, beta1_far, w2_far, gamma2_far, beta2_far, cot_far,
    encoded, out_w1, out_g1, out_b1, out_w2, out_g2, out_b2,
    grads, top_out, bottom_out, west_out, east_out, rows_in, west_in, east_in, halo_send, halo_recv,
    field, cotangent, x_store, h_store, g_store, z_keep, scale_keep, turn, stage, strips,
    x, cot, w1, gamma1, beta1, w2, gamma2, beta2, fetched, *scratch,
):
    barrier = pltpu.get_barrier_semaphore()
    first, last, rows, west, east = neighbours()
    met = partners() + [device for device, _ in rows] + [west, east]
    for device in met:
        pl.semaphore_signal(barrier, inc=1, device_id=device, device_id_type=MESH)

    pairs = [
        (x_far, x), (cot_far, cot), (w1_far, w1), (gamma1_far, gamma1),
        (beta1_far, beta1), (w2_far, w2), (gamma2_far, gamma2), (beta2_far, beta2),
    ]
    fetches = [pltpu.make_async_copy(far, near, fetched.at[i]) for i, (far, near) in enumerate(pairs)]
    for fetch in fetches:
        fetch.start()
    fetches[0].wait()
    fetches[1].wait()
    field[3:27, 0:16] = x[...].astype(F32)
    cotangent[1:25, 0:16] = cot[...].astype(F32)
    top_out[0] = cot[0]
    bottom_out[0] = cot[23]
    for k in range(3):
        top_out[1 + k] = x[k]
        bottom_out[1 + k] = x[23 - k]

    def strip(target, tile, places, edge):
        for half, lanes in enumerate((128, 64)):
            span = slice(128 * half, 128 * half + lanes)
            for ref, chosen, at_row in ((x, places, 0), (cot, (edge,), 72)):
                stage.reshape(24, 8, 128)[:, :, 0:lanes] = ref[:, tile : tile + 8, span].astype(F32)
                for k, place in enumerate(chosen):
                    rows24 = stage[pl.ds(place - tile, 24, stride=8), :]
                    strips[half, at_row + 24 * k : at_row + 24 * k + 24] = rows24
        target[...] = strips[...].astype(BF16)

    strip(west_out, 0, (0, 1, 2), 0)
    strip(east_out, 8, (13, 14, 15), 15)

    pl.semaphore_wait(barrier, len(met))

    def halo(source, target, sent, landed, device):
        return pltpu.make_async_remote_copy(
            src_ref=source,
            dst_ref=target,
            send_sem=halo_send.at[sent],
            recv_sem=halo_recv.at[landed],
            device_id=device,
            device_id_type=MESH,
        )

    copies = [halo(west_out, east_in, 6, 6, west), halo(east_out, west_in, 7, 7, east)]
    for index, (device, slot) in enumerate(rows):
        source = top_out if index < 3 else bottom_out
        copies.append(halo(source, rows_in.at[slot], index, slot, device))
    for copy in copies:
        copy.start()

    for slot in range(6):
        halo(top_out, rows_in.at[slot], 0, slot, rows[0][0]).wait_recv()
    lane8 = lax.broadcasted_iota(jnp.int32, (8, 192), 0)
    for side in range(2):
        for k in range(4):
            target = cotangent if k == 0 else field
            if k == 0:
                row = 25 * side
            else:
                row = 26 + k if side else 3 - k
            target[row, 0:16] = rows_in[3 * side + 1, k].astype(F32)
            from_west = rows_in[3 * side, k].astype(F32)[8:16]
            from_east = rows_in[3 * side + 2, k].astype(F32)[0:8]
            target[row, 16:24] = jnp.where(lane8 < 4, from_east, from_west)
    copies[0].wait_recv()
    copies[1].wait_recv()
    for half, lanes in enumerate((128, 64)):
        span = slice(128 * half, 128 * half + lanes)
        for target, start, size in ((field, 3, 3), (cotangent, 1, 1)):
            for source, offset in ((east_in, 0), (west_in, 8 - size)):
                arrived = source[half].astype(F32)
                for k in range(size):
                    at_row = 24 * k if size == 3 else 72
                    stage[pl.ds(offset + k, 24, stride=8), :] = arrived[at_row : at_row + 24]
            target[start : start + 24, 16:24, span] = stage.reshape(24, 8, 128)[:, :, 0:lanes]

    for fetch in fetches[2:]:
        fetch.wait()
    keep_shifted(x_store, field[...])
    z1 = outer_convolution(x_store, w1, 28, 2, first, last)
    scale1 = lax.rsqrt(beta1[...] + dot_split(z1 * z1, gamma1[...], ((1,), (1,))))
    hidden = (z1 * scale1).astype(BF16).astype(F32)
    keep_shifted(h_store, hidden.reshape(28, 24, 192))
    z_keep[...] = flat(z1.reshape(28, 24, 192)[2:26, 0:16])
    scale_keep[...] = flat(scale1.reshape(28, 24, 192)[2:26, 0:16])

    z2 = outer_convolution(h_store, w2, 26, 1, first, last)
    sq2 = z2 * z2
    scale2 = lax.rsqrt(beta2[...] + dot_split(sq2, gamma2[...], ((1,), (1,))))
    encoded[...] = (z2 * scale2).reshape(26, 24, 192)[1:25, 0:16].astype(BF16)
    upper = flat(cotangent[...])
    lever2 = upper * z2 * scale2 * scale2 * scale2
    lower2 = upper * scale2 - z2 * dot_split(lever2, gamma2[...])
    grad2 = lower2.astype(BF16).astype(F32).reshape(26, 24, 192)
    keep_shifted(g_store, grad2)

    def inside(value):
        return flat(value.reshape(26, 24, 192)[1:25, 0:16])

    one, two = reductions(grads, scratch)
    pack_gradients(grads.at[1], h_store, 1, inside(grad2), inside(lever2), inside(sq2), turn)
    two.step(0)

    total = None
    blank = jnp.zeros((1, 16, 192), F32)
    for a in range(3):
        for b in range(3):
            shifted = g_store.at[2 - b]
            if a == 0:
                window = jnp.concatenate([shifted[2:25, 0:16], blank], axis=0)
            elif a == 1:
                window = shifted[1:25, 0:16]
            else:
                window = jnp.concatenate([blank, shifted[1:24, 0:16]], axis=0)
            term = dot(flat(window).astype(BF16), w2[3 * a + b], ((1,), (1,)))
            total = term if total is None else total + term
    ghosts = []
    for row, a in ((0, 2 - 2 * first), (25, 2 * last)):
        ghost = None
        for b in range(3):
            term = dot(g_store[2 - b, row, 0:16].astype(BF16), w2[3 * a + b], ((1,), (1,)))
            ghost = term if ghost is None else ghost + term
        ghosts.append(ghost)
    upper1 = jnp.concatenate([total[0:16] + ghosts[0], total[16:368], total[368:384] + ghosts[1]], axis=0)
    two.step(1)

    z1 = z_keep[...]
    scale1 = scale_keep[...]
    lever1 = upper1 * z1 * scale1 * scale1 * scale1
    lower1 = upper1 * scale1 - z1 * dot_split(lever1, gamma1[...])
    grad1 = lower1.astype(BF16).astype(F32)
    pack_gradients(grads.at[0], x_store, 2, grad1, lever1, z1 * z1, turn)
    one.step(0)
    one.step(1)
    two.step(2)
    for index in range(2, 7):
        one.step(index)
        two.step(index + 1)
    two.unpack(out_w2, out_g2, out_b2)
    one.step(7)
    one.unpack(out_w1, out_g1, out_b1)
    for copy in copies:
        copy.wait_send()
    two.drain()
    one.drain()


def write_out(*refs):
    sources, targets, done = refs[:7], refs[7:14], refs[14]
    copies = [pltpu.make_async_copy(sources[i], targets[i], done.at[i]) for i in (1, 4, 0, 2, 5, 3, 6)]
    for copy in copies:
        copy.start()
    for copy in copies:
        copy.wait()


def per_device(
    fields,
    first_weight,
    first_gamma,
    first_beta,
    second_weight,
    second_gamma,
    second_beta,
    cotangent,
):
    gradients = [
        jax.ShapeDtypeStruct((9, 192, 192), BF16),
        jax.ShapeDtypeStruct((192, 192), F32),
        jax.ShapeDtypeStruct((1, 192), F32),
    ]
    shape = (3, 3, 192, 192)
    shapes = [jax.ShapeDtypeStruct((24, 16, 192), BF16)] + gradients * 2
    anywhere, vmem = pl.BlockSpec(memory_space=pl.ANY), pl.BlockSpec(memory_space=pltpu.VMEM)
    operands = [
        fields,
        first_weight.reshape(9, 192, 192),
        first_gamma,
        first_beta.reshape(1, 192),
        second_weight.reshape(9, 192, 192),
        second_gamma,
        second_beta.reshape(1, 192),
        cotangent,
    ]
    results = pl.pallas_call(
        kernel,
        out_shape=shapes,
        in_specs=[anywhere] * 8,
        out_specs=[vmem] * 7,
        scratch_shapes=[
            pltpu.VMEM((2, 2, BLOCKS, 128, 128), F32),
            pltpu.VMEM((4, 16, 192), BF16),
            pltpu.VMEM((4, 16, 192), BF16),
            pltpu.VMEM((2, 96, 128), BF16),
            pltpu.VMEM((2, 96, 128), BF16),
            pltpu.VMEM((6, 4, 16, 192), BF16),
            pltpu.VMEM((2, 96, 128), BF16),
            pltpu.VMEM((2, 96, 128), BF16),
            pltpu.SemaphoreType.DMA((8,)),
            pltpu.SemaphoreType.DMA((8,)),
            pltpu.VMEM((30, 24, 192), F32),
            pltpu.VMEM((26, 24, 192), F32),
            pltpu.VMEM((3, 30, 24, 192), F32),
            pltpu.VMEM((3, 28, 24, 192), F32),
            pltpu.VMEM((3, 26, 24, 192), F32),
            pltpu.VMEM((384, 192), F32),
            pltpu.VMEM((384, 192), F32),
            pltpu.VMEM((128, 128), F32),
            pltpu.VMEM((192, 128), F32),
            pltpu.VMEM((2, 96, 128), F32),
            pltpu.VMEM((24, 16, 192), BF16),
            pltpu.VMEM((24, 16, 192), BF16),
            pltpu.VMEM((9, 192, 192), BF16),
            pltpu.VMEM((192, 192), F32),
            pltpu.VMEM((1, 192), F32),
            pltpu.VMEM((9, 192, 192), BF16),
            pltpu.VMEM((192, 192), F32),
            pltpu.VMEM((1, 192), F32),
            pltpu.SemaphoreType.DMA((8,)),
            *reduction_scratch(),
        ],
        compiler_params=pltpu.CompilerParams(
            collective_id=0, has_side_effects=True, vmem_limit_bytes=44 * 1024 * 1024
        ),
    )(*[pltpu.with_memory_space_constraint(operand, pltpu.HBM) for operand in operands])
    encoded, w1, g1, b1, w2, g2, b2 = pl.pallas_call(
        write_out,
        out_shape=shapes,
        in_specs=[vmem] * 7,
        out_specs=[anywhere] * 7,
        scratch_shapes=[pltpu.SemaphoreType.DMA((7,))],
        compiler_params=pltpu.CompilerParams(vmem_limit_bytes=8 * 1024 * 1024),
    )(*results)
    return (encoded, w1.reshape(shape), g1, b1.reshape(192), w2.reshape(shape), g2, b2.reshape(192))


def solution(mesh):
    return jax.shard_map(
        per_device,
        mesh=mesh,
        in_specs=(P("lat", "lon", None), P(), P(), P(), P(), P(), P(), P("lat", "lon", None)),
        out_specs=(P("lat", "lon", None), P(), P(), P(), P(), P(), P()),
        check_vma=False,
    )
```

```python
import jax
import jax.numpy as jnp
from jax import lax
from jax.experimental import pallas as pl
from jax.experimental.pallas import tpu as pltpu
from jax.sharding import PartitionSpec as P

MESH = pl.DeviceIdType.MESH
BF16 = jnp.bfloat16
F32 = jnp.float32
NX, NY, NZ = 4, 8, 8
SIZES = {"x": NX, "y": NY, "z": NZ}
BLOCKS = 12
SLOTS = 36


def coordinates():
    lat, lon = lax.axis_index("lat"), lax.axis_index("lon")
    core = lax.rem(lon, 2)
    x = lax.rem(lax.div(lon, 2), NX)
    z = lax.div(lon, 2 * NX) * 2 + lax.rem(lat, 2)
    y = lax.div(lat, 2)
    return core, x, y, z


def at(core, x, y, z):
    return (y * 2 + lax.rem(z, 2), lax.div(z, 2) * (2 * NX) + x * 2 + core)


def partners():
    core, x, y, z = coordinates()
    found = [at(1 - core, x, y, z)]
    found += [at(core, lax.rem(x + d, NX), y, z) for d in range(1, NX)]
    found += [at(core, x, lax.rem(y + d, NY), z) for d in range(1, NY)]
    found += [at(core, x, y, lax.rem(z + d, NZ)) for d in range(1, NZ)]
    return found


def far_first(size):
    return sorted(range(1, size), key=lambda d: -min(d, size - d))


class Link:
    def __init__(self, axis, send, recv):
        place = dict(zip(("core", "x", "y", "z"), coordinates()))
        self.size, self.me = SIZES[axis], place[axis]
        self.axis, self.place = axis, place
        self.send_sem, self.recv_sem = send, recv

    def copy(self, source, target, d):
        place = dict(self.place)
        place[self.axis] = lax.rem(self.me + d, self.size)
        return pltpu.make_async_remote_copy(
            src_ref=source,
            dst_ref=target,
            send_sem=self.send_sem,
            recv_sem=self.recv_sem,
            device_id=at(**place),
            device_id_type=MESH,
        )


class Scatter(Link):
    def __init__(self, axis, send, recv, out, into):
        super().__init__(axis, send, recv)
        self.out, self.into = out, into

    def start(self, piece):
        for d in far_first(self.size):
            self.out[d - 1] = piece(lax.rem(self.me + d, self.size)).astype(BF16)
            self.copy(self.out.at[d - 1], self.into.at[d - 1], d).start()

    def finish(self, own):
        self.copy(self.out, self.into, 1).wait_recv()
        total = own
        for d in range(1, self.size):
            total = total + self.into[d - 1].astype(F32)
        return total

    def drain(self):
        self.copy(self.out, self.into, 1).wait_send()


class Share(Link):
    def __init__(self, axis, send, recv, held):
        super().__init__(axis, send, recv)
        self.held = held

    def start(self, value):
        self.held[self.me] = value.astype(BF16)
        for d in far_first(self.size):
            self.copy(self.held.at[self.me], self.held.at[self.me], d).start()

    def others(self):
        span = self.held.at[0 : self.size - 1]
        return self.copy(span, span, 1)

    def finish(self):
        self.others().wait_recv()

    def total(self):
        self.finish()
        total = self.held[0].astype(F32)
        for k in range(1, self.size):
            total = total + self.held[k].astype(F32)
        return total

    def drain(self):
        self.others().wait_send()


class Reduction:
    def __init__(self, layer, grads, core_out, core_in, x_out, x_in, y_out, y_in, z_out, z_in, y_out2, y_in2, z_out2, z_in2, held16, held32, held4, sums16, sums32, full, send, recv):
        self.grads, self.full = grads, full
        self.core_out, self.core_in = core_out, core_in
        self.me = coordinates()
        self.send, self.recv = send.at[layer], recv.at[layer]
        self.slots = 0
        self.streams = [
            self.twice(0, "x", "y", "z", (x_out.at[0], x_in.at[0]), (y_out, y_in), held16.at[0], held16.at[1], sums16.at[0]),
            self.twice(4, "x", "z", "y", (x_out.at[1], x_in.at[1]), (z_out, z_in), held16.at[2], held16.at[3], sums16.at[1]),
            self.once(8, "y", "x", "z", (y_out2, y_in2), held4.at[0], held32.at[0], held32.at[1], sums32.at[0]),
            self.once(10, "z", "x", "y", (z_out2, z_in2), held4.at[1], held32.at[2], held32.at[3], sums32.at[1]),
        ]

    def slot(self):
        self.slots += 1
        return self.send.at[self.slots - 1], self.recv.at[self.slots - 1]

    def place(self, axis):
        return self.me["xyz".index(axis) + 1]

    def partner_copy(self, sems, source, target):
        core, x, y, z = self.me
        return pltpu.make_async_remote_copy(
            src_ref=source,
            dst_ref=target,
            send_sem=sems[0],
            recv_sem=sems[1],
            device_id=at(1 - core, x, y, z),
            device_id_type=MESH,
        )

    def core_phase(self, first, count):
        sems = self.slot()
        span = slice(first, first + count)
        copy = self.partner_copy(sems, self.core_out.at[span], self.core_in.at[span])

        def start():
            self.core_out[span] = self.grads[1 - self.me[0], span].astype(BF16)
            copy.start()

        return start, copy

    def half(self, block):
        return self.grads[self.me[0], block] + self.core_in[block].astype(F32)

    def turned(self, piece):
        return piece.astype(F32).T.astype(BF16)

    def twice(self, first, axis, second, third, wide, narrow, held, spread, sums):
        core = self.me[0]
        begin, core_copy = self.core_phase(first, 4)
        one = Scatter(axis, *self.slot(), *wide)
        two = Scatter(second, *self.slot(), *narrow)
        three = Share(third, *self.slot(), held)
        four = Share(second, *self.slot(), spread)
        gather_sems = [self.slot() for _ in range(1, NX)]
        last_sems = [self.slot() for _ in range(NX)]
        me, here = self.place(axis), self.place(second)

        def block(d):
            return first + lax.rem(me + NX - d, NX)

        def gather(d, arrival=False):
            ref = self.full.at[core, block(d) if arrival else block(0)]
            return Link(axis, *gather_sems[d - 1]).copy(ref, ref, d)

        def last(d, arrival=False):
            ref = self.full.at[1 - core if arrival else core, block(d)]
            return self.partner_copy(last_sems[d], ref, ref)

        def step1():
            core_copy.wait_recv()
            one.start(lambda k: self.half(first + k))

        def step2():
            sums[...] = one.finish(self.half(first + me)).reshape(sums.shape)
            two.start(lambda k: sums[k])

        def step3():
            three.start(two.finish(sums[here]))

        def step4():
            four.start(three.total())

        def step5():
            four.finish()
            self.full[core, block(0)] = self.turned(spread[...].reshape(128, 128))
            for d in range(1, NX):
                gather(d).start()
            last(0).start()

        def step6():
            for d in range(1, NX):
                gather(d, arrival=True).wait_recv()
                last(d).start()

        def done():
            for d in range(NX):
                last(d, arrival=True).wait_recv()

        def drain():
            core_copy.wait_send()
            for phase in (one, two, three, four):
                phase.drain()
            for d in range(NX):
                last(d).wait_send()
            for d in range(1, NX):
                gather(d).wait_send()

        return (begin, step1, step2, step3, step4, step5, step6, done, drain)

    def once(self, first, axis, second, third, wide, held, held_more, spread, sums):
        core = self.me[0]
        begin, core_copy = self.core_phase(first, 2)
        one = Scatter(axis, *self.slot(), *wide)
        two = Share(second, *self.slot(), held)
        three = Share(third, *self.slot(), held_more)
        four = Share(axis, *self.slot(), spread)
        last_sems = self.slot()
        me = self.place(axis)

        def last(arrival=False):
            ref = self.full.at[1 - core if arrival else core, first : first + 2]
            return self.partner_copy(last_sems, ref, ref)

        def step1():
            core_copy.wait_recv()
            total = self.grads[core, first : first + 2] + self.core_in[first : first + 2].astype(F32)
            sums[...] = total.reshape(sums.shape)
            one.start(lambda k: sums[k])

        def step2():
            two.start(one.finish(sums[me]))

        def step3():
            three.start(two.total())

        def step4():
            four.start(three.total())

        def step5():
            four.finish()
            whole = spread[...].reshape(2, 128, 128)
            for side in range(2):
                self.full[core, first + side] = self.turned(whole[side])
            last().start()

        def step6():
            pass

        def done():
            last(arrival=True).wait_recv()

        def drain():
            core_copy.wait_send()
            for phase in (one, two, three, four):
                phase.drain()
            last().wait_send()

        return (begin, step1, step2, step3, step4, step5, step6, done, drain)

    def step(self, index, streams=(0, 1, 2, 3)):
        for k in streams:
            self.streams[k][index]()

    def drain(self):
        self.step(8)

    def block(self, index):
        return self.full[divmod(index, BLOCKS)]

    def unpack(self, wgrad, ggrad, bgrad):
        for tap in range(10):
            pair, odd = divmod(tap, 2)
            low = slice(64 * odd, 64 * odd + 64)
            target = ggrad if tap == 9 else wgrad.at[tap]
            dtype = F32 if tap == 9 else BF16
            target[0:128, 0:128] = self.block(tap).astype(dtype)
            target[0:128, 128:192] = self.block(15 + pair)[:, low].astype(dtype)
            target[128:192, 0:128] = self.block(10 + pair)[low].astype(dtype)
            half, side = divmod(10 + pair, 2)
            corner = self.block(15 + half)[low, 64 * side : 64 * side + 64]
            target[128:192, 128:192] = corner.astype(dtype)
        offsets = self.block(23).astype(F32)
        bgrad[0:1, 0:128] = offsets[0:1]
        bgrad[0:1, 128:192] = offsets[1:2, 0:64]


def reduction_scratch():
    return [
        pltpu.VMEM((2, BLOCKS, 128, 128), BF16),
        pltpu.VMEM((2, BLOCKS, 128, 128), BF16),
        pltpu.VMEM((2, 2, NX - 1, 128, 128), BF16),
        pltpu.VMEM((2, 2, NX - 1, 128, 128), BF16),
        pltpu.VMEM((2, NY - 1, 16, 128), BF16),
        pltpu.VMEM((2, NY - 1, 16, 128), BF16),
        pltpu.VMEM((2, NZ - 1, 16, 128), BF16),
        pltpu.VMEM((2, NZ - 1, 16, 128), BF16),
        pltpu.VMEM((2, NY - 1, 32, 128), BF16),
        pltpu.VMEM((2, NY - 1, 32, 128), BF16),
        pltpu.VMEM((2, NZ - 1, 32, 128), BF16),
        pltpu.VMEM((2, NZ - 1, 32, 128), BF16),
        pltpu.VMEM((2, 4, 8, 16, 128), BF16),
        pltpu.VMEM((2, 4, 8, 32, 128), BF16),
        pltpu.VMEM((2, 2, NX, 32, 128), BF16),
        pltpu.VMEM((2, 2, 8, 16, 128), F32),
        pltpu.VMEM((2, 2, 8, 32, 128), F32),
        pltpu.VMEM((2, 2, BLOCKS, 128, 128), BF16),
        pltpu.SemaphoreType.DMA((2, SLOTS)),
        pltpu.SemaphoreType.DMA((2, SLOTS)),
    ]


def reductions(grads, scratch):
    *buffers, send, recv = scratch
    return [
        Reduction(layer, grads.at[layer], *[buffer.at[layer] for buffer in buffers], send, recv)
        for layer in range(2)
    ]


def neighbours():
    lat, lon = lax.axis_index("lat"), lax.axis_index("lon")
    lats, lons = lax.axis_size("lat"), lax.axis_size("lon")
    first = (lat == 0).astype(jnp.int32)
    last = (lat == lats - 1).astype(jnp.int32)
    rows = []
    for pole, step, side in ((first, -1, 1), (last, 1, 0)):
        for east in (-1, 0, 1):
            device = (lat + step * (1 - pole), lax.rem(lon + lons + east + pole * (lons // 2), lons))
            landing = side + pole * (1 - 2 * side)
            rows.append((device, 4 + landing if east == 0 else 2 * landing + (1 - east) // 2))
    west = (lat, lax.rem(lon + lons - 1, lons))
    east = (lat, lax.rem(lon + 1, lons))
    return first, last, rows, west, east


def dot(left, right, dims=((1,), (0,))):
    return lax.dot_general(left, right, (dims, ((), ())), preferred_element_type=F32)


def split(value):
    high = value.astype(BF16)
    return high, (value - high.astype(F32)).astype(BF16)


def dot_split(left, right, dims=((1,), (0,))):
    left_high, left_low = split(left)
    right_high, right_low = split(right)
    return dot(left_high, right_high, dims) + dot(left_high, right_low, dims) + dot(left_low, right_high, dims)


def flat(value):
    return value.reshape(-1, value.shape[-1])


def keep_shifted(store, value, rows=slice(None)):
    store[0, rows] = pltpu.roll(value, 1, axis=1)
    store[1, rows] = value
    store[2, rows] = pltpu.roll(value, 23, axis=1)


def outer_window(store, rows, ghosts, a, b, first, last):
    turned = 2 - 2 * a
    top = store[b, pl.ds(a + first * turned, ghosts)]
    middle = store[b, ghosts + a : rows - ghosts + a]
    bottom = store[b, pl.ds(rows - ghosts + a + last * turned, ghosts)]
    return flat(jnp.concatenate([top, middle, bottom], axis=0)).astype(BF16)


def inner_window(store, a, b, start):
    return flat(store[b, start + a : start + a + 24, 0:16]).astype(BF16)


def outer_convolution(store, weight, rows, ghosts, first, last):
    total = None
    for a in range(3):
        for b in range(3):
            term = dot(outer_window(store, rows, ghosts, a, b, first, last), weight[3 * a + b])
            total = term if total is None else total + term
    return total


def place_block(grads, index, value):
    core, block = divmod(index, BLOCKS)
    grads[core, block] = value


def place_lower(grads, tile, value):
    core, block = divmod(15 + tile // 2, BLOCKS)
    start = 64 * (tile % 2)
    grads[core, block, start : start + 64] = value


def pack_gradients(grads, store, start, grad, lever, sq, turn):
    turned = grad.T.astype(BF16)
    kept = None
    for tap in range(10):
        if tap < 9:
            block = dot(turned, inner_window(store, tap // 3, tap % 3, start))
        else:
            block = -0.5 * dot_split(sq.T, lever)
        place_block(grads, tap, block[0:128, 0:128])
        place_lower(grads, tap, block[128:192, 0:128])
        if tap % 2 == 0:
            kept = block[:, 128:192]
        else:
            both = jnp.concatenate([kept, block[:, 128:192]], axis=1)
            tile = 10 + tap // 2
            place_block(grads, tile, both[0:128])
            place_lower(grads, tile, both[128:192])
    offsets = -0.5 * jnp.sum(lever, axis=0, keepdims=True)
    turn[...] = jnp.zeros_like(turn)
    turn[0:1, :] = offsets[:, 0:128]
    turn[1:2, 0:64] = offsets[:, 128:192]
    place_lower(grads, 15, jnp.zeros((64, 128), F32))
    place_block(grads, 23, turn[...].T)


def normal_scale(z, gamma, beta):
    return lax.rsqrt(beta[...] + dot_split(z * z, gamma[...], ((1,), (1,))))


def first_kernel(
    x_far, w1_far, gamma1_far, beta1_far, w2_far, gamma2_far, beta2_far, cot_far,
    cotangent, x_store, h_store, z_keep, scale_keep, gamma1, w2, gamma2, beta2,
    x, cot, w1, beta1, field, top_out, bottom_out, west_out, east_out, corner_out, middle_in, corner_in, west_in, east_in, stage, strips,
    fetched, halo_send, halo_recv,
):
    barrier = pltpu.get_barrier_semaphore()
    first, last, rows, west, east = neighbours()
    met = [device for device, _ in rows] + [west, east]
    for device in met:
        pl.semaphore_signal(barrier, inc=1, device_id=device, device_id_type=MESH)

    pairs = [
        (x_far, x), (cot_far, cot), (w1_far, w1), (gamma1_far, gamma1),
        (beta1_far, beta1), (w2_far, w2), (gamma2_far, gamma2), (beta2_far, beta2),
    ]
    fetches = [pltpu.make_async_copy(far, near, fetched.at[i]) for i, (far, near) in enumerate(pairs)]
    for fetch in fetches:
        fetch.start()
    fetches[0].wait()
    fetches[1].wait()
    for side, out in enumerate((top_out, bottom_out)):
        lines = [cot[23 * side]] + [x[23 - k if side else k] for k in range(3)]
        for k, line in enumerate(lines):
            out[k] = line
        for edge, lanes in ((0, slice(0, 4)), (1, slice(12, 16))):
            corner = jnp.concatenate([line.astype(F32)[lanes] for line in lines], axis=0)
            corner_out[2 * side + edge] = corner.astype(BF16)

    def strip(target, tile, places, edge):
        for half, lanes in enumerate((128, 64)):
            span = slice(128 * half, 128 * half + lanes)
            for ref, chosen, at_row in ((x, places, 0), (cot, (edge,), 72)):
                stage.reshape(24, 8, 128)[:, :, 0:lanes] = ref[:, tile : tile + 8, span].astype(F32)
                for k, place in enumerate(chosen):
                    rows24 = stage[pl.ds(place - tile, 24, stride=8), :]
                    strips[half, at_row + 24 * k : at_row + 24 * k + 24] = rows24
        target[...] = strips[...].astype(BF16)

    strip(west_out, 0, (0, 1, 2), 0)
    strip(east_out, 8, (13, 14, 15), 15)

    pl.semaphore_wait(barrier, len(met))

    def halo(source, target, sent, landed, device):
        return pltpu.make_async_remote_copy(
            src_ref=source,
            dst_ref=target,
            send_sem=halo_send.at[sent],
            recv_sem=halo_recv.at[landed],
            device_id=device,
            device_id_type=MESH,
        )

    copies = [halo(west_out, east_in, 6, 6, west), halo(east_out, west_in, 7, 7, east)]
    for index in (0, 2, 3, 5, 1, 4):
        device, slot = rows[index]
        if index in (1, 4):
            source, target = (top_out, bottom_out)[index // 3], middle_in.at[slot - 4]
        else:
            source, target = corner_out.at[2 * (index // 3) + (index % 3) // 2], corner_in.at[slot]
        copies.append(halo(source, target, index, slot, device))
    for copy in copies[2:] + copies[:2]:
        copy.start()

    field[3:27, 0:16] = x[...].astype(F32)
    cotangent[1:25, 0:16] = cot[...].astype(F32)
    for fetch in fetches[2:]:
        fetch.wait()

    copies[0].wait_recv()
    copies[1].wait_recv()
    for half, lanes in enumerate((128, 64)):
        span = slice(128 * half, 128 * half + lanes)
        for target, start, size in ((field, 3, 3), (cotangent, 1, 1)):
            for source, offset in ((east_in, 0), (west_in, 8 - size)):
                arrived = source[half].astype(F32)
                for k in range(size):
                    at_row = 24 * k if size == 3 else 72
                    stage[pl.ds(offset + k, 24, stride=8), :] = arrived[at_row : at_row + 24]
            target[start : start + 24, 16:24, span] = stage.reshape(24, 8, 128)[:, :, 0:lanes]

    def layer(window):
        z = None
        for a in range(3):
            for b in range(3):
                term = dot(flat(window(a, b)).astype(BF16), w1[3 * a + b])
                z = term if z is None else z + term
        scale = normal_scale(z, gamma1, beta1)
        hidden = (z * scale).astype(BF16).astype(F32)
        return [value.reshape(-1, 24, 192) for value in (z, scale, hidden)]

    keep_shifted(x_store, field[3:27], slice(3, 27))
    z, scale, hidden = layer(lambda a, b: x_store[b, 3 + a : 25 + a])
    z_keep[1:23] = z[:, 0:16]
    scale_keep[1:23] = scale[:, 0:16]
    keep_shifted(h_store, hidden, slice(3, 25))

    for slot in range(6):
        source, target = (top_out, middle_in.at[slot - 4]) if slot > 3 else (corner_out.at[0], corner_in.at[slot])
        halo(source, target, 0, slot, rows[0][0]).wait_recv()
    for side in range(2):
        from_west = corner_in[2 * side].astype(F32)
        from_east = corner_in[2 * side + 1].astype(F32)
        for k in range(4):
            target = cotangent if k == 0 else field
            if k == 0:
                row = 25 * side
            else:
                row = 26 + k if side else 3 - k
            target[row, 0:16] = middle_in[side, k].astype(F32)
            span = slice(4 * k, 4 * k + 4)
            target[row, 16:24] = jnp.concatenate([from_east[span], from_west[span]], axis=0)
    keep_shifted(x_store, field[0:3], slice(0, 3))
    keep_shifted(x_store, field[27:30], slice(27, 30))

    def edge_window(a, b):
        top = x_store[b, pl.ds(a + first * (2 - 2 * a), 2)]
        bottom = x_store[b, pl.ds(26 + a + last * (2 - 2 * a), 2)]
        return jnp.concatenate([top, x_store[b, 2 + a : 3 + a], x_store[b, 25 + a : 26 + a], bottom], axis=0)

    z, scale, hidden = layer(edge_window)
    for place, row in ((0, 2), (23, 3)):
        z_keep[place] = z[row, 0:16]
        scale_keep[place] = scale[row, 0:16]
    keep_shifted(h_store, hidden[0:3], slice(0, 3))
    keep_shifted(h_store, hidden[3:6], slice(25, 28))
    for copy in copies:
        copy.wait_send()


def second_kernel(
    cotangent, x_store, h_store, z_keep, scale_keep, gamma1, w2, gamma2, beta2,
    encoded, out_w1, out_g1, out_b1, out_w2, out_g2, out_b2,
    grads, g_store, turn, *scratch,
):
    barrier = pltpu.get_barrier_semaphore()
    first, last = neighbours()[:2]
    met = partners()
    for device in met:
        pl.semaphore_signal(barrier, inc=1, device_id=device, device_id_type=MESH)

    z2 = outer_convolution(h_store, w2, 26, 1, first, last)
    sq2 = z2 * z2
    scale2 = lax.rsqrt(beta2[...] + dot_split(sq2, gamma2[...], ((1,), (1,))))
    encoded[...] = (z2 * scale2).reshape(26, 24, 192)[1:25, 0:16].astype(BF16)
    upper = flat(cotangent[...])
    lever2 = upper * z2 * scale2 * scale2 * scale2
    lower2 = upper * scale2 - z2 * dot_split(lever2, gamma2[...])
    grad2 = lower2.astype(BF16).astype(F32).reshape(26, 24, 192)
    keep_shifted(g_store, grad2)

    def inside(value):
        return flat(value.reshape(26, 24, 192)[1:25, 0:16])

    one, two = reductions(grads, scratch)
    pack_gradients(grads.at[1], h_store, 1, inside(grad2), inside(lever2), inside(sq2), turn)
    pl.semaphore_wait(barrier, len(met))
    two.step(0)

    total = None
    blank = jnp.zeros((1, 16, 192), F32)
    for a in range(3):
        for b in range(3):
            shifted = g_store.at[2 - b]
            if a == 0:
                window = jnp.concatenate([shifted[2:25, 0:16], blank], axis=0)
            elif a == 1:
                window = shifted[1:25, 0:16]
            else:
                window = jnp.concatenate([blank, shifted[1:24, 0:16]], axis=0)
            term = dot(flat(window).astype(BF16), w2[3 * a + b], ((1,), (1,)))
            total = term if total is None else total + term
    ghosts = []
    for row, a in ((0, 2 - 2 * first), (25, 2 * last)):
        ghost = None
        for b in range(3):
            term = dot(g_store[2 - b, row, 0:16].astype(BF16), w2[3 * a + b], ((1,), (1,)))
            ghost = term if ghost is None else ghost + term
        ghosts.append(ghost)
    upper1 = jnp.concatenate([total[0:16] + ghosts[0], total[16:368], total[368:384] + ghosts[1]], axis=0)
    two.step(1)

    z1 = flat(z_keep[...])
    scale1 = flat(scale_keep[...])
    lever1 = upper1 * z1 * scale1 * scale1 * scale1
    lower1 = upper1 * scale1 - z1 * dot_split(lever1, gamma1[...])
    grad1 = lower1.astype(BF16).astype(F32)
    pack_gradients(grads.at[0], x_store, 2, grad1, lever1, z1 * z1, turn)
    one.step(0)
    one.step(1)
    two.step(2)
    for index in range(2, 7):
        one.step(index)
        two.step(index + 1)
    two.unpack(out_w2, out_g2, out_b2)
    one.step(7)
    one.unpack(out_w1, out_g1, out_b1)
    two.drain()
    one.drain()


def write_out(*refs):
    sources, targets, done = refs[:7], refs[7:14], refs[14]
    copies = [pltpu.make_async_copy(sources[i], targets[i], done.at[i]) for i in (1, 4, 0, 2, 5, 3, 6)]
    for copy in copies:
        copy.start()
    for copy in copies:
        copy.wait()


def per_device(
    fields,
    first_weight,
    first_gamma,
    first_beta,
    second_weight,
    second_gamma,
    second_beta,
    cotangent,
):
    gradients = [
        jax.ShapeDtypeStruct((9, 192, 192), BF16),
        jax.ShapeDtypeStruct((192, 192), F32),
        jax.ShapeDtypeStruct((1, 192), F32),
    ]
    shape = (3, 3, 192, 192)
    shapes = [jax.ShapeDtypeStruct((24, 16, 192), BF16)] + gradients * 2
    anywhere, vmem = pl.BlockSpec(memory_space=pl.ANY), pl.BlockSpec(memory_space=pltpu.VMEM)
    operands = [
        fields,
        first_weight.reshape(9, 192, 192),
        first_gamma,
        first_beta.reshape(1, 192),
        second_weight.reshape(9, 192, 192),
        second_gamma,
        second_beta.reshape(1, 192),
        cotangent,
    ]
    carried = [
        jax.ShapeDtypeStruct(extent, dtype)
        for extent, dtype in (
            ((26, 24, 192), F32),
            ((3, 30, 24, 192), F32),
            ((3, 28, 24, 192), F32),
            ((24, 16, 192), F32),
            ((24, 16, 192), F32),
            ((192, 192), F32),
            ((9, 192, 192), BF16),
            ((192, 192), F32),
            ((1, 192), F32),
        )
    ]
    middle = pl.pallas_call(
        first_kernel,
        out_shape=carried,
        in_specs=[anywhere] * 8,
        out_specs=[vmem] * 9,
        scratch_shapes=[
            pltpu.VMEM((24, 16, 192), BF16),
            pltpu.VMEM((24, 16, 192), BF16),
            pltpu.VMEM((9, 192, 192), BF16),
            pltpu.VMEM((1, 192), F32),
            pltpu.VMEM((30, 24, 192), F32),
            pltpu.VMEM((4, 16, 192), BF16),
            pltpu.VMEM((4, 16, 192), BF16),
            pltpu.VMEM((2, 96, 128), BF16),
            pltpu.VMEM((2, 96, 128), BF16),
            pltpu.VMEM((4, 16, 192), BF16),
            pltpu.VMEM((2, 4, 16, 192), BF16),
            pltpu.VMEM((4, 16, 192), BF16),
            pltpu.VMEM((2, 96, 128), BF16),
            pltpu.VMEM((2, 96, 128), BF16),
            pltpu.VMEM((192, 128), F32),
            pltpu.VMEM((2, 96, 128), F32),
            pltpu.SemaphoreType.DMA((8,)),
            pltpu.SemaphoreType.DMA((8,)),
            pltpu.SemaphoreType.DMA((8,)),
        ],
        compiler_params=pltpu.CompilerParams(
            collective_id=0, has_side_effects=True, vmem_limit_bytes=32 * 1024 * 1024
        ),
    )(*[pltpu.with_memory_space_constraint(operand, pltpu.HBM) for operand in operands])
    results = pl.pallas_call(
        second_kernel,
        out_shape=shapes,
        in_specs=[vmem] * 9,
        out_specs=[vmem] * 7,
        scratch_shapes=[
            pltpu.VMEM((2, 2, BLOCKS, 128, 128), F32),
            pltpu.VMEM((3, 26, 24, 192), F32),
            pltpu.VMEM((128, 128), F32),
            *reduction_scratch(),
        ],
        compiler_params=pltpu.CompilerParams(
            collective_id=1, has_side_effects=True, vmem_limit_bytes=32 * 1024 * 1024
        ),
    )(*middle)
    encoded, w1, g1, b1, w2, g2, b2 = pl.pallas_call(
        write_out,
        out_shape=shapes,
        in_specs=[vmem] * 7,
        out_specs=[anywhere] * 7,
        scratch_shapes=[pltpu.SemaphoreType.DMA((7,))],
        compiler_params=pltpu.CompilerParams(vmem_limit_bytes=8 * 1024 * 1024),
    )(*results)
    return (encoded, w1.reshape(shape), g1, b1.reshape(192), w2.reshape(shape), g2, b2.reshape(192))


def solution(mesh):
    return jax.shard_map(
        per_device,
        mesh=mesh,
        in_specs=(P("lat", "lon", None), P(), P(), P(), P(), P(), P(), P("lat", "lon", None)),
        out_specs=(P("lat", "lon", None), P(), P(), P(), P(), P(), P()),
        check_vma=False,
    )
```

```python
import jax
import jax.numpy as jnp
from jax import lax
from jax.experimental import pallas as pl
from jax.experimental.pallas import tpu as pltpu
from jax.sharding import PartitionSpec as P

MESH = pl.DeviceIdType.MESH
BF16 = jnp.bfloat16
F32 = jnp.float32
NX, NY, NZ = 4, 8, 8
SIZES = {"x": NX, "y": NY, "z": NZ}
BLOCKS = 12
SLOTS = 36
DEALT = ((0, 1, 10, 15), (2, 3, 11, 16)), ((4, 5, 12, 17), (6, 7, 13, 20)), ((8, 9), (18, 21)), ((14, 19), (22, 23))
FIRSTS = (0, 4, 8, 10)
PLACES = {
    part: (core, FIRSTS[stream] + k)
    for stream, cores in enumerate(DEALT)
    for core, parts in enumerate(cores)
    for k, part in enumerate(parts)
}


def coordinates():
    lat, lon = lax.axis_index("lat"), lax.axis_index("lon")
    core = lax.rem(lon, 2)
    x = lax.rem(lax.div(lon, 2), NX)
    z = lax.div(lon, 2 * NX) * 2 + lax.rem(lat, 2)
    y = lax.div(lat, 2)
    return core, x, y, z


def at(core, x, y, z):
    return (y * 2 + lax.rem(z, 2), lax.div(z, 2) * (2 * NX) + x * 2 + core)


def partners():
    core, x, y, z = coordinates()
    found = [at(1 - core, x, y, z)]
    found += [at(core, lax.rem(x + d, NX), y, z) for d in range(1, NX)]
    found += [at(core, x, lax.rem(y + d, NY), z) for d in range(1, NY)]
    found += [at(core, x, y, lax.rem(z + d, NZ)) for d in range(1, NZ)]
    return found


def far_first(size):
    return sorted(range(1, size), key=lambda d: -min(d, size - d))


class Link:
    def __init__(self, axis, send, recv):
        place = dict(zip(("core", "x", "y", "z"), coordinates()))
        self.size, self.me = SIZES[axis], place[axis]
        self.axis, self.place = axis, place
        self.send_sem, self.recv_sem = send, recv

    def copy(self, source, target, d):
        place = dict(self.place)
        place[self.axis] = lax.rem(self.me + d, self.size)
        return pltpu.make_async_remote_copy(
            src_ref=source,
            dst_ref=target,
            send_sem=self.send_sem,
            recv_sem=self.recv_sem,
            device_id=at(**place),
            device_id_type=MESH,
        )


class Scatter(Link):
    def __init__(self, axis, send, recv, out, into):
        super().__init__(axis, send, recv)
        self.out, self.into = out, into

    def start(self, piece):
        for d in far_first(self.size):
            self.out[d - 1] = piece(lax.rem(self.me + d, self.size)).astype(BF16)
            self.copy(self.out.at[d - 1], self.into.at[d - 1], d).start()

    def finish(self, own):
        self.copy(self.out, self.into, 1).wait_recv()
        total = own
        for d in range(1, self.size):
            total = total + self.into[d - 1].astype(F32)
        return total

    def drain(self):
        self.copy(self.out, self.into, 1).wait_send()


class Share(Link):
    def __init__(self, axis, send, recv, held):
        super().__init__(axis, send, recv)
        self.held = held

    def start(self, value):
        self.held[self.me] = value.astype(BF16)
        for d in far_first(self.size):
            self.copy(self.held.at[self.me], self.held.at[self.me], d).start()

    def others(self):
        span = self.held.at[0 : self.size - 1]
        return self.copy(span, span, 1)

    def finish(self):
        self.others().wait_recv()

    def total(self):
        self.finish()
        total = self.held[0].astype(F32)
        for k in range(1, self.size):
            total = total + self.held[k].astype(F32)
        return total

    def drain(self):
        self.others().wait_send()


class Reduction:
    def __init__(self, layer, grads, core_out, core_in, x_out, x_in, y_out, y_in, z_out, z_in, y_out2, y_in2, z_out2, z_in2, held16, held32, held4, sums16, sums32, full, send, recv):
        self.grads, self.full = grads, full
        self.core_out, self.core_in = core_out, core_in
        self.me = coordinates()
        self.send, self.recv = send.at[layer], recv.at[layer]
        self.slots = 0
        self.streams = [
            self.twice(0, "x", "y", "z", (x_out.at[0], x_in.at[0]), (y_out, y_in), held16.at[0], held16.at[1], sums16.at[0]),
            self.twice(4, "x", "z", "y", (x_out.at[1], x_in.at[1]), (z_out, z_in), held16.at[2], held16.at[3], sums16.at[1]),
            self.once(8, "y", "x", "z", (y_out2, y_in2), held4.at[0], held32.at[0], held32.at[1], sums32.at[0]),
            self.once(10, "z", "x", "y", (z_out2, z_in2), held4.at[1], held32.at[2], held32.at[3], sums32.at[1]),
        ]

    def slot(self):
        self.slots += 1
        return self.send.at[self.slots - 1], self.recv.at[self.slots - 1]

    def place(self, axis):
        return self.me["xyz".index(axis) + 1]

    def partner_copy(self, sems, source, target):
        core, x, y, z = self.me
        return pltpu.make_async_remote_copy(
            src_ref=source,
            dst_ref=target,
            send_sem=sems[0],
            recv_sem=sems[1],
            device_id=at(1 - core, x, y, z),
            device_id_type=MESH,
        )

    def core_phase(self, first, count):
        sems = self.slot()
        span = slice(first, first + count)
        copy = self.partner_copy(sems, self.core_out.at[span], self.core_in.at[span])

        def start():
            self.core_out[span] = self.grads[1 - self.me[0], span].astype(BF16)
            copy.start()

        return start, copy

    def half(self, block):
        return self.grads[self.me[0], block] + self.core_in[block].astype(F32)

    def turned(self, piece):
        return piece.astype(F32).T.astype(BF16)

    def twice(self, first, axis, second, third, wide, narrow, held, spread, sums):
        core = self.me[0]
        begin, core_copy = self.core_phase(first, 4)
        one = Scatter(axis, *self.slot(), *wide)
        two = Scatter(second, *self.slot(), *narrow)
        three = Share(third, *self.slot(), held)
        four = Share(second, *self.slot(), spread)
        gather_sems = [self.slot() for _ in range(1, NX)]
        last_sems = [self.slot() for _ in range(NX)]
        me, here = self.place(axis), self.place(second)

        def block(d):
            return first + lax.rem(me + NX - d, NX)

        def gather(d, arrival=False):
            ref = self.full.at[core, block(d) if arrival else block(0)]
            return Link(axis, *gather_sems[d - 1]).copy(ref, ref, d)

        def last(d, arrival=False):
            ref = self.full.at[1 - core if arrival else core, block(d)]
            return self.partner_copy(last_sems[d], ref, ref)

        def step1():
            core_copy.wait_recv()
            one.start(lambda k: self.half(first + k))

        def step2():
            sums[...] = one.finish(self.half(first + me)).reshape(sums.shape)
            two.start(lambda k: sums[k])

        def step3():
            three.start(two.finish(sums[here]))

        def step4():
            four.start(three.total())

        def step5():
            four.finish()
            self.full[core, block(0)] = self.turned(spread[...].reshape(128, 128))
            for d in range(1, NX):
                gather(d).start()
            last(0).start()

        def step6():
            for d in range(1, NX):
                gather(d, arrival=True).wait_recv()
                last(d).start()

        def done():
            for d in range(NX):
                last(d, arrival=True).wait_recv()

        def drain():
            core_copy.wait_send()
            for phase in (one, two, three, four):
                phase.drain()
            for d in range(NX):
                last(d).wait_send()
            for d in range(1, NX):
                gather(d).wait_send()

        return (begin, step1, step2, step3, step4, step5, step6, done, drain)

    def once(self, first, axis, second, third, wide, held, held_more, spread, sums):
        core = self.me[0]
        begin, core_copy = self.core_phase(first, 2)
        one = Scatter(axis, *self.slot(), *wide)
        two = Share(second, *self.slot(), held)
        three = Share(third, *self.slot(), held_more)
        four = Share(axis, *self.slot(), spread)
        last_sems = self.slot()
        me = self.place(axis)

        def last(arrival=False):
            ref = self.full.at[1 - core if arrival else core, first : first + 2]
            return self.partner_copy(last_sems, ref, ref)

        def step1():
            core_copy.wait_recv()
            total = self.grads[core, first : first + 2] + self.core_in[first : first + 2].astype(F32)
            sums[...] = total.reshape(sums.shape)
            one.start(lambda k: sums[k])

        def step2():
            two.start(one.finish(sums[me]))

        def step3():
            three.start(two.total())

        def step4():
            four.start(three.total())

        def step5():
            four.finish()
            whole = spread[...].reshape(2, 128, 128)
            for side in range(2):
                self.full[core, first + side] = self.turned(whole[side])
            last().start()

        def step6():
            pass

        def done():
            last(arrival=True).wait_recv()

        def drain():
            core_copy.wait_send()
            for phase in (one, two, three, four):
                phase.drain()
            last().wait_send()

        return (begin, step1, step2, step3, step4, step5, step6, done, drain)

    def step(self, index, streams=(0, 1, 2, 3)):
        for k in streams:
            self.streams[k][index]()

    def drain(self):
        self.step(8)

    def block(self, index):
        return self.full[PLACES[index]]

    def unpack(self, wgrad, ggrad, bgrad):
        for tap in range(10):
            pair, odd = divmod(tap, 2)
            low = slice(64 * odd, 64 * odd + 64)
            target = ggrad if tap == 9 else wgrad.at[tap]
            dtype = F32 if tap == 9 else BF16
            target[0:128, 0:128] = self.block(tap).astype(dtype)
            target[0:128, 128:192] = self.block(15 + pair)[:, low].astype(dtype)
            target[128:192, 0:128] = self.block(10 + pair)[low].astype(dtype)
            half, side = divmod(10 + pair, 2)
            corner = self.block(15 + half)[low, 64 * side : 64 * side + 64]
            target[128:192, 128:192] = corner.astype(dtype)
        offsets = self.block(23).astype(F32)
        bgrad[0:1, 0:128] = offsets[0:1]
        bgrad[0:1, 128:192] = offsets[1:2, 0:64]


def reduction_scratch():
    return [
        pltpu.VMEM((2, BLOCKS, 128, 128), BF16),
        pltpu.VMEM((2, BLOCKS, 128, 128), BF16),
        pltpu.VMEM((2, 2, NX - 1, 128, 128), BF16),
        pltpu.VMEM((2, 2, NX - 1, 128, 128), BF16),
        pltpu.VMEM((2, NY - 1, 16, 128), BF16),
        pltpu.VMEM((2, NY - 1, 16, 128), BF16),
        pltpu.VMEM((2, NZ - 1, 16, 128), BF16),
        pltpu.VMEM((2, NZ - 1, 16, 128), BF16),
        pltpu.VMEM((2, NY - 1, 32, 128), BF16),
        pltpu.VMEM((2, NY - 1, 32, 128), BF16),
        pltpu.VMEM((2, NZ - 1, 32, 128), BF16),
        pltpu.VMEM((2, NZ - 1, 32, 128), BF16),
        pltpu.VMEM((2, 4, 8, 16, 128), BF16),
        pltpu.VMEM((2, 4, 8, 32, 128), BF16),
        pltpu.VMEM((2, 2, NX, 32, 128), BF16),
        pltpu.VMEM((2, 2, 8, 16, 128), F32),
        pltpu.VMEM((2, 2, 8, 32, 128), F32),
        pltpu.VMEM((2, 2, BLOCKS, 128, 128), BF16),
        pltpu.SemaphoreType.DMA((2, SLOTS)),
        pltpu.SemaphoreType.DMA((2, SLOTS)),
    ]


def reductions(grads, scratch):
    *buffers, send, recv = scratch
    return [
        Reduction(layer, grads.at[layer], *[buffer.at[layer] for buffer in buffers], send, recv)
        for layer in range(2)
    ]


def neighbours():
    lat, lon = lax.axis_index("lat"), lax.axis_index("lon")
    lats, lons = lax.axis_size("lat"), lax.axis_size("lon")
    first = (lat == 0).astype(jnp.int32)
    last = (lat == lats - 1).astype(jnp.int32)
    rows = []
    for pole, step, side in ((first, -1, 1), (last, 1, 0)):
        for east in (-1, 0, 1):
            device = (lat + step * (1 - pole), lax.rem(lon + lons + east + pole * (lons // 2), lons))
            landing = side + pole * (1 - 2 * side)
            rows.append((device, 4 + landing if east == 0 else 2 * landing + (1 - east) // 2))
    west = (lat, lax.rem(lon + lons - 1, lons))
    east = (lat, lax.rem(lon + 1, lons))
    return first, last, rows, west, east


def dot(left, right, dims=((1,), (0,))):
    return lax.dot_general(left, right, (dims, ((), ())), preferred_element_type=F32)


def split(value):
    high = value.astype(BF16)
    return high, (value - high.astype(F32)).astype(BF16)


def dot_split(left, right, dims=((1,), (0,))):
    left_high, left_low = split(left)
    right_high, right_low = split(right)
    return dot(left_high, right_high, dims) + dot(left_high, right_low, dims) + dot(left_low, right_high, dims)


def flat(value):
    return value.reshape(-1, value.shape[-1])


def keep_shifted(store, value, rows=slice(None)):
    store[0, rows] = pltpu.roll(value, 1, axis=1)
    store[1, rows] = value
    store[2, rows] = pltpu.roll(value, 23, axis=1)


def outer_window(store, rows, ghosts, a, b, first, last):
    turned = 2 - 2 * a
    top = store[b, pl.ds(a + first * turned, ghosts)]
    middle = store[b, ghosts + a : rows - ghosts + a]
    bottom = store[b, pl.ds(rows - ghosts + a + last * turned, ghosts)]
    return flat(jnp.concatenate([top, middle, bottom], axis=0)).astype(BF16)


def inner_window(store, a, b, start):
    return flat(store[b, start + a : start + a + 24, 0:16]).astype(BF16)


def outer_convolution(store, weight, rows, ghosts, first, last):
    total = None
    for a in range(3):
        for b in range(3):
            term = dot(outer_window(store, rows, ghosts, a, b, first, last), weight[3 * a + b])
            total = term if total is None else total + term
    return total


def place_block(grads, index, value):
    core, block = PLACES[index]
    grads[core, block] = value


def place_lower(grads, tile, value):
    core, block = PLACES[15 + tile // 2]
    start = 64 * (tile % 2)
    grads[core, block, start : start + 64] = value


def pack_gradients(grads, store, start, grad, lever, sq, turn, after=None):
    turned = grad.T.astype(BF16)
    kept = None
    for tap in range(10):
        if tap < 9:
            block = dot(turned, inner_window(store, tap // 3, tap % 3, start))
        else:
            block = -0.5 * dot_split(sq.T, lever)
        place_block(grads, tap, block[0:128, 0:128])
        place_lower(grads, tap, block[128:192, 0:128])
        if tap % 2 == 0:
            kept = block[:, 128:192]
        else:
            both = jnp.concatenate([kept, block[:, 128:192]], axis=1)
            tile = 10 + tap // 2
            place_block(grads, tile, both[0:128])
            place_lower(grads, tile, both[128:192])
        if after and tap in after:
            after[tap]()
    offsets = -0.5 * jnp.sum(lever, axis=0, keepdims=True)
    turn[...] = jnp.zeros_like(turn)
    turn[0:1, :] = offsets[:, 0:128]
    turn[1:2, 0:64] = offsets[:, 128:192]
    place_lower(grads, 15, jnp.zeros((64, 128), F32))
    place_block(grads, 23, turn[...].T)


def normal_scale(z, gamma, beta):
    return lax.rsqrt(beta[...] + dot((z * z).astype(BF16), gamma[...].astype(BF16), ((1,), (1,))))


def first_kernel(
    x_far, w1_far, gamma1_far, beta1_far, w2_far, gamma2_far, beta2_far, cot_far,
    cotangent, x_store, h_store, z_keep, scale_keep, gamma1, w2, gamma2, beta2,
    x, cot, w1, beta1, field, top_out, bottom_out, west_out, east_out, corner_out, middle_in, corner_in, west_in, east_in, stage, strips,
    fetched, halo_send, halo_recv,
):
    barrier = pltpu.get_barrier_semaphore()
    first, last, rows, west, east = neighbours()
    met = [west, east] + [device for device, _ in rows]
    for device in met:
        pl.semaphore_signal(barrier, inc=1, device_id=device, device_id_type=MESH)

    pairs = [
        (x_far, x), (cot_far, cot), (w1_far, w1), (gamma1_far, gamma1),
        (beta1_far, beta1), (w2_far, w2), (gamma2_far, gamma2), (beta2_far, beta2),
    ]
    fetches = [pltpu.make_async_copy(far, near, fetched.at[i]) for i, (far, near) in enumerate(pairs)]
    for fetch in fetches:
        fetch.start()
    fetches[0].wait()
    fetches[1].wait()
    for side, out in enumerate((top_out, bottom_out)):
        lines = [cot[23 * side]] + [x[23 - k if side else k] for k in range(3)]
        for k, line in enumerate(lines):
            out[k] = line
        for edge, lanes in ((0, slice(0, 4)), (1, slice(12, 16))):
            corner = jnp.concatenate([line.astype(F32)[lanes] for line in lines], axis=0)
            corner_out[2 * side + edge] = corner.astype(BF16)

    def strip(target, tile, places, edge):
        for half, lanes in enumerate((128, 64)):
            span = slice(128 * half, 128 * half + lanes)
            for ref, chosen, at_row in ((x, places, 0), (cot, (edge,), 72)):
                stage.reshape(24, 8, 128)[:, :, 0:lanes] = ref[:, tile : tile + 8, span].astype(F32)
                for k, place in enumerate(chosen):
                    rows24 = stage[pl.ds(place - tile, 24, stride=8), :]
                    strips[half, at_row + 24 * k : at_row + 24 * k + 24] = rows24
        target[...] = strips[...].astype(BF16)

    strip(west_out, 0, (0, 1, 2), 0)
    strip(east_out, 8, (13, 14, 15), 15)

    pl.semaphore_wait(barrier, len(met))

    def halo(source, target, sent, landed, device):
        return pltpu.make_async_remote_copy(
            src_ref=source,
            dst_ref=target,
            send_sem=halo_send.at[sent],
            recv_sem=halo_recv.at[landed],
            device_id=device,
            device_id_type=MESH,
        )

    copies = [halo(west_out, east_in, 6, 6, west), halo(east_out, west_in, 7, 7, east)]
    for index in (0, 2, 3, 5, 1, 4):
        device, slot = rows[index]
        if index in (1, 4):
            source, target = (top_out, bottom_out)[index // 3], middle_in.at[slot - 4]
        else:
            source, target = corner_out.at[2 * (index // 3) + (index % 3) // 2], corner_in.at[slot]
        copies.append(halo(source, target, index, slot, device))
    for copy in copies:
        copy.start()

    field[3:27, 0:16] = x[...].astype(F32)
    cotangent[1:25, 0:16] = cot[...].astype(F32)
    for fetch in fetches[2:]:
        fetch.wait()

    copies[0].wait_recv()
    copies[1].wait_recv()
    for half, lanes in enumerate((128, 64)):
        span = slice(128 * half, 128 * half + lanes)
        for target, start, size in ((field, 3, 3), (cotangent, 1, 1)):
            for source, offset in ((east_in, 0), (west_in, 8 - size)):
                arrived = source[half].astype(F32)
                for k in range(size):
                    at_row = 24 * k if size == 3 else 72
                    stage[pl.ds(offset + k, 24, stride=8), :] = arrived[at_row : at_row + 24]
            target[start : start + 24, 16:24, span] = stage.reshape(24, 8, 128)[:, :, 0:lanes]

    def layer(window):
        z = None
        for a in range(3):
            for b in range(3):
                term = dot(flat(window(a, b)).astype(BF16), w1[3 * a + b])
                z = term if z is None else z + term
        scale = normal_scale(z, gamma1, beta1)
        hidden = (z * scale).astype(BF16).astype(F32)
        return [value.reshape(-1, 24, 192) for value in (z, scale, hidden)]

    keep_shifted(x_store, field[3:27], slice(3, 27))
    z, scale, hidden = layer(lambda a, b: x_store[b, 3 + a : 25 + a])
    z_keep[1:23] = z[:, 0:16]
    scale_keep[1:23] = scale[:, 0:16]
    keep_shifted(h_store, hidden, slice(3, 25))

    for slot in range(6):
        source, target = (top_out, middle_in.at[slot - 4]) if slot > 3 else (corner_out.at[0], corner_in.at[slot])
        halo(source, target, 0, slot, rows[0][0]).wait_recv()
    for side in range(2):
        from_west = corner_in[2 * side].astype(F32)
        from_east = corner_in[2 * side + 1].astype(F32)
        for k in range(4):
            target = cotangent if k == 0 else field
            if k == 0:
                row = 25 * side
            else:
                row = 26 + k if side else 3 - k
            target[row, 0:16] = middle_in[side, k].astype(F32)
            span = slice(4 * k, 4 * k + 4)
            target[row, 16:24] = jnp.concatenate([from_east[span], from_west[span]], axis=0)
    keep_shifted(x_store, field[0:3], slice(0, 3))
    keep_shifted(x_store, field[27:30], slice(27, 30))

    def edge_window(a, b):
        top = x_store[b, pl.ds(a + first * (2 - 2 * a), 2)]
        bottom = x_store[b, pl.ds(26 + a + last * (2 - 2 * a), 2)]
        return jnp.concatenate([top, x_store[b, 2 + a : 3 + a], x_store[b, 25 + a : 26 + a], bottom], axis=0)

    z, scale, hidden = layer(edge_window)
    for place, row in ((0, 2), (23, 3)):
        z_keep[place] = z[row, 0:16]
        scale_keep[place] = scale[row, 0:16]
    keep_shifted(h_store, hidden[0:3], slice(0, 3))
    keep_shifted(h_store, hidden[3:6], slice(25, 28))
    for copy in copies:
        copy.wait_send()


def second_kernel(
    cotangent, x_store, h_store, z_keep, scale_keep, gamma1, w2, gamma2, beta2,
    encoded, out_w1, out_g1, out_b1, out_w2, out_g2, out_b2,
    grads, g_store, turn, *scratch,
):
    barrier = pltpu.get_barrier_semaphore()
    first, last = neighbours()[:2]
    met = partners()
    for device in met:
        pl.semaphore_signal(barrier, inc=1, device_id=device, device_id_type=MESH)

    z2 = outer_convolution(h_store, w2, 26, 1, first, last)
    sq2 = z2 * z2
    scale2 = normal_scale(z2, gamma2, beta2)
    encoded[...] = (z2 * scale2).reshape(26, 24, 192)[1:25, 0:16].astype(BF16)
    upper = flat(cotangent[...])
    lever2 = upper * z2 * scale2 * scale2 * scale2
    lower2 = upper * scale2 - z2 * dot(lever2.astype(BF16), gamma2[...].astype(BF16))
    grad2 = lower2.astype(BF16).astype(F32).reshape(26, 24, 192)
    keep_shifted(g_store, grad2)

    def inside(value):
        return flat(value.reshape(26, 24, 192)[1:25, 0:16])

    one, two = reductions(grads, scratch)
    pack_gradients(grads.at[1], h_store, 1, inside(grad2), inside(lever2), inside(sq2), turn)
    pl.semaphore_wait(barrier, len(met))
    two.step(0)

    total = None
    blank = jnp.zeros((1, 16, 192), F32)
    for a in range(3):
        for b in range(3):
            shifted = g_store.at[2 - b]
            if a == 0:
                window = jnp.concatenate([shifted[2:25, 0:16], blank], axis=0)
            elif a == 1:
                window = shifted[1:25, 0:16]
            else:
                window = jnp.concatenate([blank, shifted[1:24, 0:16]], axis=0)
            term = dot(flat(window).astype(BF16), w2[3 * a + b], ((1,), (1,)))
            total = term if total is None else total + term
    ghosts = []
    for row, a in ((0, 2 - 2 * first), (25, 2 * last)):
        ghost = None
        for b in range(3):
            term = dot(g_store[2 - b, row, 0:16].astype(BF16), w2[3 * a + b], ((1,), (1,)))
            ghost = term if ghost is None else ghost + term
        ghosts.append(ghost)
    upper1 = jnp.concatenate([total[0:16] + ghosts[0], total[16:368], total[368:384] + ghosts[1]], axis=0)

    z1 = flat(z_keep[...])
    scale1 = flat(scale_keep[...])
    lever1 = upper1 * z1 * scale1 * scale1 * scale1
    lower1 = upper1 * scale1 - z1 * dot(lever1.astype(BF16), gamma1[...].astype(BF16))
    grad1 = lower1.astype(BF16).astype(F32)
    two.step(1)
    ready = {3: lambda: one.step(0, (0,)), 7: lambda: one.step(0, (1,))}
    pack_gradients(grads.at[0], x_store, 2, grad1, lever1, z1 * z1, turn, ready)
    one.step(0, (2, 3))
    one.step(1)
    two.step(2)
    for index in range(2, 7):
        one.step(index)
        two.step(index + 1)
    two.unpack(out_w2, out_g2, out_b2)
    one.step(7)
    one.unpack(out_w1, out_g1, out_b1)
    two.drain()
    one.drain()


def write_out(*refs):
    sources, targets, done = refs[:7], refs[7:14], refs[14]
    copies = [pltpu.make_async_copy(sources[i], targets[i], done.at[i]) for i in (1, 4, 0, 2, 5, 3, 6)]
    for copy in copies:
        copy.start()
    for copy in copies:
        copy.wait()


def per_device(
    fields,
    first_weight,
    first_gamma,
    first_beta,
    second_weight,
    second_gamma,
    second_beta,
    cotangent,
):
    gradients = [
        jax.ShapeDtypeStruct((9, 192, 192), BF16),
        jax.ShapeDtypeStruct((192, 192), F32),
        jax.ShapeDtypeStruct((1, 192), F32),
    ]
    shape = (3, 3, 192, 192)
    shapes = [jax.ShapeDtypeStruct((24, 16, 192), BF16)] + gradients * 2
    anywhere, vmem = pl.BlockSpec(memory_space=pl.ANY), pl.BlockSpec(memory_space=pltpu.VMEM)
    operands = [
        fields,
        first_weight.reshape(9, 192, 192),
        first_gamma,
        first_beta.reshape(1, 192),
        second_weight.reshape(9, 192, 192),
        second_gamma,
        second_beta.reshape(1, 192),
        cotangent,
    ]
    carried = [
        jax.ShapeDtypeStruct(extent, dtype)
        for extent, dtype in (
            ((26, 24, 192), F32),
            ((3, 30, 24, 192), F32),
            ((3, 28, 24, 192), F32),
            ((24, 16, 192), F32),
            ((24, 16, 192), F32),
            ((192, 192), F32),
            ((9, 192, 192), BF16),
            ((192, 192), F32),
            ((1, 192), F32),
        )
    ]
    middle = pl.pallas_call(
        first_kernel,
        out_shape=carried,
        in_specs=[anywhere] * 8,
        out_specs=[vmem] * 9,
        scratch_shapes=[
            pltpu.VMEM((24, 16, 192), BF16),
            pltpu.VMEM((24, 16, 192), BF16),
            pltpu.VMEM((9, 192, 192), BF16),
            pltpu.VMEM((1, 192), F32),
            pltpu.VMEM((30, 24, 192), F32),
            pltpu.VMEM((4, 16, 192), BF16),
            pltpu.VMEM((4, 16, 192), BF16),
            pltpu.VMEM((2, 96, 128), BF16),
            pltpu.VMEM((2, 96, 128), BF16),
            pltpu.VMEM((4, 16, 192), BF16),
            pltpu.VMEM((2, 4, 16, 192), BF16),
            pltpu.VMEM((4, 16, 192), BF16),
            pltpu.VMEM((2, 96, 128), BF16),
            pltpu.VMEM((2, 96, 128), BF16),
            pltpu.VMEM((192, 128), F32),
            pltpu.VMEM((2, 96, 128), F32),
            pltpu.SemaphoreType.DMA((8,)),
            pltpu.SemaphoreType.DMA((8,)),
            pltpu.SemaphoreType.DMA((8,)),
        ],
        compiler_params=pltpu.CompilerParams(
            collective_id=0, has_side_effects=True, vmem_limit_bytes=32 * 1024 * 1024
        ),
    )(*[pltpu.with_memory_space_constraint(operand, pltpu.HBM) for operand in operands])
    results = pl.pallas_call(
        second_kernel,
        out_shape=shapes,
        in_specs=[vmem] * 9,
        out_specs=[vmem] * 7,
        scratch_shapes=[
            pltpu.VMEM((2, 2, BLOCKS, 128, 128), F32),
            pltpu.VMEM((3, 26, 24, 192), F32),
            pltpu.VMEM((128, 128), F32),
            *reduction_scratch(),
        ],
        compiler_params=pltpu.CompilerParams(
            collective_id=1, has_side_effects=True, vmem_limit_bytes=32 * 1024 * 1024
        ),
    )(*middle)
    encoded, w1, g1, b1, w2, g2, b2 = pl.pallas_call(
        write_out,
        out_shape=shapes,
        in_specs=[vmem] * 7,
        out_specs=[anywhere] * 7,
        scratch_shapes=[pltpu.SemaphoreType.DMA((7,))],
        compiler_params=pltpu.CompilerParams(vmem_limit_bytes=8 * 1024 * 1024),
    )(*results)
    return (encoded, w1.reshape(shape), g1, b1.reshape(192), w2.reshape(shape), g2, b2.reshape(192))


def solution(mesh):
    return jax.shard_map(
        per_device,
        mesh=mesh,
        in_specs=(P("lat", "lon", None), P(), P(), P(), P(), P(), P(), P("lat", "lon", None)),
        out_specs=(P("lat", "lon", None), P(), P(), P(), P(), P(), P()),
        check_vma=False,
    )
```

```python
import jax
import jax.numpy as jnp
from jax import lax
from jax.experimental import pallas as pl
from jax.experimental.pallas import tpu as pltpu
from jax.sharding import PartitionSpec as P

MESH = pl.DeviceIdType.MESH
BF16 = jnp.bfloat16
F32 = jnp.float32
NX, NY, NZ = 4, 8, 8
SIZES = {"x": NX, "y": NY, "z": NZ}
BLOCKS = 12
SLOTS = 36
DEALT = ((0, 1, 10, 15), (2, 3, 11, 16)), ((4, 5, 12, 17), (6, 7, 13, 20)), ((8, 9), (18, 21)), ((14, 19), (22, 23))
FIRSTS = (0, 4, 8, 10)
PLACES = {
    part: (core, FIRSTS[stream] + k)
    for stream, cores in enumerate(DEALT)
    for core, parts in enumerate(cores)
    for k, part in enumerate(parts)
}


def coordinates():
    lat, lon = lax.axis_index("lat"), lax.axis_index("lon")
    core = lax.rem(lon, 2)
    x = lax.rem(lax.div(lon, 2), NX)
    z = lax.div(lon, 2 * NX) * 2 + lax.rem(lat, 2)
    y = lax.div(lat, 2)
    return core, x, y, z


def at(core, x, y, z):
    return (y * 2 + lax.rem(z, 2), lax.div(z, 2) * (2 * NX) + x * 2 + core)


def partners():
    core, x, y, z = coordinates()
    found = [at(1 - core, x, y, z)]
    found += [at(core, lax.rem(x + d, NX), y, z) for d in range(1, NX)]
    found += [at(core, x, lax.rem(y + d, NY), z) for d in range(1, NY)]
    found += [at(core, x, y, lax.rem(z + d, NZ)) for d in range(1, NZ)]
    return found


def far_first(size):
    return sorted(range(1, size), key=lambda d: -min(d, size - d))


class Link:
    def __init__(self, axis, send, recv):
        place = dict(zip(("core", "x", "y", "z"), coordinates()))
        self.size, self.me = SIZES[axis], place[axis]
        self.axis, self.place = axis, place
        self.send_sem, self.recv_sem = send, recv

    def copy(self, source, target, d):
        place = dict(self.place)
        place[self.axis] = lax.rem(self.me + d, self.size)
        return pltpu.make_async_remote_copy(
            src_ref=source,
            dst_ref=target,
            send_sem=self.send_sem,
            recv_sem=self.recv_sem,
            device_id=at(**place),
            device_id_type=MESH,
        )


class Scatter(Link):
    def __init__(self, axis, send, recv, out, into):
        super().__init__(axis, send, recv)
        self.out, self.into = out, into

    def start(self, piece):
        for d in far_first(self.size):
            self.out[d - 1] = piece(lax.rem(self.me + d, self.size)).astype(BF16)
            self.copy(self.out.at[d - 1], self.into.at[d - 1], d).start()

    def finish(self, own):
        self.copy(self.out, self.into, 1).wait_recv()
        total = own
        for d in range(1, self.size):
            total = total + self.into[d - 1].astype(F32)
        return total

    def drain(self):
        self.copy(self.out, self.into, 1).wait_send()


class Share(Link):
    def __init__(self, axis, send, recv, held):
        super().__init__(axis, send, recv)
        self.held = held

    def start(self, value):
        self.held[self.me] = value.astype(BF16)
        for d in far_first(self.size):
            self.copy(self.held.at[self.me], self.held.at[self.me], d).start()

    def others(self):
        span = self.held.at[0 : self.size - 1]
        return self.copy(span, span, 1)

    def finish(self):
        self.others().wait_recv()

    def total(self):
        self.finish()
        total = self.held[0].astype(F32)
        for k in range(1, self.size):
            total = total + self.held[k].astype(F32)
        return total

    def drain(self):
        self.others().wait_send()


class Reduction:
    def __init__(self, layer, grads, core_out, core_in, x_out, x_in, y_out, y_in, z_out, z_in, y_out2, y_in2, z_out2, z_in2, held16, held32, held4, sums16, sums32, full, send, recv):
        self.grads, self.full = grads, full
        self.core_out, self.core_in = core_out, core_in
        self.me = coordinates()
        self.send, self.recv = send.at[layer], recv.at[layer]
        self.slots = 0
        self.streams = [
            self.twice(0, "x", "y", "z", (x_out.at[0], x_in.at[0]), (y_out, y_in), held16.at[0], held16.at[1], sums16.at[0]),
            self.twice(4, "x", "z", "y", (x_out.at[1], x_in.at[1]), (z_out, z_in), held16.at[2], held16.at[3], sums16.at[1]),
            self.once(8, "y", "x", "z", (y_out2, y_in2), held4.at[0], held32.at[0], held32.at[1], sums32.at[0]),
            self.once(10, "z", "x", "y", (z_out2, z_in2), held4.at[1], held32.at[2], held32.at[3], sums32.at[1]),
        ]

    def slot(self):
        self.slots += 1
        return self.send.at[self.slots - 1], self.recv.at[self.slots - 1]

    def place(self, axis):
        return self.me["xyz".index(axis) + 1]

    def partner_copy(self, sems, source, target):
        core, x, y, z = self.me
        return pltpu.make_async_remote_copy(
            src_ref=source,
            dst_ref=target,
            send_sem=sems[0],
            recv_sem=sems[1],
            device_id=at(1 - core, x, y, z),
            device_id_type=MESH,
        )

    def core_phase(self, first, count):
        sems = self.slot()
        span = slice(first, first + count)
        copy = self.partner_copy(sems, self.core_out.at[span], self.core_in.at[span])

        def start():
            self.core_out[span] = self.grads[1 - self.me[0], span].astype(BF16)
            copy.start()

        return start, copy

    def half(self, block):
        return self.grads[self.me[0], block] + self.core_in[block].astype(F32)

    def turned(self, piece):
        return piece.astype(F32).T.astype(BF16)

    def twice(self, first, axis, second, third, wide, narrow, held, spread, sums):
        core = self.me[0]
        begin, core_copy = self.core_phase(first, 4)
        one = Scatter(axis, *self.slot(), *wide)
        two = Scatter(second, *self.slot(), *narrow)
        three = Share(third, *self.slot(), held)
        four = Share(second, *self.slot(), spread)
        gather_sems = [self.slot() for _ in range(1, NX)]
        last_sems = [self.slot() for _ in range(NX)]
        me, here = self.place(axis), self.place(second)

        def block(d):
            return first + lax.rem(me + NX - d, NX)

        def gather(d, arrival=False):
            ref = self.full.at[core, block(d) if arrival else block(0)]
            return Link(axis, *gather_sems[d - 1]).copy(ref, ref, d)

        def last(d, arrival=False):
            ref = self.full.at[1 - core if arrival else core, block(d)]
            return self.partner_copy(last_sems[d], ref, ref)

        def step1():
            core_copy.wait_recv()
            one.start(lambda k: self.half(first + k))

        def step2():
            sums[...] = one.finish(self.half(first + me)).reshape(sums.shape)
            two.start(lambda k: sums[k])

        def step3():
            three.start(two.finish(sums[here]))

        def step4():
            four.start(three.total())

        def step5():
            four.finish()
            self.full[core, block(0)] = self.turned(spread[...].reshape(128, 128))
            for d in range(1, NX):
                gather(d).start()
            last(0).start()

        def step6():
            for d in range(1, NX):
                gather(d, arrival=True).wait_recv()
                last(d).start()

        def done():
            for d in range(NX):
                last(d, arrival=True).wait_recv()

        def drain():
            core_copy.wait_send()
            for phase in (one, two, three, four):
                phase.drain()
            for d in range(NX):
                last(d).wait_send()
            for d in range(1, NX):
                gather(d).wait_send()

        return (begin, step1, step2, step3, step4, step5, step6, done, drain)

    def once(self, first, axis, second, third, wide, held, held_more, spread, sums):
        core = self.me[0]
        begin, core_copy = self.core_phase(first, 2)
        one = Scatter(axis, *self.slot(), *wide)
        two = Share(second, *self.slot(), held)
        three = Share(third, *self.slot(), held_more)
        four = Share(axis, *self.slot(), spread)
        last_sems = self.slot()
        me = self.place(axis)

        def last(arrival=False):
            ref = self.full.at[1 - core if arrival else core, first : first + 2]
            return self.partner_copy(last_sems, ref, ref)

        def step1():
            core_copy.wait_recv()
            total = self.grads[core, first : first + 2] + self.core_in[first : first + 2].astype(F32)
            sums[...] = total.reshape(sums.shape)
            one.start(lambda k: sums[k])

        def step2():
            two.start(one.finish(sums[me]))

        def step3():
            three.start(two.total())

        def step4():
            four.start(three.total())

        def step5():
            four.finish()
            whole = spread[...].reshape(2, 128, 128)
            for side in range(2):
                self.full[core, first + side] = self.turned(whole[side])
            last().start()

        def step6():
            pass

        def done():
            last(arrival=True).wait_recv()

        def drain():
            core_copy.wait_send()
            for phase in (one, two, three, four):
                phase.drain()
            last().wait_send()

        return (begin, step1, step2, step3, step4, step5, step6, done, drain)

    def step(self, index, streams=(0, 1, 2, 3)):
        for k in streams:
            self.streams[k][index]()

    def drain(self):
        self.step(8)

    def block(self, index):
        return self.full[PLACES[index]]

    def unpack(self, wgrad, ggrad, bgrad):
        for tap in range(10):
            pair, odd = divmod(tap, 2)
            low = slice(64 * odd, 64 * odd + 64)
            target = ggrad if tap == 9 else wgrad.at[tap]
            dtype = F32 if tap == 9 else BF16
            target[0:128, 0:128] = self.block(tap).astype(dtype)
            target[0:128, 128:192] = self.block(15 + pair)[:, low].astype(dtype)
            target[128:192, 0:128] = self.block(10 + pair)[low].astype(dtype)
            half, side = divmod(10 + pair, 2)
            corner = self.block(15 + half)[low, 64 * side : 64 * side + 64]
            target[128:192, 128:192] = corner.astype(dtype)
        offsets = self.block(23).astype(F32)
        bgrad[0:1, 0:128] = offsets[0:1]
        bgrad[0:1, 128:192] = offsets[1:2, 0:64]


def reduction_scratch():
    return [
        pltpu.VMEM((2, BLOCKS, 128, 128), BF16),
        pltpu.VMEM((2, BLOCKS, 128, 128), BF16),
        pltpu.VMEM((2, 2, NX - 1, 128, 128), BF16),
        pltpu.VMEM((2, 2, NX - 1, 128, 128), BF16),
        pltpu.VMEM((2, NY - 1, 16, 128), BF16),
        pltpu.VMEM((2, NY - 1, 16, 128), BF16),
        pltpu.VMEM((2, NZ - 1, 16, 128), BF16),
        pltpu.VMEM((2, NZ - 1, 16, 128), BF16),
        pltpu.VMEM((2, NY - 1, 32, 128), BF16),
        pltpu.VMEM((2, NY - 1, 32, 128), BF16),
        pltpu.VMEM((2, NZ - 1, 32, 128), BF16),
        pltpu.VMEM((2, NZ - 1, 32, 128), BF16),
        pltpu.VMEM((2, 4, 8, 16, 128), BF16),
        pltpu.VMEM((2, 4, 8, 32, 128), BF16),
        pltpu.VMEM((2, 2, NX, 32, 128), BF16),
        pltpu.VMEM((2, 2, 8, 16, 128), F32),
        pltpu.VMEM((2, 2, 8, 32, 128), F32),
        pltpu.VMEM((2, 2, BLOCKS, 128, 128), BF16),
        pltpu.SemaphoreType.DMA((2, SLOTS)),
        pltpu.SemaphoreType.DMA((2, SLOTS)),
    ]


def reductions(grads, scratch):
    *buffers, send, recv = scratch
    return [
        Reduction(layer, grads.at[layer], *[buffer.at[layer] for buffer in buffers], send, recv)
        for layer in range(2)
    ]


def neighbours():
    lat, lon = lax.axis_index("lat"), lax.axis_index("lon")
    lats, lons = lax.axis_size("lat"), lax.axis_size("lon")
    first = (lat == 0).astype(jnp.int32)
    last = (lat == lats - 1).astype(jnp.int32)
    rows = []
    for pole, step, side in ((first, -1, 1), (last, 1, 0)):
        for east in (-1, 0, 1):
            device = (lat + step * (1 - pole), lax.rem(lon + lons + east + pole * (lons // 2), lons))
            landing = side + pole * (1 - 2 * side)
            rows.append((device, 4 + landing if east == 0 else 2 * landing + (1 - east) // 2))
    west = (lat, lax.rem(lon + lons - 1, lons))
    east = (lat, lax.rem(lon + 1, lons))
    return first, last, rows, west, east


def dot(left, right, dims=((1,), (0,))):
    return lax.dot_general(left, right, (dims, ((), ())), preferred_element_type=F32)


def split(value):
    high = value.astype(BF16)
    return high, (value - high.astype(F32)).astype(BF16)


def dot_split(left, right, dims=((1,), (0,))):
    left_high, left_low = split(left)
    right_high, right_low = split(right)
    return dot(left_high, right_high, dims) + dot(left_high, right_low, dims) + dot(left_low, right_high, dims)


def flat(value):
    return value.reshape(-1, value.shape[-1])


def keep_shifted(store, value, rows=slice(None)):
    store[0, rows] = pltpu.roll(value, 1, axis=1)
    store[1, rows] = value
    store[2, rows] = pltpu.roll(value, 23, axis=1)


def outer_window(store, rows, ghosts, a, b, first, last):
    turned = 2 - 2 * a
    top = store[b, pl.ds(a + first * turned, ghosts)]
    middle = store[b, ghosts + a : rows - ghosts + a]
    bottom = store[b, pl.ds(rows - ghosts + a + last * turned, ghosts)]
    return flat(jnp.concatenate([top, middle, bottom], axis=0)).astype(BF16)


def inner_window(store, a, b, start):
    return flat(store[b, start + a : start + a + 24, 0:16]).astype(BF16)


def gathered(windows, weight):
    return dot(jnp.concatenate(windows, axis=1), weight[...].reshape(9 * 192, 192))


def outer_convolution(store, weight, rows, ghosts, first, last):
    taps = [(a, b) for a in range(3) for b in range(3)]
    return gathered([outer_window(store, rows, ghosts, a, b, first, last) for a, b in taps], weight)


def place_block(grads, index, value):
    core, block = PLACES[index]
    grads[core, block] = value


def place_lower(grads, tile, value):
    core, block = PLACES[15 + tile // 2]
    start = 64 * (tile % 2)
    grads[core, block, start : start + 64] = value


def pack_gradients(grads, store, start, grad, lever, sq, turn, after=None):
    turned = grad.T.astype(BF16)
    kept = None
    for tap in range(10):
        if tap < 9:
            block = dot(turned, inner_window(store, tap // 3, tap % 3, start))
        else:
            block = -0.5 * dot_split(sq.T, lever)
        place_block(grads, tap, block[0:128, 0:128])
        place_lower(grads, tap, block[128:192, 0:128])
        if tap % 2 == 0:
            kept = block[:, 128:192]
        else:
            both = jnp.concatenate([kept, block[:, 128:192]], axis=1)
            tile = 10 + tap // 2
            place_block(grads, tile, both[0:128])
            place_lower(grads, tile, both[128:192])
        if after and tap in after:
            after[tap]()
    offsets = -0.5 * jnp.sum(lever, axis=0, keepdims=True)
    turn[...] = jnp.zeros_like(turn)
    turn[0:1, :] = offsets[:, 0:128]
    turn[1:2, 0:64] = offsets[:, 128:192]
    place_lower(grads, 15, jnp.zeros((64, 128), F32))
    place_block(grads, 23, turn[...].T)


def normal_scale(z, gamma, beta):
    return lax.rsqrt(beta[...] + dot((z * z).astype(BF16), gamma[...]))


def first_kernel(
    x_far, w1_far, gamma1_far, beta1_far, w2_far, gamma2_far, beta2_far, cot_far,
    cotangent, x_store, h_store, z_keep, scale_keep, gamma1, w2, gamma2, beta2, w2_turned, gamma2_turned,
    gamma1_turned, x, cot, w1, beta1, field, top_out, bottom_out, west_out, east_out, corner_out, middle_in, corner_in, west_in, east_in, stage, strips,
    fetched, halo_send, halo_recv,
):
    barrier = pltpu.get_barrier_semaphore()
    first, last, rows, west, east = neighbours()
    met = [west, east] + [device for device, _ in rows]
    for device in met:
        pl.semaphore_signal(barrier, inc=1, device_id=device, device_id_type=MESH)

    pairs = [
        (x_far, x), (cot_far, cot), (w1_far, w1), (gamma1_far, gamma1),
        (beta1_far, beta1), (w2_far, w2), (gamma2_far, gamma2), (beta2_far, beta2),
    ]
    fetches = [pltpu.make_async_copy(far, near, fetched.at[i]) for i, (far, near) in enumerate(pairs)]
    for fetch in fetches:
        fetch.start()
    fetches[0].wait()
    fetches[1].wait()
    for side, out in enumerate((top_out, bottom_out)):
        lines = [cot[23 * side]] + [x[23 - k if side else k] for k in range(3)]
        for k, line in enumerate(lines):
            out[k] = line
        for edge, lanes in ((0, slice(0, 4)), (1, slice(12, 16))):
            corner = jnp.concatenate([line.astype(F32)[lanes] for line in lines], axis=0)
            corner_out[2 * side + edge] = corner.astype(BF16)

    def strip(target, tile, places, edge):
        for half, lanes in enumerate((128, 64)):
            span = slice(128 * half, 128 * half + lanes)
            for ref, chosen, at_row in ((x, places, 0), (cot, (edge,), 72)):
                stage.reshape(24, 8, 128)[:, :, 0:lanes] = ref[:, tile : tile + 8, span].astype(F32)
                for k, place in enumerate(chosen):
                    rows24 = stage[pl.ds(place - tile, 24, stride=8), :]
                    strips[half, at_row + 24 * k : at_row + 24 * k + 24] = rows24
        target[...] = strips[...].astype(BF16)

    strip(west_out, 0, (0, 1, 2), 0)
    strip(east_out, 8, (13, 14, 15), 15)

    pl.semaphore_wait(barrier, len(met))

    def halo(source, target, sent, landed, device):
        return pltpu.make_async_remote_copy(
            src_ref=source,
            dst_ref=target,
            send_sem=halo_send.at[sent],
            recv_sem=halo_recv.at[landed],
            device_id=device,
            device_id_type=MESH,
        )

    copies = [halo(west_out, east_in, 6, 6, west), halo(east_out, west_in, 7, 7, east)]
    for index in (0, 2, 3, 5, 1, 4):
        device, slot = rows[index]
        if index in (1, 4):
            source, target = (top_out, bottom_out)[index // 3], middle_in.at[slot - 4]
        else:
            source, target = corner_out.at[2 * (index // 3) + (index % 3) // 2], corner_in.at[slot]
        copies.append(halo(source, target, index, slot, device))
    for copy in copies:
        copy.start()

    field[3:27, 0:16] = x[...].astype(F32)
    cotangent[1:25, 0:16] = cot[...].astype(F32)
    for fetch in fetches[2:]:
        fetch.wait()
    gamma1_turned[...] = gamma1[...].T.astype(BF16)
    gamma2_turned[...] = gamma2[...].T.astype(BF16)
    for tap in range(9):
        w2_turned[tap] = w2[tap].astype(F32).T.astype(BF16)

    copies[0].wait_recv()
    copies[1].wait_recv()
    for half, lanes in enumerate((128, 64)):
        span = slice(128 * half, 128 * half + lanes)
        for target, start, size in ((field, 3, 3), (cotangent, 1, 1)):
            for source, offset in ((east_in, 0), (west_in, 8 - size)):
                arrived = source[half].astype(F32)
                for k in range(size):
                    at_row = 24 * k if size == 3 else 72
                    stage[pl.ds(offset + k, 24, stride=8), :] = arrived[at_row : at_row + 24]
            target[start : start + 24, 16:24, span] = stage.reshape(24, 8, 128)[:, :, 0:lanes]

    def layer(window):
        z = gathered([flat(window(a, b)).astype(BF16) for a in range(3) for b in range(3)], w1)
        scale = normal_scale(z, gamma1_turned, beta1)
        hidden = (z * scale).astype(BF16).astype(F32)
        return [value.reshape(-1, 24, 192) for value in (z, scale, hidden)]

    keep_shifted(x_store, field[3:27], slice(3, 27))
    z, scale, hidden = layer(lambda a, b: x_store[b, 3 + a : 25 + a])
    z_keep[1:23] = z[:, 0:16]
    scale_keep[1:23] = scale[:, 0:16]
    keep_shifted(h_store, hidden, slice(3, 25))

    for slot in range(6):
        source, target = (top_out, middle_in.at[slot - 4]) if slot > 3 else (corner_out.at[0], corner_in.at[slot])
        halo(source, target, 0, slot, rows[0][0]).wait_recv()
    for side in range(2):
        from_west = corner_in[2 * side].astype(F32)
        from_east = corner_in[2 * side + 1].astype(F32)
        for k in range(4):
            target = cotangent if k == 0 else field
            if k == 0:
                row = 25 * side
            else:
                row = 26 + k if side else 3 - k
            target[row, 0:16] = middle_in[side, k].astype(F32)
            span = slice(4 * k, 4 * k + 4)
            target[row, 16:24] = jnp.concatenate([from_east[span], from_west[span]], axis=0)
    keep_shifted(x_store, field[0:3], slice(0, 3))
    keep_shifted(x_store, field[27:30], slice(27, 30))

    def edge_window(a, b):
        top = x_store[b, pl.ds(a + first * (2 - 2 * a), 2)]
        bottom = x_store[b, pl.ds(26 + a + last * (2 - 2 * a), 2)]
        return jnp.concatenate([top, x_store[b, 2 + a : 3 + a], x_store[b, 25 + a : 26 + a], bottom], axis=0)

    z, scale, hidden = layer(edge_window)
    for place, row in ((0, 2), (23, 3)):
        z_keep[place] = z[row, 0:16]
        scale_keep[place] = scale[row, 0:16]
    keep_shifted(h_store, hidden[0:3], slice(0, 3))
    keep_shifted(h_store, hidden[3:6], slice(25, 28))
    for copy in copies:
        copy.wait_send()


def second_kernel(
    cotangent, x_store, h_store, z_keep, scale_keep, gamma1, w2, gamma2, beta2, w2_turned, gamma2_turned,
    encoded, out_w1, out_g1, out_b1, out_w2, out_g2, out_b2,
    grads, g_store, turn, *scratch,
):
    barrier = pltpu.get_barrier_semaphore()
    first, last = neighbours()[:2]
    met = partners()
    for device in met:
        pl.semaphore_signal(barrier, inc=1, device_id=device, device_id_type=MESH)

    z2 = outer_convolution(h_store, w2, 26, 1, first, last)
    sq2 = z2 * z2
    scale2 = normal_scale(z2, gamma2_turned, beta2)
    encoded[...] = (z2 * scale2).reshape(26, 24, 192)[1:25, 0:16].astype(BF16)
    upper = flat(cotangent[...])
    lever2 = upper * z2 * scale2 * scale2 * scale2
    lower2 = upper * scale2 - z2 * dot(lever2.astype(BF16), gamma2[...].astype(BF16))
    grad2 = lower2.astype(BF16).astype(F32).reshape(26, 24, 192)
    keep_shifted(g_store, grad2)

    def inside(value):
        return flat(value.reshape(26, 24, 192)[1:25, 0:16])

    one, two = reductions(grads, scratch)
    pack_gradients(grads.at[1], h_store, 1, inside(grad2), inside(lever2), inside(sq2), turn)
    pl.semaphore_wait(barrier, len(met))
    two.step(0)

    blank = jnp.zeros((1, 16, 192), F32)
    windows = []
    for a in range(3):
        for b in range(3):
            shifted = g_store.at[2 - b]
            if a == 0:
                window = jnp.concatenate([shifted[2:25, 0:16], blank], axis=0)
            elif a == 1:
                window = shifted[1:25, 0:16]
            else:
                window = jnp.concatenate([blank, shifted[1:24, 0:16]], axis=0)
            windows.append(flat(window).astype(BF16))
    total = gathered(windows, w2_turned)
    ghosts = []
    for row, a in ((0, 2 - 2 * first), (25, 2 * last)):
        ghost = None
        for b in range(3):
            term = dot(g_store[2 - b, row, 0:16].astype(BF16), w2_turned[3 * a + b])
            ghost = term if ghost is None else ghost + term
        ghosts.append(ghost)
    upper1 = jnp.concatenate([total[0:16] + ghosts[0], total[16:368], total[368:384] + ghosts[1]], axis=0)

    z1 = flat(z_keep[...])
    scale1 = flat(scale_keep[...])
    lever1 = upper1 * z1 * scale1 * scale1 * scale1
    lower1 = upper1 * scale1 - z1 * dot(lever1.astype(BF16), gamma1[...].astype(BF16))
    grad1 = lower1.astype(BF16).astype(F32)
    two.step(1)
    ready = {3: lambda: one.step(0, (0,)), 7: lambda: one.step(0, (1,))}
    pack_gradients(grads.at[0], x_store, 2, grad1, lever1, z1 * z1, turn, ready)
    one.step(0, (2, 3))
    one.step(1)
    two.step(2)
    for index in range(2, 7):
        one.step(index)
        two.step(index + 1)
    two.unpack(out_w2, out_g2, out_b2)
    one.step(7)
    one.unpack(out_w1, out_g1, out_b1)
    two.drain()
    one.drain()


def write_out(*refs):
    sources, targets, done = refs[:7], refs[7:14], refs[14]
    copies = [pltpu.make_async_copy(sources[i], targets[i], done.at[i]) for i in (1, 4, 0, 2, 5, 3, 6)]
    for copy in copies:
        copy.start()
    for copy in copies:
        copy.wait()


def per_device(
    fields,
    first_weight,
    first_gamma,
    first_beta,
    second_weight,
    second_gamma,
    second_beta,
    cotangent,
):
    gradients = [
        jax.ShapeDtypeStruct((9, 192, 192), BF16),
        jax.ShapeDtypeStruct((192, 192), F32),
        jax.ShapeDtypeStruct((1, 192), F32),
    ]
    shape = (3, 3, 192, 192)
    shapes = [jax.ShapeDtypeStruct((24, 16, 192), BF16)] + gradients * 2
    anywhere, vmem = pl.BlockSpec(memory_space=pl.ANY), pl.BlockSpec(memory_space=pltpu.VMEM)
    operands = [
        fields,
        first_weight.reshape(9, 192, 192),
        first_gamma,
        first_beta.reshape(1, 192),
        second_weight.reshape(9, 192, 192),
        second_gamma,
        second_beta.reshape(1, 192),
        cotangent,
    ]
    carried = [
        jax.ShapeDtypeStruct(extent, dtype)
        for extent, dtype in (
            ((26, 24, 192), F32),
            ((3, 30, 24, 192), F32),
            ((3, 28, 24, 192), F32),
            ((24, 16, 192), F32),
            ((24, 16, 192), F32),
            ((192, 192), F32),
            ((9, 192, 192), BF16),
            ((192, 192), F32),
            ((1, 192), F32),
            ((9, 192, 192), BF16),
            ((192, 192), BF16),
        )
    ]
    middle = pl.pallas_call(
        first_kernel,
        out_shape=carried,
        in_specs=[anywhere] * 8,
        out_specs=[vmem] * 11,
        scratch_shapes=[
            pltpu.VMEM((192, 192), BF16),
            pltpu.VMEM((24, 16, 192), BF16),
            pltpu.VMEM((24, 16, 192), BF16),
            pltpu.VMEM((9, 192, 192), BF16),
            pltpu.VMEM((1, 192), F32),
            pltpu.VMEM((30, 24, 192), F32),
            pltpu.VMEM((4, 16, 192), BF16),
            pltpu.VMEM((4, 16, 192), BF16),
            pltpu.VMEM((2, 96, 128), BF16),
            pltpu.VMEM((2, 96, 128), BF16),
            pltpu.VMEM((4, 16, 192), BF16),
            pltpu.VMEM((2, 4, 16, 192), BF16),
            pltpu.VMEM((4, 16, 192), BF16),
            pltpu.VMEM((2, 96, 128), BF16),
            pltpu.VMEM((2, 96, 128), BF16),
            pltpu.VMEM((192, 128), F32),
            pltpu.VMEM((2, 96, 128), F32),
            pltpu.SemaphoreType.DMA((8,)),
            pltpu.SemaphoreType.DMA((8,)),
            pltpu.SemaphoreType.DMA((8,)),
        ],
        compiler_params=pltpu.CompilerParams(
            collective_id=0, has_side_effects=True, vmem_limit_bytes=32 * 1024 * 1024
        ),
    )(*[pltpu.with_memory_space_constraint(operand, pltpu.HBM) for operand in operands])
    results = pl.pallas_call(
        second_kernel,
        out_shape=shapes,
        in_specs=[vmem] * 11,
        out_specs=[vmem] * 7,
        scratch_shapes=[
            pltpu.VMEM((2, 2, BLOCKS, 128, 128), F32),
            pltpu.VMEM((3, 26, 24, 192), F32),
            pltpu.VMEM((128, 128), F32),
            *reduction_scratch(),
        ],
        compiler_params=pltpu.CompilerParams(
            collective_id=1, has_side_effects=True, vmem_limit_bytes=32 * 1024 * 1024
        ),
    )(*middle)
    encoded, w1, g1, b1, w2, g2, b2 = pl.pallas_call(
        write_out,
        out_shape=shapes,
        in_specs=[vmem] * 7,
        out_specs=[anywhere] * 7,
        scratch_shapes=[pltpu.SemaphoreType.DMA((7,))],
        compiler_params=pltpu.CompilerParams(vmem_limit_bytes=8 * 1024 * 1024),
    )(*results)
    return (encoded, w1.reshape(shape), g1, b1.reshape(192), w2.reshape(shape), g2, b2.reshape(192))


def solution(mesh):
    return jax.shard_map(
        per_device,
        mesh=mesh,
        in_specs=(P("lat", "lon", None), P(), P(), P(), P(), P(), P(), P("lat", "lon", None)),
        out_specs=(P("lat", "lon", None), P(), P(), P(), P(), P(), P()),
        check_vma=False,
    )
```

```python
import jax
import jax.numpy as jnp
from jax import lax
from jax.experimental import pallas as pl
from jax.experimental.pallas import tpu as pltpu
from jax.sharding import PartitionSpec as P

MESH = pl.DeviceIdType.MESH
BF16 = jnp.bfloat16
F32 = jnp.float32
NX, NY, NZ = 4, 8, 8
SIZES = {"x": NX, "y": NY, "z": NZ}
BLOCKS = 12
SLOTS = 36
DEALT = ((0, 1, 10, 15), (2, 3, 11, 16)), ((4, 5, 12, 17), (6, 7, 13, 20)), ((8, 9), (18, 21)), ((14, 19), (22, 23))
FIRSTS = (0, 4, 8, 10)
PLACES = {
    part: (core, FIRSTS[stream] + k)
    for stream, cores in enumerate(DEALT)
    for core, parts in enumerate(cores)
    for k, part in enumerate(parts)
}


def coordinates():
    lat, lon = lax.axis_index("lat"), lax.axis_index("lon")
    core = lax.rem(lon, 2)
    x = lax.rem(lax.div(lon, 2), NX)
    z = lax.div(lon, 2 * NX) * 2 + lax.rem(lat, 2)
    y = lax.div(lat, 2)
    return core, x, y, z


def at(core, x, y, z):
    return (y * 2 + lax.rem(z, 2), lax.div(z, 2) * (2 * NX) + x * 2 + core)


def partners():
    core, x, y, z = coordinates()
    found = [at(1 - core, x, y, z)]
    found += [at(core, lax.rem(x + d, NX), y, z) for d in range(1, NX)]
    found += [at(core, x, lax.rem(y + d, NY), z) for d in range(1, NY)]
    found += [at(core, x, y, lax.rem(z + d, NZ)) for d in range(1, NZ)]
    return found


def far_first(size):
    return sorted(range(1, size), key=lambda d: -min(d, size - d))


class Link:
    def __init__(self, axis, send, recv):
        place = dict(zip(("core", "x", "y", "z"), coordinates()))
        self.size, self.me = SIZES[axis], place[axis]
        self.axis, self.place = axis, place
        self.send_sem, self.recv_sem = send, recv

    def copy(self, source, target, d):
        place = dict(self.place)
        place[self.axis] = lax.rem(self.me + d, self.size)
        return pltpu.make_async_remote_copy(
            src_ref=source,
            dst_ref=target,
            send_sem=self.send_sem,
            recv_sem=self.recv_sem,
            device_id=at(**place),
            device_id_type=MESH,
        )


class Scatter(Link):
    def __init__(self, axis, send, recv, out, into):
        super().__init__(axis, send, recv)
        self.out, self.into = out, into

    def start(self, piece):
        for d in far_first(self.size):
            self.out[d - 1] = piece(lax.rem(self.me + d, self.size)).astype(BF16)
            self.copy(self.out.at[d - 1], self.into.at[d - 1], d).start()

    def finish(self, own):
        self.copy(self.out, self.into, 1).wait_recv()
        total = own
        for d in range(1, self.size):
            total = total + self.into[d - 1].astype(F32)
        return total

    def drain(self):
        self.copy(self.out, self.into, 1).wait_send()


class Share(Link):
    def __init__(self, axis, send, recv, held):
        super().__init__(axis, send, recv)
        self.held = held

    def start(self, value):
        self.held[self.me] = value.astype(BF16)
        for d in far_first(self.size):
            self.copy(self.held.at[self.me], self.held.at[self.me], d).start()

    def others(self):
        span = self.held.at[0 : self.size - 1]
        return self.copy(span, span, 1)

    def finish(self):
        self.others().wait_recv()

    def total(self):
        self.finish()
        total = self.held[0].astype(F32)
        for k in range(1, self.size):
            total = total + self.held[k].astype(F32)
        return total

    def drain(self):
        self.others().wait_send()


class Reduction:
    def __init__(self, layer, grads, core_out, core_in, x_out, x_in, y_out, y_in, z_out, z_in, y_out2, y_in2, z_out2, z_in2, held16, held32, held4, sums16, sums32, full, send, recv):
        self.grads, self.full = grads, full
        self.core_out, self.core_in = core_out, core_in
        self.me = coordinates()
        self.send, self.recv = send.at[layer], recv.at[layer]
        self.slots = 0
        self.streams = [
            self.twice(0, "x", "y", "z", (x_out.at[0], x_in.at[0]), (y_out, y_in), held16.at[0], held16.at[1], sums16.at[0]),
            self.twice(4, "x", "z", "y", (x_out.at[1], x_in.at[1]), (z_out, z_in), held16.at[2], held16.at[3], sums16.at[1]),
            self.once(8, "y", "x", "z", (y_out2, y_in2), held4.at[0], held32.at[0], held32.at[1], sums32.at[0]),
            self.once(10, "z", "x", "y", (z_out2, z_in2), held4.at[1], held32.at[2], held32.at[3], sums32.at[1]),
        ]

    def slot(self):
        self.slots += 1
        return self.send.at[self.slots - 1], self.recv.at[self.slots - 1]

    def place(self, axis):
        return self.me["xyz".index(axis) + 1]

    def partner_copy(self, sems, source, target):
        core, x, y, z = self.me
        return pltpu.make_async_remote_copy(
            src_ref=source,
            dst_ref=target,
            send_sem=sems[0],
            recv_sem=sems[1],
            device_id=at(1 - core, x, y, z),
            device_id_type=MESH,
        )

    def core_phase(self, first, count):
        sems = self.slot()
        span = slice(first, first + count)
        copy = self.partner_copy(sems, self.core_out.at[span], self.core_in.at[span])

        def start():
            self.core_out[span] = self.grads[1 - self.me[0], span].astype(BF16)
            copy.start()

        return start, copy

    def half(self, block):
        return self.grads[self.me[0], block] + self.core_in[block].astype(F32)

    def turned(self, piece):
        return piece.astype(F32).T.astype(BF16)

    def twice(self, first, axis, second, third, wide, narrow, held, spread, sums):
        core = self.me[0]
        begin, core_copy = self.core_phase(first, 4)
        one = Scatter(axis, *self.slot(), *wide)
        two = Scatter(second, *self.slot(), *narrow)
        three = Share(third, *self.slot(), held)
        four = Share(second, *self.slot(), spread)
        gather_sems = [self.slot() for _ in range(1, NX)]
        last_sems = [self.slot() for _ in range(NX)]
        me, here = self.place(axis), self.place(second)

        def block(d):
            return first + lax.rem(me + NX - d, NX)

        def gather(d, arrival=False):
            ref = self.full.at[core, block(d) if arrival else block(0)]
            return Link(axis, *gather_sems[d - 1]).copy(ref, ref, d)

        def last(d, arrival=False):
            ref = self.full.at[1 - core if arrival else core, block(d)]
            return self.partner_copy(last_sems[d], ref, ref)

        def step1():
            core_copy.wait_recv()
            one.start(lambda k: self.half(first + k))

        def step2():
            sums[...] = one.finish(self.half(first + me)).reshape(sums.shape)
            two.start(lambda k: sums[k])

        def step3():
            three.start(two.finish(sums[here]))

        def step4():
            four.start(three.total())

        def step5():
            four.finish()
            self.full[core, block(0)] = self.turned(spread[...].reshape(128, 128))
            for d in range(1, NX):
                gather(d).start()
            last(0).start()

        def step6():
            for d in range(1, NX):
                gather(d, arrival=True).wait_recv()
                last(d).start()

        def done():
            for d in range(NX):
                last(d, arrival=True).wait_recv()

        def drain():
            core_copy.wait_send()
            for phase in (one, two, three, four):
                phase.drain()
            for d in range(NX):
                last(d).wait_send()
            for d in range(1, NX):
                gather(d).wait_send()

        return (begin, step1, step2, step3, step4, step5, step6, done, drain)

    def once(self, first, axis, second, third, wide, held, held_more, spread, sums):
        core = self.me[0]
        begin, core_copy = self.core_phase(first, 2)
        one = Scatter(axis, *self.slot(), *wide)
        two = Share(second, *self.slot(), held)
        three = Share(third, *self.slot(), held_more)
        four = Share(axis, *self.slot(), spread)
        last_sems = self.slot()
        me = self.place(axis)

        def last(arrival=False):
            ref = self.full.at[1 - core if arrival else core, first : first + 2]
            return self.partner_copy(last_sems, ref, ref)

        def step1():
            core_copy.wait_recv()
            total = self.grads[core, first : first + 2] + self.core_in[first : first + 2].astype(F32)
            sums[...] = total.reshape(sums.shape)
            one.start(lambda k: sums[k])

        def step2():
            two.start(one.finish(sums[me]))

        def step3():
            three.start(two.total())

        def step4():
            four.start(three.total())

        def step5():
            four.finish()
            whole = spread[...].reshape(2, 128, 128)
            for side in range(2):
                self.full[core, first + side] = self.turned(whole[side])
            last().start()

        def step6():
            pass

        def done():
            last(arrival=True).wait_recv()

        def drain():
            core_copy.wait_send()
            for phase in (one, two, three, four):
                phase.drain()
            last().wait_send()

        return (begin, step1, step2, step3, step4, step5, step6, done, drain)

    def step(self, index, streams=(0, 1, 2, 3)):
        for k in streams:
            self.streams[k][index]()

    def drain(self):
        self.step(8)

    def block(self, index):
        return self.full[PLACES[index]]

    def unpack(self, wgrad, ggrad, bgrad):
        for tap in range(10):
            pair, odd = divmod(tap, 2)
            low = slice(64 * odd, 64 * odd + 64)
            target = ggrad if tap == 9 else wgrad.at[tap]
            dtype = F32 if tap == 9 else BF16
            target[0:128, 0:128] = self.block(tap).astype(dtype)
            target[0:128, 128:192] = self.block(15 + pair)[:, low].astype(dtype)
            target[128:192, 0:128] = self.block(10 + pair)[low].astype(dtype)
            half, side = divmod(10 + pair, 2)
            corner = self.block(15 + half)[low, 64 * side : 64 * side + 64]
            target[128:192, 128:192] = corner.astype(dtype)
        offsets = self.block(23).astype(F32)
        bgrad[0:1, 0:128] = offsets[0:1]
        bgrad[0:1, 128:192] = offsets[1:2, 0:64]


def reduction_scratch():
    return [
        pltpu.VMEM((2, BLOCKS, 128, 128), BF16),
        pltpu.VMEM((2, BLOCKS, 128, 128), BF16),
        pltpu.VMEM((2, 2, NX - 1, 128, 128), BF16),
        pltpu.VMEM((2, 2, NX - 1, 128, 128), BF16),
        pltpu.VMEM((2, NY - 1, 16, 128), BF16),
        pltpu.VMEM((2, NY - 1, 16, 128), BF16),
        pltpu.VMEM((2, NZ - 1, 16, 128), BF16),
        pltpu.VMEM((2, NZ - 1, 16, 128), BF16),
        pltpu.VMEM((2, NY - 1, 32, 128), BF16),
        pltpu.VMEM((2, NY - 1, 32, 128), BF16),
        pltpu.VMEM((2, NZ - 1, 32, 128), BF16),
        pltpu.VMEM((2, NZ - 1, 32, 128), BF16),
        pltpu.VMEM((2, 4, 8, 16, 128), BF16),
        pltpu.VMEM((2, 4, 8, 32, 128), BF16),
        pltpu.VMEM((2, 2, NX, 32, 128), BF16),
        pltpu.VMEM((2, 2, 8, 16, 128), F32),
        pltpu.VMEM((2, 2, 8, 32, 128), F32),
        pltpu.VMEM((2, 2, BLOCKS, 128, 128), BF16),
        pltpu.SemaphoreType.DMA((2, SLOTS)),
        pltpu.SemaphoreType.DMA((2, SLOTS)),
    ]


def reductions(grads, scratch):
    *buffers, send, recv = scratch
    return [
        Reduction(layer, grads.at[layer], *[buffer.at[layer] for buffer in buffers], send, recv)
        for layer in range(2)
    ]


def neighbours():
    lat, lon = lax.axis_index("lat"), lax.axis_index("lon")
    lats, lons = lax.axis_size("lat"), lax.axis_size("lon")
    first = (lat == 0).astype(jnp.int32)
    last = (lat == lats - 1).astype(jnp.int32)
    rows = []
    for pole, step, side in ((first, -1, 1), (last, 1, 0)):
        for east in (-1, 0, 1):
            device = (lat + step * (1 - pole), lax.rem(lon + lons + east + pole * (lons // 2), lons))
            landing = side + pole * (1 - 2 * side)
            rows.append((device, 4 + landing if east == 0 else 2 * landing + (1 - east) // 2))
    west = (lat, lax.rem(lon + lons - 1, lons))
    east = (lat, lax.rem(lon + 1, lons))
    return first, last, rows, west, east


def dot(left, right, dims=((1,), (0,))):
    return lax.dot_general(left, right, (dims, ((), ())), preferred_element_type=F32)


def split(value):
    high = value.astype(BF16)
    return high, (value - high.astype(F32)).astype(BF16)


def dot_split(left, right, dims=((1,), (0,))):
    left_high, left_low = split(left)
    right_high, right_low = split(right)
    return dot(left_high, right_high, dims) + dot(left_high, right_low, dims) + dot(left_low, right_high, dims)


def flat(value):
    return value.reshape(-1, value.shape[-1])


def keep_shifted(store, value, rows=slice(None)):
    store[0, rows] = pltpu.roll(value, 1, axis=1)
    store[1, rows] = value
    store[2, rows] = pltpu.roll(value, 23, axis=1)


def outer_window(store, rows, ghosts, a, b, first, last):
    turned = 2 - 2 * a
    top = store[b, pl.ds(a + first * turned, ghosts)]
    middle = store[b, ghosts + a : rows - ghosts + a]
    bottom = store[b, pl.ds(rows - ghosts + a + last * turned, ghosts)]
    return flat(jnp.concatenate([top, middle, bottom], axis=0)).astype(BF16)


def inner_window(store, a, b, start):
    return flat(store[b, start + a : start + a + 24, 0:16]).astype(BF16)


def gathered(windows, weight):
    return dot(jnp.concatenate(windows, axis=1), weight[...].reshape(9 * 192, 192))


def outer_convolution(store, weight, rows, ghosts, first, last):
    taps = [(a, b) for a in range(3) for b in range(3)]
    return gathered([outer_window(store, rows, ghosts, a, b, first, last) for a, b in taps], weight)


def place_block(grads, index, value):
    core, block = PLACES[index]
    grads[core, block] = value


def place_lower(grads, tile, value):
    core, block = PLACES[15 + tile // 2]
    start = 64 * (tile % 2)
    grads[core, block, start : start + 64] = value


def pack_gradients(grads, store, start, grad, lever, sq, turn, after=None):
    turned = grad.T.astype(BF16)
    kept = None
    for tap in range(10):
        if tap < 9:
            block = dot(turned, inner_window(store, tap // 3, tap % 3, start))
        else:
            block = -0.5 * dot_split(sq.T, lever)
        place_block(grads, tap, block[0:128, 0:128])
        place_lower(grads, tap, block[128:192, 0:128])
        if tap % 2 == 0:
            kept = block[:, 128:192]
        else:
            both = jnp.concatenate([kept, block[:, 128:192]], axis=1)
            tile = 10 + tap // 2
            place_block(grads, tile, both[0:128])
            place_lower(grads, tile, both[128:192])
        if after and tap in after:
            after[tap]()
    offsets = -0.5 * jnp.sum(lever, axis=0, keepdims=True)
    turn[...] = jnp.zeros_like(turn)
    turn[0:1, :] = offsets[:, 0:128]
    turn[1:2, 0:64] = offsets[:, 128:192]
    place_lower(grads, 15, jnp.zeros((64, 128), F32))
    place_block(grads, 23, turn[...].T)


def normal_scale(z, gamma, beta):
    return lax.rsqrt(beta[...] + dot((z * z).astype(BF16), gamma[...]))


def first_kernel(
    x_far, w1_far, gamma1_far, beta1_far, w2_far, gamma2_far, beta2_far, cot_far,
    cotangent, x_store, h_store, z_keep, scale_keep, gamma1, w2, gamma2, beta2, w2_turned, gamma2_turned,
    gamma1_turned, x, cot, w1, beta1, field, top_out, bottom_out, west_out, east_out, corner_out, middle_in, corner_in, west_in, east_in, stage, strips,
    fetched, halo_send, halo_recv,
):
    barrier = pltpu.get_barrier_semaphore()
    first, last, rows, west, east = neighbours()
    met = [west, east] + [device for device, _ in rows]
    for device in met:
        pl.semaphore_signal(barrier, inc=1, device_id=device, device_id_type=MESH)

    pairs = [
        (x_far, x), (cot_far, cot), (w1_far, w1), (gamma1_far, gamma1),
        (beta1_far, beta1), (w2_far, w2), (gamma2_far, gamma2), (beta2_far, beta2),
    ]
    fetches = [pltpu.make_async_copy(far, near, fetched.at[i]) for i, (far, near) in enumerate(pairs)]
    for fetch in fetches:
        fetch.start()
    fetches[0].wait()
    fetches[1].wait()
    for side, out in enumerate((top_out, bottom_out)):
        lines = [cot[23 * side]] + [x[23 - k if side else k] for k in range(3)]
        for k, line in enumerate(lines):
            out[k] = line
        for edge, lanes in ((0, slice(0, 4)), (1, slice(12, 16))):
            corner = jnp.concatenate([line.astype(F32)[lanes] for line in lines], axis=0)
            corner_out[2 * side + edge] = corner.astype(BF16)

    def strip(target, tile, places, edge):
        for half, lanes in enumerate((128, 64)):
            span = slice(128 * half, 128 * half + lanes)
            for ref, chosen, at_row in ((x, places, 0), (cot, (edge,), 72)):
                stage.reshape(24, 8, 128)[:, :, 0:lanes] = ref[:, tile : tile + 8, span].astype(F32)
                for k, place in enumerate(chosen):
                    rows24 = stage[pl.ds(place - tile, 24, stride=8), :]
                    strips[half, at_row + 24 * k : at_row + 24 * k + 24] = rows24
        target[0:96] = strips[0].astype(BF16)
        upper = strips[1]
        target[96:144] = jnp.concatenate([upper[0:48, 0:64], upper[48:96, 0:64]], axis=1).astype(BF16)

    strip(west_out, 0, (0, 1, 2), 0)
    strip(east_out, 8, (13, 14, 15), 15)

    pl.semaphore_wait(barrier, len(met))

    def halo(source, target, sent, landed, device):
        return pltpu.make_async_remote_copy(
            src_ref=source,
            dst_ref=target,
            send_sem=halo_send.at[sent],
            recv_sem=halo_recv.at[landed],
            device_id=device,
            device_id_type=MESH,
        )

    copies = [halo(west_out, east_in, 6, 6, west), halo(east_out, west_in, 7, 7, east)]
    for index in (0, 2, 3, 5, 1, 4):
        device, slot = rows[index]
        if index in (1, 4):
            source, target = (top_out, bottom_out)[index // 3], middle_in.at[slot - 4]
        else:
            source, target = corner_out.at[2 * (index // 3) + (index % 3) // 2], corner_in.at[slot]
        copies.append(halo(source, target, index, slot, device))
    for copy in copies:
        copy.start()

    field[3:27, 0:16] = x[...].astype(F32)
    cotangent[1:25, 0:16] = cot[...].astype(F32)
    for fetch in fetches[2:]:
        fetch.wait()
    gamma1_turned[...] = gamma1[...].T.astype(BF16)
    gamma2_turned[...] = gamma2[...].T.astype(BF16)
    for tap in range(9):
        w2_turned[tap] = w2[tap].astype(F32).T.astype(BF16)

    copies[0].wait_recv()
    copies[1].wait_recv()
    for half, lanes in enumerate((128, 64)):
        span = slice(128 * half, 128 * half + lanes)
        for target, start, size in ((field, 3, 3), (cotangent, 1, 1)):
            for source, offset in ((east_in, 0), (west_in, 8 - size)):
                if half == 0:
                    arrived = source[0:96].astype(F32)
                else:
                    shared = source[96:144].astype(F32)
                    arrived = jnp.concatenate([shared, pltpu.roll(shared, 64, axis=1)], axis=0)
                for k in range(size):
                    at_row = 24 * k if size == 3 else 72
                    stage[pl.ds(offset + k, 24, stride=8), :] = arrived[at_row : at_row + 24]
            target[start : start + 24, 16:24, span] = stage.reshape(24, 8, 128)[:, :, 0:lanes]

    def layer(window):
        z = gathered([flat(window(a, b)).astype(BF16) for a in range(3) for b in range(3)], w1)
        scale = normal_scale(z, gamma1_turned, beta1)
        hidden = (z * scale).astype(BF16).astype(F32)
        return [value.reshape(-1, 24, 192) for value in (z, scale, hidden)]

    keep_shifted(x_store, field[3:27], slice(3, 27))
    z, scale, hidden = layer(lambda a, b: x_store[b, 3 + a : 25 + a])
    z_keep[1:23] = z[:, 0:16]
    scale_keep[1:23] = scale[:, 0:16]
    keep_shifted(h_store, hidden, slice(3, 25))

    for slot in range(6):
        source, target = (top_out, middle_in.at[slot - 4]) if slot > 3 else (corner_out.at[0], corner_in.at[slot])
        halo(source, target, 0, slot, rows[0][0]).wait_recv()
    for side in range(2):
        from_west = corner_in[2 * side].astype(F32)
        from_east = corner_in[2 * side + 1].astype(F32)
        for k in range(4):
            target = cotangent if k == 0 else field
            if k == 0:
                row = 25 * side
            else:
                row = 26 + k if side else 3 - k
            target[row, 0:16] = middle_in[side, k].astype(F32)
            span = slice(4 * k, 4 * k + 4)
            target[row, 16:24] = jnp.concatenate([from_east[span], from_west[span]], axis=0)
    keep_shifted(x_store, field[0:3], slice(0, 3))
    keep_shifted(x_store, field[27:30], slice(27, 30))

    def edge_window(a, b):
        top = x_store[b, pl.ds(a + first * (2 - 2 * a), 2)]
        bottom = x_store[b, pl.ds(26 + a + last * (2 - 2 * a), 2)]
        return jnp.concatenate([top, x_store[b, 2 + a : 3 + a], x_store[b, 25 + a : 26 + a], bottom], axis=0)

    z, scale, hidden = layer(edge_window)
    for place, row in ((0, 2), (23, 3)):
        z_keep[place] = z[row, 0:16]
        scale_keep[place] = scale[row, 0:16]
    keep_shifted(h_store, hidden[0:3], slice(0, 3))
    keep_shifted(h_store, hidden[3:6], slice(25, 28))
    for copy in copies:
        copy.wait_send()


def second_kernel(
    cotangent, x_store, h_store, z_keep, scale_keep, gamma1, w2, gamma2, beta2, w2_turned, gamma2_turned,
    encoded, out_w1, out_g1, out_b1, out_w2, out_g2, out_b2,
    grads, g_store, turn, *scratch,
):
    barrier = pltpu.get_barrier_semaphore()
    first, last = neighbours()[:2]
    met = partners()
    for device in met:
        pl.semaphore_signal(barrier, inc=1, device_id=device, device_id_type=MESH)

    z2 = outer_convolution(h_store, w2, 26, 1, first, last)
    sq2 = z2 * z2
    scale2 = normal_scale(z2, gamma2_turned, beta2)
    encoded[...] = (z2 * scale2).reshape(26, 24, 192)[1:25, 0:16].astype(BF16)
    upper = flat(cotangent[...])
    lever2 = upper * z2 * scale2 * scale2 * scale2
    lower2 = upper * scale2 - z2 * dot(lever2.astype(BF16), gamma2[...].astype(BF16))
    grad2 = lower2.astype(BF16).astype(F32).reshape(26, 24, 192)
    keep_shifted(g_store, grad2)

    def inside(value):
        return flat(value.reshape(26, 24, 192)[1:25, 0:16])

    one, two = reductions(grads, scratch)
    pack_gradients(grads.at[1], h_store, 1, inside(grad2), inside(lever2), inside(sq2), turn)
    pl.semaphore_wait(barrier, len(met))
    two.step(0)

    blank = jnp.zeros((1, 16, 192), F32)
    windows = []
    for a in range(3):
        for b in range(3):
            shifted = g_store.at[2 - b]
            if a == 0:
                window = jnp.concatenate([shifted[2:25, 0:16], blank], axis=0)
            elif a == 1:
                window = shifted[1:25, 0:16]
            else:
                window = jnp.concatenate([blank, shifted[1:24, 0:16]], axis=0)
            windows.append(flat(window).astype(BF16))
    total = gathered(windows, w2_turned)
    ghosts = []
    for row, a in ((0, 2 - 2 * first), (25, 2 * last)):
        ghost = None
        for b in range(3):
            term = dot(g_store[2 - b, row, 0:16].astype(BF16), w2_turned[3 * a + b])
            ghost = term if ghost is None else ghost + term
        ghosts.append(ghost)
    upper1 = jnp.concatenate([total[0:16] + ghosts[0], total[16:368], total[368:384] + ghosts[1]], axis=0)

    z1 = flat(z_keep[...])
    scale1 = flat(scale_keep[...])
    lever1 = upper1 * z1 * scale1 * scale1 * scale1
    lower1 = upper1 * scale1 - z1 * dot(lever1.astype(BF16), gamma1[...].astype(BF16))
    grad1 = lower1.astype(BF16).astype(F32)
    two.step(1)
    ready = {3: lambda: one.step(0, (0,)), 7: lambda: one.step(0, (1,))}
    pack_gradients(grads.at[0], x_store, 2, grad1, lever1, z1 * z1, turn, ready)
    one.step(0, (2, 3))
    one.step(1)
    two.step(2)
    for index in range(2, 7):
        one.step(index)
        two.step(index + 1)
    two.unpack(out_w2, out_g2, out_b2)
    one.step(7)
    one.unpack(out_w1, out_g1, out_b1)
    two.drain()
    one.drain()


def write_out(*refs):
    sources, targets, done = refs[:7], refs[7:14], refs[14]
    copies = [pltpu.make_async_copy(sources[i], targets[i], done.at[i]) for i in (1, 4, 0, 2, 5, 3, 6)]
    for copy in copies:
        copy.start()
    for copy in copies:
        copy.wait()


def per_device(
    fields,
    first_weight,
    first_gamma,
    first_beta,
    second_weight,
    second_gamma,
    second_beta,
    cotangent,
):
    gradients = [
        jax.ShapeDtypeStruct((9, 192, 192), BF16),
        jax.ShapeDtypeStruct((192, 192), F32),
        jax.ShapeDtypeStruct((1, 192), F32),
    ]
    shape = (3, 3, 192, 192)
    shapes = [jax.ShapeDtypeStruct((24, 16, 192), BF16)] + gradients * 2
    anywhere, vmem = pl.BlockSpec(memory_space=pl.ANY), pl.BlockSpec(memory_space=pltpu.VMEM)
    operands = [
        fields,
        first_weight.reshape(9, 192, 192),
        first_gamma,
        first_beta.reshape(1, 192),
        second_weight.reshape(9, 192, 192),
        second_gamma,
        second_beta.reshape(1, 192),
        cotangent,
    ]
    carried = [
        jax.ShapeDtypeStruct(extent, dtype)
        for extent, dtype in (
            ((26, 24, 192), F32),
            ((3, 30, 24, 192), F32),
            ((3, 28, 24, 192), F32),
            ((24, 16, 192), F32),
            ((24, 16, 192), F32),
            ((192, 192), F32),
            ((9, 192, 192), BF16),
            ((192, 192), F32),
            ((1, 192), F32),
            ((9, 192, 192), BF16),
            ((192, 192), BF16),
        )
    ]
    middle = pl.pallas_call(
        first_kernel,
        out_shape=carried,
        in_specs=[anywhere] * 8,
        out_specs=[vmem] * 11,
        scratch_shapes=[
            pltpu.VMEM((192, 192), BF16),
            pltpu.VMEM((24, 16, 192), BF16),
            pltpu.VMEM((24, 16, 192), BF16),
            pltpu.VMEM((9, 192, 192), BF16),
            pltpu.VMEM((1, 192), F32),
            pltpu.VMEM((30, 24, 192), F32),
            pltpu.VMEM((4, 16, 192), BF16),
            pltpu.VMEM((4, 16, 192), BF16),
            pltpu.VMEM((144, 128), BF16),
            pltpu.VMEM((144, 128), BF16),
            pltpu.VMEM((4, 16, 192), BF16),
            pltpu.VMEM((2, 4, 16, 192), BF16),
            pltpu.VMEM((4, 16, 192), BF16),
            pltpu.VMEM((144, 128), BF16),
            pltpu.VMEM((144, 128), BF16),
            pltpu.VMEM((192, 128), F32),
            pltpu.VMEM((2, 96, 128), F32),
            pltpu.SemaphoreType.DMA((8,)),
            pltpu.SemaphoreType.DMA((8,)),
            pltpu.SemaphoreType.DMA((8,)),
        ],
        compiler_params=pltpu.CompilerParams(
            collective_id=0, has_side_effects=True, vmem_limit_bytes=32 * 1024 * 1024
        ),
    )(*[pltpu.with_memory_space_constraint(operand, pltpu.HBM) for operand in operands])
    results = pl.pallas_call(
        second_kernel,
        out_shape=shapes,
        in_specs=[vmem] * 11,
        out_specs=[vmem] * 7,
        scratch_shapes=[
            pltpu.VMEM((2, 2, BLOCKS, 128, 128), F32),
            pltpu.VMEM((3, 26, 24, 192), F32),
            pltpu.VMEM((128, 128), F32),
            *reduction_scratch(),
        ],
        compiler_params=pltpu.CompilerParams(
            collective_id=1, has_side_effects=True, vmem_limit_bytes=32 * 1024 * 1024
        ),
    )(*middle)
    encoded, w1, g1, b1, w2, g2, b2 = pl.pallas_call(
        write_out,
        out_shape=shapes,
        in_specs=[vmem] * 7,
        out_specs=[anywhere] * 7,
        scratch_shapes=[pltpu.SemaphoreType.DMA((7,))],
        compiler_params=pltpu.CompilerParams(vmem_limit_bytes=8 * 1024 * 1024),
    )(*results)
    return (encoded, w1.reshape(shape), g1, b1.reshape(192), w2.reshape(shape), g2, b2.reshape(192))


def solution(mesh):
    return jax.shard_map(
        per_device,
        mesh=mesh,
        in_specs=(P("lat", "lon", None), P(), P(), P(), P(), P(), P(), P("lat", "lon", None)),
        out_specs=(P("lat", "lon", None), P(), P(), P(), P(), P(), P()),
        check_vma=False,
    )
```
